32 devices in a mesh: space: 2 (over x), blk: 16 (over z, y, core).
Axes of the slice: x: 2, y: 2, z: 4, core: 2. Of those that a mesh axis runs over, the one named last changes fastest.
Arguments:
- snapshots: bfloat16 [20480, 1024], P('blk', 'space'), may hold values from -6 to 6
- row_scales: float32 [20480], P('blk'), may hold values from 0.3 to 3
- block_offsets: int32 [64], P('blk'), may hold values from 0 to 768, as said below
- freq_index: int32 [16], replicated, may hold values from 1 to 255
Outputs:
- modes: float32 [16, 1024, 128], P('blk', 'space')
- r_factor: float32 [16, 2, 64, 64], P('blk')
The draws below stay inside these ranges and needn't reach their ends.
Inputs may be any that keep to these rules, and one draw needn't show every extreme that they name: `block_offsets`: block offsets index the snapshots held by the block's own index of blk; within every group of 4 blocks they are distinct and increasing, block i of a group lies between i * 256 - 512 / 4 and i * 256 + 512 / 4; in the first group the first is 0 and the last is 768.
All inputs are finite; a program needn't handle non-finite values.
Results may differ from the reference program's by a relative error of at most 0.0064.
Values may be sent and summed in bfloat16 or wider, within the bound.
No kernel may reach another device: no remote copies, remote signals or barrier semaphores. Data moves between devices by JAX's collectives and lax.ppermute only.
A program may use at most 64 MiB of HBM per device.

```python
import math
import jax
import jax.numpy as jnp
from jax import lax

NFFT = 512
BLK_DEV = 4
FREQS = 16
BLOCKS = 64
SNAP_DEV = 1280
SNAPS = 20480
POINTS = 1024


def draw_block_offsets(key, part):
    groups = BLOCKS // BLK_DEV
    top = SNAP_DEV - NFFT
    jitter = jax.random.randint(key, (groups, BLK_DEV), 0, NFFT // 4, dtype=jnp.int32)
    base = jnp.arange(BLK_DEV, dtype=jnp.int32) * (NFFT // 2)
    values = base[None, :] + jitter
    values = values.at[:, BLK_DEV - 1].set(top - jitter[:, BLK_DEV - 1])
    values = values.at[0, 0].set(0)
    values = values.at[0, BLK_DEV - 1].set(top)
    return values.reshape(BLOCKS).astype(jnp.int32)


def plant(values, key, least, top_value):
    longest = values.shape.index(max(values.shape))
    spots = []
    for shift in (0, 1):
        where = [jax.random.randint(jax.random.fold_in(key, axis), (), 0, length) for axis, length in enumerate(values.shape)]
        where[longest] = (where[longest] + shift) % values.shape[longest]
        spots.append(tuple(where))
    return values.at[spots[0]].set(least).at[spots[1]].set(top_value)


def levels(own_key, extent, split, low, largest):
    gain = 1.0
    for axis_at, shards_of in split:
        steps = jax.random.uniform(jax.random.fold_in(jax.random.fold_in(own_key, 6), axis_at), (shards_of,), jnp.float32, low / len(split), largest / len(split))
        gain = gain * jnp.repeat(jnp.exp(steps), extent[axis_at] // shards_of).reshape((-1,) + (1,) * (len(extent) - 1 - axis_at))
    return gain


def noise(rng, extent, scale, reach, split=(), kind=jnp.bfloat16):
    factor_of = levels(rng, extent, split, -0.22, 0.18) if split else 1.0
    drawn = jax.random.normal(rng, extent, jnp.float32) * scale * factor_of
    return jnp.minimum(jnp.maximum(drawn, -reach), reach).astype(kind)


def setup_inputs(seed: int = 0) -> dict:
    arg_keys = jax.random.split(jax.random.key(seed), 5)
    snapshots = noise(arg_keys[0], (SNAPS, POINTS), 1.0, 6.0, ((0, 16), (1, 2)))
    row_scales = jnp.clip(jnp.exp(math.log(3.0) - 2.3025851 * jax.random.uniform(arg_keys[1], (SNAPS,), jnp.float32) ** levels(arg_keys[1], (SNAPS,), ((0, 16),), -0.2, 0.2)), 0.3, 3.0)
    block_offsets = draw_block_offsets(jax.random.fold_in(arg_keys[4], 71), 0)
    freq_index = plant(jax.random.randint(arg_keys[3], (FREQS,), 1, NFFT // 2), jax.random.fold_in(arg_keys[3], 1), 1, (NFFT // 2) - 1).astype(jnp.int32)
    return dict(snapshots=snapshots, row_scales=row_scales, block_offsets=block_offsets, freq_index=freq_index)


def trig_table(freq_index):
    times = jnp.arange(NFFT, dtype=jnp.int32)
    phase = freq_index[:, None] * times[None, :] % NFFT
    angle = 2.0 * math.pi / NFFT * phase.astype(jnp.float32)
    inv_root = 1.0 / math.sqrt(NFFT)
    table = jnp.stack([jnp.cos(angle), -jnp.sin(angle)], 1).reshape(2 * freq_index.shape[0], NFFT) * inv_root
    hann = 0.5 - 0.5 * jnp.cos(2.0 * math.pi / NFFT * times.astype(jnp.float32))
    return (table, hann)

def reference(snapshots, row_scales, block_offsets, freq_index):
    table, hann = trig_table(freq_index)
    starts = jnp.arange(BLOCKS, dtype=jnp.int32) // BLK_DEV * SNAP_DEV + block_offsets.astype(jnp.int32)

    def one_block(start):
        window = lax.dynamic_slice_in_dim(snapshots, start, NFFT, 0)
        scaled = lax.dynamic_slice_in_dim(row_scales, start, NFFT, 0)
        coef = (table * (hann * scaled)[None, :]).astype(jnp.bfloat16)
        return jnp.dot(coef.astype(jnp.float32), window.astype(jnp.float32), preferred_element_type=jnp.float32).astype(jnp.bfloat16)
    spectra = lax.map(one_block, starts)
    spectra = spectra.reshape(BLOCKS, FREQS, 2, POINTS).transpose(1, 3, 0, 2).reshape(FREQS, POINTS, 2 * BLOCKS)

    def per_freq(single):
        pairs = single.reshape(POINTS, BLOCKS, 2)
        rotated = jnp.stack([-pairs[:, :, 1], pairs[:, :, 0]], -1).reshape(POINTS, 2 * BLOCKS)
        stacked = jnp.concatenate([single, rotated], 0)
        gram = jnp.dot(stacked.T.astype(jnp.float32), stacked.astype(jnp.float32), preferred_element_type=jnp.float32) / POINTS
        lower_factor = jnp.linalg.cholesky(gram)
        upper = lower_factor.T
        solved = jax.scipy.linalg.solve_triangular(lower_factor, single.astype(jnp.float32).T, lower=True)
        r_pair = jnp.stack([upper[0::2, 0::2], upper[0::2, 1::2]], 0)
        return (solved.T, r_pair)
    modes, r_factor = lax.map(per_freq, spectra)
    return (modes, r_factor)
```

```python
import functools
import math

import jax
import jax.numpy as jnp
from jax import lax
from jax.experimental import pallas as pl
from jax.experimental.pallas import tpu as pltpu
from jax.sharding import PartitionSpec as P

NFFT = 512
PANEL = 4
SUB = 8
SIN_COEFS = (
    0.9999999765895043,
    -0.1666664763439475,
    0.008332899819203531,
    -0.0001980089750772882,
    2.5904879854375602e-06,
)


def cos_of_phase(phase):
    folded = jnp.abs((phase & (NFFT - 1)) - NFFT // 2) - NFFT // 4
    x = folded.astype(jnp.float32) * (2.0 * math.pi / NFFT)
    square = x * x
    total = jnp.full_like(x, SIN_COEFS[-1])
    for coef in SIN_COEFS[-2::-1]:
        total = total * square + coef
    return total * x


def spectra_kernel(offsets_ref, freq_ref, scales_ref, snap_ref, out_ref, coef_ref):
    snaps = snap_ref.shape[0]
    blocks = offsets_ref.shape[0]
    rows = 2 * blocks
    freqs = freq_ref.shape[0]
    row = lax.broadcasted_iota(jnp.int32, (rows, snaps), 0)
    time = lax.broadcasted_iota(jnp.int32, (rows, snaps), 1)
    start = jnp.zeros((rows, snaps), jnp.int32)
    for b in range(blocks):
        start = jnp.where(row // 2 == b, offsets_ref[b], start)
    shifted = time - start
    hann = 0.5 - 0.5 * cos_of_phase(shifted)
    inside = (shifted >= 0) & (shifted < NFFT)
    scales = jnp.broadcast_to(scales_ref[...], (rows, snaps))
    weight = jnp.where(inside, hann * scales * (1.0 / math.sqrt(NFFT)), 0.0)
    base = shifted[:, :NFFT].astype(jnp.float32)
    quarter = (row[:, :NFFT] % 2) * (NFFT // 4)
    repeats = -(-snaps // NFFT)

    def rows_of(f):
        freq = freq_ref[f].astype(jnp.float32)
        table = cos_of_phase((base * freq).astype(jnp.int32) + quarter)
        return jnp.concatenate([table] * repeats, 1)[:, :snaps] * weight

    for f in range(0, freqs, 2):
        pair = jnp.concatenate([rows_of(f), rows_of(f + 1)], 0)
        coef_ref[f * rows:(f + 2) * rows, :] = pair.astype(jnp.bfloat16)
    out_ref[...] = jnp.dot(
        coef_ref[...], snap_ref[...], preferred_element_type=jnp.float32
    ).astype(jnp.bfloat16)


def block_spectra(snapshots, row_scales, block_offsets, freq_index):
    snaps, points = snapshots.shape
    rows = 2 * block_offsets.shape[0] * freq_index.shape[0]
    return pl.pallas_call(
        spectra_kernel,
        out_shape=jax.ShapeDtypeStruct((rows, points), jnp.bfloat16),
        in_specs=[
            pl.BlockSpec(memory_space=pltpu.SMEM),
            pl.BlockSpec(memory_space=pltpu.SMEM),
            pl.BlockSpec(memory_space=pltpu.VMEM),
            pl.BlockSpec(memory_space=pltpu.VMEM),
        ],
        out_specs=pl.BlockSpec(memory_space=pltpu.VMEM),
        scratch_shapes=[pltpu.VMEM((rows, snaps), jnp.bfloat16)],
        compiler_params=pltpu.CompilerParams(vmem_limit_bytes=24 * 2**20),
        name="spectra",
    )(block_offsets, freq_index, row_scales.reshape(1, snaps), snapshots)


def rotated(x, lane):
    axis = x.ndim - 1
    width = x.shape[axis]
    after = pltpu.roll(x, width - 1, axis)
    before = pltpu.roll(x, 1, axis)
    return jnp.where(lane % 2 == 0, -after, before)


def gram_kernel(x_ref, out_ref, full_ref):
    x = x_ref[...]
    width = x.shape[0]
    full_ref[...] = lax.dot_general(
        x, x, (((1,), (1,)), ((), ())), preferred_element_type=jnp.float32
    )
    even = full_ref[pl.ds(0, width // 2, stride=2), :]
    odd = full_ref[pl.ds(1, width // 2, stride=2), :]
    lane = lax.broadcasted_iota(jnp.int32, odd.shape, 1)
    out_ref[...] = even - rotated(odd, lane)


def complex_gram(x):
    width = x.shape[0]
    return pl.pallas_call(
        gram_kernel,
        out_shape=jax.ShapeDtypeStruct((width // 2, width), jnp.float32),
        in_specs=[pl.BlockSpec(memory_space=pltpu.VMEM)],
        out_specs=pl.BlockSpec(memory_space=pltpu.VMEM),
        scratch_shapes=[pltpu.VMEM((width, width), jnp.float32)],
        name="gram",
    )(x)


def eliminate(rows, panel):
    count = len(rows)
    shape = rows[0].shape
    sub = lax.broadcasted_iota(jnp.int32, shape, 0)
    lane = lax.broadcasted_iota(jnp.int32, shape, 1)

    def over_lanes(x, at):
        return jnp.broadcast_to(x[:, at:at + 1], shape)

    def over_rows(x, at):
        return jnp.broadcast_to(x[at:at + 1, :], shape)

    rows = list(rows)
    pivots = [jnp.ones(shape, jnp.float32) for _ in range(count)]
    for first in range(0, count * SUB, panel):
        own = first // SUB
        live = range(own, count)
        re = [{i: over_lanes(rows[i], 2 * (first + c)) for i in live} for c in range(panel)]
        im = [{i: over_lanes(rows[i], 2 * (first + c) + 1) for i in live} for c in range(panel)]
        head, turned = rows[own], rotated(rows[own], lane)
        for c in range(panel):
            at = (first + c) % SUB
            k = first + c
            pivot = over_rows(re[c][own], at)
            pivots[own] = jnp.where(sub == at, pivot, pivots[own])
            inverse = 1.0 / pivot
            upper = {
                later: (over_rows(re[later][own], at), over_rows(im[later][own], at))
                for later in range(c + 1, panel)
            }
            for i in live:
                re[c][i] = re[c][i] * inverse
                im[c][i] = im[c][i] * inverse
                for later, (u_re, u_im) in upper.items():
                    re[later][i] = re[later][i] - (re[c][i] * u_re - im[c][i] * u_im)
                    im[later][i] = im[later][i] - (re[c][i] * u_im + im[c][i] * u_re)
            below = sub > at
            m_re = jnp.where(below, re[c][own], 0.0)
            m_im = jnp.where(below, im[c][own], 0.0)
            on_re, on_im = lane == 2 * k, lane == 2 * k + 1
            p = jnp.where(on_re, 1.0, jnp.where(on_im, 0.0, over_rows(head, at)))
            q = jnp.where(on_im, 1.0, jnp.where(on_re, 0.0, over_rows(turned, at)))
            cleared = below & (on_re | on_im)
            head = jnp.where(cleared, 0.0, head) - (m_re * p + m_im * q)
            turned = jnp.where(cleared, 0.0, turned) - (m_re * q - m_im * p)
        rows[own] = head
        if own + 1 == count:
            continue
        inside = (lane >= 2 * first) & (lane < 2 * (first + panel))
        rest = {i: jnp.where(inside, 0.0, rows[i]) for i in range(own + 1, count)}
        for c in range(panel):
            at = (first + c) % SUB
            k = first + c
            on_re, on_im = lane == 2 * k, lane == 2 * k + 1
            drop = (lane >= 2 * k) & (lane < 2 * (first + panel))
            p = jnp.where(on_re, 1.0, jnp.where(drop, 0.0, over_rows(head, at)))
            q = jnp.where(on_im, 1.0, jnp.where(drop, 0.0, over_rows(turned, at)))
            for i in rest:
                rest[i] = rest[i] - (re[c][i] * p + im[c][i] * q)
        for i in rest:
            rows[i] = rest[i]
    return rows, pivots


def modes_kernel(scale, x_ref, own_ref, other_ref, modes_ref, factor_ref, basis_ref, upper_ref):
    size = own_ref.shape[0]
    count = size // SUB
    rows = [
        (own_ref[i * SUB:(i + 1) * SUB, :] + other_ref[i * SUB:(i + 1) * SUB, :]) * scale
        for i in range(count)
    ]
    rows, pivots = eliminate(rows, PANEL)
    shape = rows[0].shape
    sub = lax.broadcasted_iota(jnp.int32, shape, 0)
    lane = lax.broadcasted_iota(jnp.int32, shape, 1)
    for i in range(count):
        root = lax.rsqrt(pivots[i])
        diagonal = 2 * (i * SUB + sub)
        right = jnp.where(lane > diagonal + 1, rows[i], jnp.where(lane == diagonal, pivots[i], 0.0))
        left = jnp.where(lane < diagonal, rows[i], jnp.where(lane == diagonal, 1.0, 0.0))
        upper_ref[i * SUB:(i + 1) * SUB, :] = right * root
        left = left * root
        basis_ref[pl.ds(2 * i * SUB, SUB, stride=2), :] = left
        basis_ref[pl.ds(2 * i * SUB + 1, SUB, stride=2), :] = rotated(left, lane)
    points = jnp.transpose(x_ref[...])
    basis = basis_ref[...]
    high = basis.astype(jnp.bfloat16)
    low = (basis - high.astype(jnp.float32)).astype(jnp.bfloat16)
    contract = (((1,), (1,)), ((), ()))
    modes_ref[...] = lax.dot_general(
        points, high, contract, preferred_element_type=jnp.float32
    ) + lax.dot_general(points, low, contract, preferred_element_type=jnp.float32)
    lane_in = lax.broadcasted_iota(jnp.int32, (2 * size, size), 0)
    lane_out = lax.broadcasted_iota(jnp.int32, (2 * size, size), 1)
    for part in range(2):
        pick = (lane_in == 2 * lane_out + part).astype(jnp.float32)
        factor_ref[part] = jnp.dot(
            upper_ref[...], pick,
            precision=lax.Precision.HIGHEST, preferred_element_type=jnp.float32,
        )


def modes_and_factor(x, own, other, scale):
    width, points = x.shape
    size = width // 2
    return pl.pallas_call(
        functools.partial(modes_kernel, scale),
        out_shape=(
            jax.ShapeDtypeStruct((points, width), jnp.float32),
            jax.ShapeDtypeStruct((2, size, size), jnp.float32),
        ),
        in_specs=[pl.BlockSpec(memory_space=pltpu.VMEM)] * 3,
        out_specs=(pl.BlockSpec(memory_space=pltpu.VMEM),) * 2,
        scratch_shapes=[
            pltpu.VMEM((width, width), jnp.float32),
            pltpu.VMEM((size, width), jnp.float32),
        ],
        compiler_params=pltpu.CompilerParams(vmem_limit_bytes=24 * 2**20),
        name="factor_and_modes",
    )(x, own, other)


def local(slabs, snapshots, row_scales, block_offsets, freq_index):
    freqs = freq_index.shape[0]
    points = snapshots.shape[1]
    spectra = block_spectra(snapshots, row_scales, block_offsets, freq_index)
    chunks = spectra.reshape(freqs, -1, points)
    regrouped = lax.all_to_all(chunks, "blk", split_axis=0, concat_axis=0, tiled=True)
    x = regrouped.reshape(-1, points)
    own = complex_gram(x)
    if slabs == 2:
        other = lax.ppermute(own, "space", [(0, 1), (1, 0)])
    else:
        own, other = lax.psum(own, "space"), jnp.zeros_like(own)
    modes, factor = modes_and_factor(x, own, other, 1.0 / (points * slabs))
    return modes[None], factor[None]


def solution(mesh):
    return jax.shard_map(
        functools.partial(local, mesh.shape["space"]),
        mesh=mesh,
        in_specs=(P("blk", "space"), P("blk"), P("blk"), P()),
        out_specs=(P("blk", "space", None), P("blk", None, None, None)),
        check_vma=False,
    )
```

```python
import functools
import math

import jax
import jax.numpy as jnp
from jax import lax
from jax.experimental import pallas as pl
from jax.experimental.pallas import tpu as pltpu
from jax.sharding import PartitionSpec as P

NFFT = 512
PANEL = 4
SUB = 8
PIECE = 256
SIN_COEFS = (
    0.9999999765895043,
    -0.1666664763439475,
    0.008332899819203531,
    -0.0001980089750772882,
    2.5904879854375602e-06,
)


def cos_of_phase(phase):
    folded = jnp.abs((phase & (NFFT - 1)) - NFFT // 2) - NFFT // 4
    x = folded.astype(jnp.float32) * (2.0 * math.pi / NFFT)
    square = x * x
    total = jnp.full_like(x, SIN_COEFS[-1])
    for coef in SIN_COEFS[-2::-1]:
        total = total * square + coef
    return total * x


def spectra_kernel(
    snap_hbm, scales_hbm, offsets_hbm, freq_hbm, out_ref,
    snap_ref, scales_ref, offsets_ref, freq_ref, coef_ref, small_sems, snap_sems,
):
    snaps = snap_ref.shape[0]
    blocks = offsets_ref.shape[0]
    rows = 2 * blocks
    freqs = freq_ref.shape[0]
    small = [
        pltpu.make_async_copy(src, dst, small_sems.at[i])
        for i, (src, dst) in enumerate(
            ((offsets_hbm, offsets_ref), (freq_hbm, freq_ref), (scales_hbm, scales_ref))
        )
    ]
    pieces = [slice(at, min(at + PIECE, snaps)) for at in range(0, snaps, PIECE)]
    large = [
        pltpu.make_async_copy(snap_hbm.at[piece], snap_ref.at[piece], snap_sems.at[i])
        for i, piece in enumerate(pieces)
    ]
    for copy in small + large:
        copy.start()
    row = lax.broadcasted_iota(jnp.int32, (rows, snaps), 0)
    time = lax.broadcasted_iota(jnp.int32, (rows, snaps), 1)
    for copy in small:
        copy.wait()
    start = jnp.zeros((rows, snaps), jnp.int32)
    for b in range(blocks):
        start = jnp.where(row // 2 == b, offsets_ref[b], start)
    shifted = time - start
    hann = 0.5 - 0.5 * cos_of_phase(shifted)
    inside = (shifted >= 0) & (shifted < NFFT)
    scales = jnp.broadcast_to(scales_ref[...].reshape(1, snaps), (rows, snaps))
    weight = jnp.where(inside, hann * scales * (1.0 / math.sqrt(NFFT)), 0.0)
    base = shifted[:, :NFFT].astype(jnp.float32)
    quarter = (row[:, :NFFT] % 2) * (NFFT // 4)
    repeats = -(-snaps // NFFT)

    def rows_of(f):
        freq = freq_ref[f].astype(jnp.float32)
        table = cos_of_phase((base * freq).astype(jnp.int32) + quarter)
        return jnp.concatenate([table] * repeats, 1)[:, :snaps] * weight

    for f in range(0, freqs, 2):
        pair = jnp.concatenate([rows_of(f), rows_of(f + 1)], 0)
        coef_ref[f * rows:(f + 2) * rows, :] = pair.astype(jnp.bfloat16)
    total = jnp.zeros(out_ref.shape, jnp.float32)
    for copy, piece in zip(large, pieces):
        copy.wait()
        total += jnp.dot(
            coef_ref[:, piece], snap_ref[piece], preferred_element_type=jnp.float32
        )
    out_ref[...] = total.astype(jnp.bfloat16)


def block_spectra(snapshots, row_scales, block_offsets, freq_index):
    snaps, points = snapshots.shape
    rows = 2 * block_offsets.shape[0] * freq_index.shape[0]
    pieces = -(-snaps // PIECE)
    return pl.pallas_call(
        spectra_kernel,
        out_shape=jax.ShapeDtypeStruct((rows, points), jnp.bfloat16),
        in_specs=[pl.BlockSpec(memory_space=pltpu.HBM)] * 4,
        out_specs=pl.BlockSpec(memory_space=pltpu.VMEM),
        scratch_shapes=[
            pltpu.VMEM((snaps, points), jnp.bfloat16),
            pltpu.VMEM((snaps,), jnp.float32),
            pltpu.SMEM(block_offsets.shape, jnp.int32),
            pltpu.SMEM(freq_index.shape, jnp.int32),
            pltpu.VMEM((rows, snaps), jnp.bfloat16),
            pltpu.SemaphoreType.DMA((3,)),
            pltpu.SemaphoreType.DMA((pieces,)),
        ],
        compiler_params=pltpu.CompilerParams(vmem_limit_bytes=60 * 2**20),
        name="spectra",
    )(snapshots, row_scales, block_offsets, freq_index)


def rotated(x, lane):
    axis = x.ndim - 1
    width = x.shape[axis]
    after = pltpu.roll(x, width - 1, axis)
    before = pltpu.roll(x, 1, axis)
    return jnp.where(lane % 2 == 0, -after, before)


def gram_kernel(x_ref, out_ref, full_ref):
    x = x_ref[...]
    width = x.shape[0]
    full_ref[...] = lax.dot_general(
        x, x, (((1,), (1,)), ((), ())), preferred_element_type=jnp.float32
    )
    even = full_ref[pl.ds(0, width // 2, stride=2), :]
    odd = full_ref[pl.ds(1, width // 2, stride=2), :]
    lane = lax.broadcasted_iota(jnp.int32, odd.shape, 1)
    out_ref[...] = even - rotated(odd, lane)


def complex_gram(x):
    width = x.shape[0]
    return pl.pallas_call(
        gram_kernel,
        out_shape=jax.ShapeDtypeStruct((width // 2, width), jnp.float32),
        in_specs=[pl.BlockSpec(memory_space=pltpu.VMEM)],
        out_specs=pl.BlockSpec(memory_space=pltpu.VMEM),
        scratch_shapes=[pltpu.VMEM((width, width), jnp.float32)],
        compiler_params=pltpu.CompilerParams(vmem_limit_bytes=4 * 2**20),
        name="gram",
    )(x)


def eliminate(rows, panel):
    count = len(rows)
    shape = rows[0].shape
    sub = lax.broadcasted_iota(jnp.int32, shape, 0)
    lane = lax.broadcasted_iota(jnp.int32, shape, 1)

    def over_lanes(x, at):
        return jnp.broadcast_to(x[:, at:at + 1], shape)

    def over_rows(x, at):
        return jnp.broadcast_to(x[at:at + 1, :], shape)

    rows = list(rows)
    pivots = [jnp.ones(shape, jnp.float32) for _ in range(count)]
    for first in range(0, count * SUB, panel):
        own = first // SUB
        live = range(own, count)
        re = [{i: over_lanes(rows[i], 2 * (first + c)) for i in live} for c in range(panel)]
        im = [{i: over_lanes(rows[i], 2 * (first + c) + 1) for i in live} for c in range(panel)]
        head, turned = rows[own], rotated(rows[own], lane)
        for c in range(panel):
            at = (first + c) % SUB
            k = first + c
            pivot = over_rows(re[c][own], at)
            pivots[own] = jnp.where(sub == at, pivot, pivots[own])
            inverse = 1.0 / pivot
            upper = {
                later: (over_rows(re[later][own], at), over_rows(im[later][own], at))
                for later in range(c + 1, panel)
            }
            for i in live:
                re[c][i] = re[c][i] * inverse
                im[c][i] = im[c][i] * inverse
                for later, (u_re, u_im) in upper.items():
                    re[later][i] = re[later][i] - (re[c][i] * u_re - im[c][i] * u_im)
                    im[later][i] = im[later][i] - (re[c][i] * u_im + im[c][i] * u_re)
            below = sub > at
            m_re = jnp.where(below, re[c][own], 0.0)
            m_im = jnp.where(below, im[c][own], 0.0)
            on_re, on_im = lane == 2 * k, lane == 2 * k + 1
            p = jnp.where(on_re, 1.0, jnp.where(on_im, 0.0, over_rows(head, at)))
            q = jnp.where(on_im, 1.0, jnp.where(on_re, 0.0, over_rows(turned, at)))
            cleared = below & (on_re | on_im)
            head = jnp.where(cleared, 0.0, head) - (m_re * p + m_im * q)
            turned = jnp.where(cleared, 0.0, turned) - (m_re * q - m_im * p)
        rows[own] = head
        if own + 1 == count:
            continue
        inside = (lane >= 2 * first) & (lane < 2 * (first + panel))
        rest = {i: jnp.where(inside, 0.0, rows[i]) for i in range(own + 1, count)}
        for c in range(panel):
            at = (first + c) % SUB
            k = first + c
            on_re, on_im = lane == 2 * k, lane == 2 * k + 1
            drop = (lane >= 2 * k) & (lane < 2 * (first + panel))
            p = jnp.where(on_re, 1.0, jnp.where(drop, 0.0, over_rows(head, at)))
            q = jnp.where(on_im, 1.0, jnp.where(drop, 0.0, over_rows(turned, at)))
            for i in rest:
                rest[i] = rest[i] - (re[c][i] * p + im[c][i] * q)
        for i in rest:
            rows[i] = rest[i]
    return rows, pivots


def modes_kernel(scale, x_ref, own_ref, other_ref, modes_ref, factor_ref, basis_ref, upper_ref):
    size = own_ref.shape[0]
    count = size // SUB
    rows = [
        (own_ref[i * SUB:(i + 1) * SUB, :] + other_ref[i * SUB:(i + 1) * SUB, :]) * scale
        for i in range(count)
    ]
    rows, pivots = eliminate(rows, PANEL)
    shape = rows[0].shape
    sub = lax.broadcasted_iota(jnp.int32, shape, 0)
    lane = lax.broadcasted_iota(jnp.int32, shape, 1)
    for i in range(count):
        root = lax.rsqrt(pivots[i])
        diagonal = 2 * (i * SUB + sub)
        right = jnp.where(lane > diagonal + 1, rows[i], jnp.where(lane == diagonal, pivots[i], 0.0))
        left = jnp.where(lane < diagonal, rows[i], jnp.where(lane == diagonal, 1.0, 0.0))
        upper_ref[i * SUB:(i + 1) * SUB, :] = right * root
        left = left * root
        basis_ref[pl.ds(2 * i * SUB, SUB, stride=2), :] = left
        basis_ref[pl.ds(2 * i * SUB + 1, SUB, stride=2), :] = rotated(left, lane)
    points = jnp.transpose(x_ref[...])
    basis = basis_ref[...]
    high = basis.astype(jnp.bfloat16)
    low = (basis - high.astype(jnp.float32)).astype(jnp.bfloat16)
    contract = (((1,), (1,)), ((), ()))
    modes_ref[...] = lax.dot_general(
        points, high, contract, preferred_element_type=jnp.float32
    ) + lax.dot_general(points, low, contract, preferred_element_type=jnp.float32)
    lane_in = lax.broadcasted_iota(jnp.int32, (2 * size, size), 0)
    lane_out = lax.broadcasted_iota(jnp.int32, (2 * size, size), 1)
    for part in range(2):
        pick = (lane_in == 2 * lane_out + part).astype(jnp.float32)
        factor_ref[part] = jnp.dot(
            upper_ref[...], pick,
            precision=lax.Precision.HIGHEST, preferred_element_type=jnp.float32,
        )


def modes_and_factor(x, own, other, scale):
    width, points = x.shape
    size = width // 2
    return pl.pallas_call(
        functools.partial(modes_kernel, scale),
        out_shape=(
            jax.ShapeDtypeStruct((points, width), jnp.float32),
            jax.ShapeDtypeStruct((2, size, size), jnp.float32),
        ),
        in_specs=[pl.BlockSpec(memory_space=pltpu.VMEM)] * 3,
        out_specs=(pl.BlockSpec(memory_space=pltpu.VMEM),) * 2,
        scratch_shapes=[
            pltpu.VMEM((width, width), jnp.float32),
            pltpu.VMEM((size, width), jnp.float32),
        ],
        compiler_params=pltpu.CompilerParams(vmem_limit_bytes=8 * 2**20),
        name="factor_and_modes",
    )(x, own, other)


def local(slabs, snapshots, row_scales, block_offsets, freq_index):
    freqs = freq_index.shape[0]
    points = snapshots.shape[1]
    spectra = block_spectra(snapshots, row_scales, block_offsets, freq_index)
    chunks = spectra.reshape(freqs, -1, points)
    regrouped = lax.all_to_all(chunks, "blk", split_axis=0, concat_axis=0, tiled=True)
    x = regrouped.reshape(-1, points)
    own = complex_gram(x)
    if slabs == 2:
        other = lax.ppermute(own, "space", [(0, 1), (1, 0)])
    else:
        own, other = lax.psum(own, "space"), jnp.zeros_like(own)
    modes, factor = modes_and_factor(x, own, other, 1.0 / (points * slabs))
    return modes[None], factor[None]


def solution(mesh):
    return jax.shard_map(
        functools.partial(local, mesh.shape["space"]),
        mesh=mesh,
        in_specs=(P("blk", "space"), P("blk"), P("blk"), P()),
        out_specs=(P("blk", "space", None), P("blk", None, None, None)),
        check_vma=False,
    )
```

```python
import functools
import math

import jax
import jax.numpy as jnp
from jax import lax
from jax.experimental import pallas as pl
from jax.experimental.pallas import tpu as pltpu
from jax.sharding import PartitionSpec as P

NFFT = 512
PANEL = 4
SUB = 8
PIECE = 256
INNER = 4
SIN_COEFS = (
    0.9999999765895043,
    -0.1666664763439475,
    0.008332899819203531,
    -0.0001980089750772882,
    2.5904879854375602e-06,
)


def cos_of_phase(phase):
    folded = jnp.abs((phase & (NFFT - 1)) - NFFT // 2) - NFFT // 4
    x = folded.astype(jnp.float32) * (2.0 * math.pi / NFFT)
    square = x * x
    total = jnp.full_like(x, SIN_COEFS[-1])
    for coef in SIN_COEFS[-2::-1]:
        total = total * square + coef
    return total * x


def spectra_kernel(
    outer, inner, snap_hbm, scales_hbm, offsets_hbm, freq_hbm, out_ref,
    snap_ref, scales_ref, offsets_ref, freq_ref, coef_ref, small_sems, snap_sems,
):
    snaps = snap_ref.shape[0]
    blocks = offsets_ref.shape[0]
    rows = 2 * blocks
    freqs = freq_ref.shape[0]
    small = [
        pltpu.make_async_copy(src, dst, small_sems.at[i])
        for i, (src, dst) in enumerate(
            ((offsets_hbm, offsets_ref), (freq_hbm, freq_ref), (scales_hbm, scales_ref))
        )
    ]
    pieces = [slice(at, min(at + PIECE, snaps)) for at in range(0, snaps, PIECE)]
    large = [
        pltpu.make_async_copy(snap_hbm.at[piece], snap_ref.at[piece], snap_sems.at[i])
        for i, piece in enumerate(pieces)
    ]
    for copy in small + large:
        copy.start()
    row = lax.broadcasted_iota(jnp.int32, (rows, snaps), 0)
    time = lax.broadcasted_iota(jnp.int32, (rows, snaps), 1)
    for copy in small:
        copy.wait()
    start = jnp.zeros((rows, snaps), jnp.int32)
    for b in range(blocks):
        start = jnp.where(row // 2 == b, offsets_ref[b], start)
    shifted = time - start
    hann = 0.5 - 0.5 * cos_of_phase(shifted)
    inside = (shifted >= 0) & (shifted < NFFT)
    scales = jnp.broadcast_to(scales_ref[...].reshape(1, snaps), (rows, snaps))
    weight = jnp.where(inside, hann * scales * (1.0 / math.sqrt(NFFT)), 0.0)
    base = shifted[:, :NFFT].astype(jnp.float32)
    quarter = (row[:, :NFFT] % 2) * (NFFT // 4)
    repeats = -(-snaps // NFFT)

    def rows_of(g):
        f = g % outer * inner + g // outer
        freq = freq_ref[f].astype(jnp.float32)
        table = cos_of_phase((base * freq).astype(jnp.int32) + quarter)
        return jnp.concatenate([table] * repeats, 1)[:, :snaps] * weight

    for f in range(0, freqs, 2):
        pair = jnp.concatenate([rows_of(f), rows_of(f + 1)], 0)
        coef_ref[f * rows:(f + 2) * rows, :] = pair.astype(jnp.bfloat16)
    total = jnp.zeros(out_ref.shape, jnp.float32)
    for copy, piece in zip(large, pieces):
        copy.wait()
        total += jnp.dot(
            coef_ref[:, piece], snap_ref[piece], preferred_element_type=jnp.float32
        )
    out_ref[...] = total.astype(jnp.bfloat16)


def block_spectra(snapshots, row_scales, block_offsets, freq_index, outer, inner):
    snaps, points = snapshots.shape
    rows = 2 * block_offsets.shape[0] * freq_index.shape[0]
    pieces = -(-snaps // PIECE)
    return pl.pallas_call(
        functools.partial(spectra_kernel, outer, inner),
        out_shape=jax.ShapeDtypeStruct((rows, points), jnp.bfloat16),
        in_specs=[pl.BlockSpec(memory_space=pltpu.HBM)] * 4,
        out_specs=pl.BlockSpec(memory_space=pltpu.VMEM),
        scratch_shapes=[
            pltpu.VMEM((snaps, points), jnp.bfloat16),
            pltpu.VMEM((snaps,), jnp.float32),
            pltpu.SMEM(block_offsets.shape, jnp.int32),
            pltpu.SMEM(freq_index.shape, jnp.int32),
            pltpu.VMEM((rows, snaps), jnp.bfloat16),
            pltpu.SemaphoreType.DMA((3,)),
            pltpu.SemaphoreType.DMA((pieces,)),
        ],
        compiler_params=pltpu.CompilerParams(vmem_limit_bytes=60 * 2**20),
        name="spectra",
    )(snapshots, row_scales, block_offsets, freq_index)


def rotated(x, lane):
    axis = x.ndim - 1
    width = x.shape[axis]
    after = pltpu.roll(x, width - 1, axis)
    before = pltpu.roll(x, 1, axis)
    return jnp.where(lane % 2 == 0, -after, before)


def gram_kernel(x_ref, out_ref, full_ref):
    x = x_ref[...]
    width = x.shape[0]
    full_ref[...] = lax.dot_general(
        x, x, (((1,), (1,)), ((), ())), preferred_element_type=jnp.float32
    )
    even = full_ref[pl.ds(0, width // 2, stride=2), :]
    odd = full_ref[pl.ds(1, width // 2, stride=2), :]
    lane = lax.broadcasted_iota(jnp.int32, odd.shape, 1)
    out_ref[...] = even - rotated(odd, lane)


def complex_gram(x):
    width = x.shape[0]
    return pl.pallas_call(
        gram_kernel,
        out_shape=jax.ShapeDtypeStruct((width // 2, width), jnp.float32),
        in_specs=[pl.BlockSpec(memory_space=pltpu.VMEM)],
        out_specs=pl.BlockSpec(memory_space=pltpu.VMEM),
        scratch_shapes=[pltpu.VMEM((width, width), jnp.float32)],
        compiler_params=pltpu.CompilerParams(vmem_limit_bytes=4 * 2**20),
        name="gram",
    )(x)


def eliminate(rows, panel):
    count = len(rows)
    shape = rows[0].shape
    sub = lax.broadcasted_iota(jnp.int32, shape, 0)
    lane = lax.broadcasted_iota(jnp.int32, shape, 1)

    def over_lanes(x, at):
        return jnp.broadcast_to(x[:, at:at + 1], shape)

    def over_rows(x, at):
        return jnp.broadcast_to(x[at:at + 1, :], shape)

    rows = list(rows)
    pivots = [jnp.ones(shape, jnp.float32) for _ in range(count)]
    for first in range(0, count * SUB, panel):
        own = first // SUB
        live = range(own, count)
        re = [{i: over_lanes(rows[i], 2 * (first + c)) for i in live} for c in range(panel)]
        im = [{i: over_lanes(rows[i], 2 * (first + c) + 1) for i in live} for c in range(panel)]
        head, turned = rows[own], rotated(rows[own], lane)
        for c in range(panel):
            at = (first + c) % SUB
            k = first + c
            pivot = over_rows(re[c][own], at)
            pivots[own] = jnp.where(sub == at, pivot, pivots[own])
            inverse = 1.0 / pivot
            upper = {
                later: (over_rows(re[later][own], at), over_rows(im[later][own], at))
                for later in range(c + 1, panel)
            }
            for i in live:
                re[c][i] = re[c][i] * inverse
                im[c][i] = im[c][i] * inverse
                for later, (u_re, u_im) in upper.items():
                    re[later][i] = re[later][i] - (re[c][i] * u_re - im[c][i] * u_im)
                    im[later][i] = im[later][i] - (re[c][i] * u_im + im[c][i] * u_re)
            below = sub > at
            m_re = jnp.where(below, re[c][own], 0.0)
            m_im = jnp.where(below, im[c][own], 0.0)
            on_re, on_im = lane == 2 * k, lane == 2 * k + 1
            p = jnp.where(on_re, 1.0, jnp.where(on_im, 0.0, over_rows(head, at)))
            q = jnp.where(on_im, 1.0, jnp.where(on_re, 0.0, over_rows(turned, at)))
            cleared = below & (on_re | on_im)
            head = jnp.where(cleared, 0.0, head) - (m_re * p + m_im * q)
            turned = jnp.where(cleared, 0.0, turned) - (m_re * q - m_im * p)
        rows[own] = head
        if own + 1 == count:
            continue
        inside = (lane >= 2 * first) & (lane < 2 * (first + panel))
        rest = {i: jnp.where(inside, 0.0, rows[i]) for i in range(own + 1, count)}
        for c in range(panel):
            at = (first + c) % SUB
            k = first + c
            on_re, on_im = lane == 2 * k, lane == 2 * k + 1
            drop = (lane >= 2 * k) & (lane < 2 * (first + panel))
            p = jnp.where(on_re, 1.0, jnp.where(drop, 0.0, over_rows(head, at)))
            q = jnp.where(on_im, 1.0, jnp.where(drop, 0.0, over_rows(turned, at)))
            for i in rest:
                rest[i] = rest[i] - (re[c][i] * p + im[c][i] * q)
        for i in rest:
            rows[i] = rest[i]
    return rows, pivots


def modes_kernel(scale, x_ref, own_ref, other_ref, modes_ref, factor_ref, basis_ref, upper_ref):
    size = own_ref.shape[0]
    count = size // SUB
    rows = [
        (own_ref[i * SUB:(i + 1) * SUB, :] + other_ref[i * SUB:(i + 1) * SUB, :]) * scale
        for i in range(count)
    ]
    rows, pivots = eliminate(rows, PANEL)
    shape = rows[0].shape
    sub = lax.broadcasted_iota(jnp.int32, shape, 0)
    lane = lax.broadcasted_iota(jnp.int32, shape, 1)
    for i in range(count):
        root = lax.rsqrt(pivots[i])
        diagonal = 2 * (i * SUB + sub)
        right = jnp.where(lane > diagonal + 1, rows[i], jnp.where(lane == diagonal, pivots[i], 0.0))
        left = jnp.where(lane < diagonal, rows[i], jnp.where(lane == diagonal, 1.0, 0.0))
        upper_ref[i * SUB:(i + 1) * SUB, :] = right * root
        left = left * root
        basis_ref[pl.ds(2 * i * SUB, SUB, stride=2), :] = left
        basis_ref[pl.ds(2 * i * SUB + 1, SUB, stride=2), :] = rotated(left, lane)
    points = jnp.transpose(x_ref[...])
    basis = basis_ref[...]
    high = basis.astype(jnp.bfloat16)
    low = (basis - high.astype(jnp.float32)).astype(jnp.bfloat16)
    contract = (((1,), (1,)), ((), ()))
    modes_ref[...] = lax.dot_general(
        points, high, contract, preferred_element_type=jnp.float32
    ) + lax.dot_general(points, low, contract, preferred_element_type=jnp.float32)
    lane_in = lax.broadcasted_iota(jnp.int32, (2 * size, size), 0)
    lane_out = lax.broadcasted_iota(jnp.int32, (2 * size, size), 1)
    for part in range(2):
        pick = (lane_in == 2 * lane_out + part).astype(jnp.float32)
        factor_ref[part] = jnp.dot(
            upper_ref[...], pick,
            precision=lax.Precision.HIGHEST, preferred_element_type=jnp.float32,
        )


def modes_and_factor(x, own, other, scale):
    width, points = x.shape
    size = width // 2
    return pl.pallas_call(
        functools.partial(modes_kernel, scale),
        out_shape=(
            jax.ShapeDtypeStruct((points, width), jnp.float32),
            jax.ShapeDtypeStruct((2, size, size), jnp.float32),
        ),
        in_specs=[pl.BlockSpec(memory_space=pltpu.VMEM)] * 3,
        out_specs=(pl.BlockSpec(memory_space=pltpu.VMEM),) * 2,
        scratch_shapes=[
            pltpu.VMEM((width, width), jnp.float32),
            pltpu.VMEM((size, width), jnp.float32),
        ],
        compiler_params=pltpu.CompilerParams(vmem_limit_bytes=8 * 2**20),
        name="factor_and_modes",
    )(x, own, other)


def local(slabs, owners, snapshots, row_scales, block_offsets, freq_index):
    freqs = freq_index.shape[0]
    points = snapshots.shape[1]
    inner = math.gcd(owners, INNER)
    outer = owners // inner
    spectra = block_spectra(snapshots, row_scales, block_offsets, freq_index, outer, inner)
    chunks = spectra.reshape(inner, outer, -1, points)
    near = [[o * inner + i for i in range(inner)] for o in range(outer)]
    far = [[o * inner + i for o in range(outer)] for i in range(inner)]
    swap = functools.partial(lax.all_to_all, axis_name="blk", split_axis=0, concat_axis=0, tiled=True)
    chunks = swap(chunks, axis_index_groups=near).transpose(1, 0, 2, 3)
    regrouped = swap(chunks, axis_index_groups=far)
    x = regrouped.reshape(-1, points)
    own = complex_gram(x)
    if slabs == 2:
        other = lax.ppermute(own, "space", [(0, 1), (1, 0)])
    else:
        own, other = lax.psum(own, "space"), jnp.zeros_like(own)
    modes, factor = modes_and_factor(x, own, other, 1.0 / (points * slabs))
    return modes[None], factor[None]


def solution(mesh):
    return jax.shard_map(
        functools.partial(local, mesh.shape["space"], mesh.shape["blk"]),
        mesh=mesh,
        in_specs=(P("blk", "space"), P("blk"), P("blk"), P()),
        out_specs=(P("blk", "space", None), P("blk", None, None, None)),
        check_vma=False,
    )
```

```python
import functools
import math

import jax
import jax.numpy as jnp
from jax import lax
from jax.experimental import pallas as pl
from jax.experimental.pallas import tpu as pltpu
from jax.sharding import PartitionSpec as P

NFFT = 512
PANEL = 4
SUB = 8
PIECE = 256
FEW_SLABS = 2
SIN_COEFS = (
    0.9999999765895043,
    -0.1666664763439475,
    0.008332899819203531,
    -0.0001980089750772882,
    2.5904879854375602e-06,
)


def cos_of_phase(phase):
    folded = jnp.abs((phase & (NFFT - 1)) - NFFT // 2) - NFFT // 4
    x = folded.astype(jnp.float32) * (2.0 * math.pi / NFFT)
    square = x * x
    total = jnp.full_like(x, SIN_COEFS[-1])
    for coef in SIN_COEFS[-2::-1]:
        total = total * square + coef
    return total * x


def spectra_kernel(
    snap_hbm, scales_hbm, offsets_hbm, freq_hbm, out_ref,
    snap_ref, scales_ref, offsets_ref, freq_ref, coef_ref, small_sems, snap_sems,
):
    snaps = snap_ref.shape[0]
    blocks = offsets_ref.shape[0]
    rows = 2 * blocks
    freqs = freq_ref.shape[0]
    small = [
        pltpu.make_async_copy(src, dst, small_sems.at[i])
        for i, (src, dst) in enumerate(
            ((offsets_hbm, offsets_ref), (freq_hbm, freq_ref), (scales_hbm, scales_ref))
        )
    ]
    pieces = [slice(at, min(at + PIECE, snaps)) for at in range(0, snaps, PIECE)]
    large = [
        pltpu.make_async_copy(snap_hbm.at[piece], snap_ref.at[piece], snap_sems.at[i])
        for i, piece in enumerate(pieces)
    ]
    for copy in small + large:
        copy.start()
    row = lax.broadcasted_iota(jnp.int32, (rows, snaps), 0)
    time = lax.broadcasted_iota(jnp.int32, (rows, snaps), 1)
    for copy in small:
        copy.wait()
    start = jnp.zeros((rows, snaps), jnp.int32)
    for b in range(blocks):
        start = jnp.where(row // 2 == b, offsets_ref[b], start)
    shifted = time - start
    hann = 0.5 - 0.5 * cos_of_phase(shifted)
    inside = (shifted >= 0) & (shifted < NFFT)
    scales = jnp.broadcast_to(scales_ref[...].reshape(1, snaps), (rows, snaps))
    weight = jnp.where(inside, hann * scales * (1.0 / math.sqrt(NFFT)), 0.0)
    base = shifted[:, :NFFT].astype(jnp.float32)
    quarter = (row[:, :NFFT] % 2) * (NFFT // 4)
    repeats = -(-snaps // NFFT)

    def rows_of(f):
        freq = freq_ref[f].astype(jnp.float32)
        table = cos_of_phase((base * freq).astype(jnp.int32) + quarter)
        return jnp.concatenate([table] * repeats, 1)[:, :snaps] * weight

    for f in range(0, freqs, 2):
        pair = jnp.concatenate([rows_of(f), rows_of(f + 1)], 0)
        coef_ref[f * rows:(f + 2) * rows, :] = pair.astype(jnp.bfloat16)
    total = jnp.zeros(out_ref.shape[1:], jnp.float32)
    for copy, piece in zip(large, pieces):
        copy.wait()
        total += jnp.dot(
            coef_ref[:, piece], snap_ref[piece], preferred_element_type=jnp.float32
        )
    result = total.astype(jnp.bfloat16)
    for copy in range(out_ref.shape[0]):
        out_ref[copy] = result


def block_spectra(copies, snapshots, row_scales, block_offsets, freq_index):
    snaps, points = snapshots.shape
    rows = 2 * block_offsets.shape[0] * freq_index.shape[0]
    pieces = -(-snaps // PIECE)
    return pl.pallas_call(
        spectra_kernel,
        out_shape=jax.ShapeDtypeStruct((copies, rows, points), jnp.bfloat16),
        in_specs=[pl.BlockSpec(memory_space=pltpu.HBM)] * 4,
        out_specs=pl.BlockSpec(memory_space=pltpu.VMEM),
        scratch_shapes=[
            pltpu.VMEM((snaps, points), jnp.bfloat16),
            pltpu.VMEM((snaps,), jnp.float32),
            pltpu.SMEM(block_offsets.shape, jnp.int32),
            pltpu.SMEM(freq_index.shape, jnp.int32),
            pltpu.VMEM((rows, snaps), jnp.bfloat16),
            pltpu.SemaphoreType.DMA((3,)),
            pltpu.SemaphoreType.DMA((pieces,)),
        ],
        compiler_params=pltpu.CompilerParams(vmem_limit_bytes=60 * 2**20),
        name="spectra",
    )(snapshots, row_scales, block_offsets, freq_index)


def rotated(x, lane):
    axis = x.ndim - 1
    width = x.shape[axis]
    after = pltpu.roll(x, width - 1, axis)
    before = pltpu.roll(x, 1, axis)
    return jnp.where(lane % 2 == 0, -after, before)


def gram_rows(slabs, full_ref):
    width = full_ref.shape[0]
    full_ref[...] = sum(
        lax.dot_general(x, x, (((1,), (1,)), ((), ())), preferred_element_type=jnp.float32)
        for x in slabs
    )
    even = full_ref[pl.ds(0, width // 2, stride=2), :]
    odd = full_ref[pl.ds(1, width // 2, stride=2), :]
    lane = lax.broadcasted_iota(jnp.int32, odd.shape, 1)
    return even - rotated(odd, lane)


def gram_kernel(x_ref, out_ref, full_ref):
    out_ref[...] = gram_rows([x_ref[...]], full_ref)


def complex_gram(x):
    width = x.shape[0]
    return pl.pallas_call(
        gram_kernel,
        out_shape=jax.ShapeDtypeStruct((width // 2, width), jnp.float32),
        in_specs=[pl.BlockSpec(memory_space=pltpu.VMEM)],
        out_specs=pl.BlockSpec(memory_space=pltpu.VMEM),
        scratch_shapes=[pltpu.VMEM((width, width), jnp.float32)],
        compiler_params=pltpu.CompilerParams(vmem_limit_bytes=4 * 2**20),
        name="gram",
    )(x)


def eliminate(rows, panel):
    count = len(rows)
    shape = rows[0].shape
    sub = lax.broadcasted_iota(jnp.int32, shape, 0)
    lane = lax.broadcasted_iota(jnp.int32, shape, 1)

    def over_lanes(x, at):
        return jnp.broadcast_to(x[:, at:at + 1], shape)

    def over_rows(x, at):
        return jnp.broadcast_to(x[at:at + 1, :], shape)

    rows = list(rows)
    pivots = [jnp.ones(shape, jnp.float32) for _ in range(count)]
    for first in range(0, count * SUB, panel):
        own = first // SUB
        live = range(own, count)
        re = [{i: over_lanes(rows[i], 2 * (first + c)) for i in live} for c in range(panel)]
        im = [{i: over_lanes(rows[i], 2 * (first + c) + 1) for i in live} for c in range(panel)]
        head, turned = rows[own], rotated(rows[own], lane)
        for c in range(panel):
            at = (first + c) % SUB
            k = first + c
            pivot = over_rows(re[c][own], at)
            pivots[own] = jnp.where(sub == at, pivot, pivots[own])
            inverse = 1.0 / pivot
            upper = {
                later: (over_rows(re[later][own], at), over_rows(im[later][own], at))
                for later in range(c + 1, panel)
            }
            for i in live:
                re[c][i] = re[c][i] * inverse
                im[c][i] = im[c][i] * inverse
                for later, (u_re, u_im) in upper.items():
                    re[later][i] = re[later][i] - (re[c][i] * u_re - im[c][i] * u_im)
                    im[later][i] = im[later][i] - (re[c][i] * u_im + im[c][i] * u_re)
            below = sub > at
            m_re = jnp.where(below, re[c][own], 0.0)
            m_im = jnp.where(below, im[c][own], 0.0)
            on_re, on_im = lane == 2 * k, lane == 2 * k + 1
            p = jnp.where(on_re, 1.0, jnp.where(on_im, 0.0, over_rows(head, at)))
            q = jnp.where(on_im, 1.0, jnp.where(on_re, 0.0, over_rows(turned, at)))
            cleared = below & (on_re | on_im)
            head = jnp.where(cleared, 0.0, head) - (m_re * p + m_im * q)
            turned = jnp.where(cleared, 0.0, turned) - (m_re * q - m_im * p)
        rows[own] = head
        if own + 1 == count:
            continue
        inside = (lane >= 2 * first) & (lane < 2 * (first + panel))
        rest = {i: jnp.where(inside, 0.0, rows[i]) for i in range(own + 1, count)}
        for c in range(panel):
            at = (first + c) % SUB
            k = first + c
            on_re, on_im = lane == 2 * k, lane == 2 * k + 1
            drop = (lane >= 2 * k) & (lane < 2 * (first + panel))
            p = jnp.where(on_re, 1.0, jnp.where(drop, 0.0, over_rows(head, at)))
            q = jnp.where(on_im, 1.0, jnp.where(drop, 0.0, over_rows(turned, at)))
            for i in rest:
                rest[i] = rest[i] - (re[c][i] * p + im[c][i] * q)
        for i in rest:
            rows[i] = rest[i]
    return rows, pivots


def modes_kernel(scale, slabs, x_ref, *refs):
    *given, modes_ref, factor_ref, basis_ref, upper_ref = refs
    width = basis_ref.shape[0]
    size = width // 2
    count = size // SUB
    if given:
        gram = given[0][...]
        mine = x_ref[...]
    else:
        gram = gram_rows([x_ref[i * width:(i + 1) * width] for i in range(slabs)], basis_ref)
        own = lax.axis_index("space")
        mine = x_ref[pl.ds(pl.multiple_of(own * width, width), width)]
    gram = gram * scale
    rows, pivots = eliminate([gram[i * SUB:(i + 1) * SUB] for i in range(count)], PANEL)
    shape = rows[0].shape
    sub = lax.broadcasted_iota(jnp.int32, shape, 0)
    lane = lax.broadcasted_iota(jnp.int32, shape, 1)
    for i in range(count):
        root = lax.rsqrt(pivots[i])
        diagonal = 2 * (i * SUB + sub)
        right = jnp.where(lane > diagonal + 1, rows[i], jnp.where(lane == diagonal, pivots[i], 0.0))
        left = jnp.where(lane < diagonal, rows[i], jnp.where(lane == diagonal, 1.0, 0.0))
        upper_ref[i * SUB:(i + 1) * SUB, :] = right * root
        left = left * root
        basis_ref[pl.ds(2 * i * SUB, SUB, stride=2), :] = left
        basis_ref[pl.ds(2 * i * SUB + 1, SUB, stride=2), :] = rotated(left, lane)
    points = jnp.transpose(mine)
    basis = basis_ref[...]
    high = basis.astype(jnp.bfloat16)
    low = (basis - high.astype(jnp.float32)).astype(jnp.bfloat16)
    contract = (((1,), (1,)), ((), ()))
    modes_ref[...] = lax.dot_general(
        points, high, contract, preferred_element_type=jnp.float32
    ) + lax.dot_general(points, low, contract, preferred_element_type=jnp.float32)
    lane_in = lax.broadcasted_iota(jnp.int32, (2 * size, size), 0)
    lane_out = lax.broadcasted_iota(jnp.int32, (2 * size, size), 1)
    for part in range(2):
        pick = (lane_in == 2 * lane_out + part).astype(jnp.float32)
        factor_ref[part] = jnp.dot(
            upper_ref[...], pick,
            precision=lax.Precision.HIGHEST, preferred_element_type=jnp.float32,
        )


def modes_and_factor(x, grams, width, slabs, scale):
    points = x.shape[1]
    size = width // 2
    return pl.pallas_call(
        functools.partial(modes_kernel, scale, slabs),
        out_shape=(
            jax.ShapeDtypeStruct((points, width), jnp.float32),
            jax.ShapeDtypeStruct((2, size, size), jnp.float32),
        ),
        in_specs=[pl.BlockSpec(memory_space=pltpu.VMEM)] * (1 + len(grams)),
        out_specs=(pl.BlockSpec(memory_space=pltpu.VMEM),) * 2,
        scratch_shapes=[
            pltpu.VMEM((width, width), jnp.float32),
            pltpu.VMEM((size, width), jnp.float32),
        ],
        compiler_params=pltpu.CompilerParams(vmem_limit_bytes=8 * 2**20),
        name="factor_and_modes",
    )(x, *grams)


def local(slabs, snapshots, row_scales, block_offsets, freq_index):
    freqs = freq_index.shape[0]
    points = snapshots.shape[1]
    width = 2 * block_offsets.shape[0] * lax.axis_size("blk")
    copies = slabs if slabs <= FEW_SLABS else 1
    spectra = block_spectra(copies, snapshots, row_scales, block_offsets, freq_index)
    chunks = spectra.reshape(copies * freqs, -1, points)
    swap = functools.partial(lax.all_to_all, split_axis=0, concat_axis=0, tiled=True)
    if copies == slabs:
        x = swap(chunks, ("space", "blk")).reshape(-1, points)
        grams = []
    else:
        x = swap(chunks, "blk").reshape(-1, points)
        grams = [lax.psum(complex_gram(x), "space")]
    modes, factor = modes_and_factor(x, grams, width, slabs, 1.0 / (points * slabs))
    return modes[None], factor[None]


def solution(mesh):
    return jax.shard_map(
        functools.partial(local, mesh.shape["space"]),
        mesh=mesh,
        in_specs=(P("blk", "space"), P("blk"), P("blk"), P()),
        out_specs=(P("blk", "space", None), P("blk", None, None, None)),
        check_vma=False,
    )
```

```python
import functools
import math

import jax
import jax.numpy as jnp
from jax import lax
from jax.experimental import pallas as pl
from jax.experimental.pallas import tpu as pltpu
from jax.sharding import PartitionSpec as P

NFFT = 512
PANEL = 4
SUB = 8
PIECE = 256
FEW_SLABS = 2
SIN_COEFS = (
    0.9999999765895043,
    -0.1666664763439475,
    0.008332899819203531,
    -0.0001980089750772882,
    2.5904879854375602e-06,
)


def cos_of_phase(phase):
    folded = jnp.abs((phase & (NFFT - 1)) - NFFT // 2) - NFFT // 4
    x = folded.astype(jnp.float32) * (2.0 * math.pi / NFFT)
    square = x * x
    total = jnp.full_like(x, SIN_COEFS[-1])
    for coef in SIN_COEFS[-2::-1]:
        total = total * square + coef
    return total * x


def spectra_kernel(
    snap_hbm, scales_hbm, offsets_hbm, freq_hbm, out_ref,
    snap_ref, scales_ref, offsets_ref, freq_ref, coef_ref, small_sems, snap_sems,
):
    snaps = snap_ref.shape[0]
    blocks = offsets_ref.shape[0]
    rows = 2 * blocks
    freqs = freq_ref.shape[0]
    small = [
        pltpu.make_async_copy(src, dst, small_sems.at[i])
        for i, (src, dst) in enumerate(
            ((offsets_hbm, offsets_ref), (freq_hbm, freq_ref), (scales_hbm, scales_ref))
        )
    ]
    pieces = [slice(at, min(at + PIECE, snaps)) for at in range(0, snaps, PIECE)]
    large = [
        pltpu.make_async_copy(snap_hbm.at[piece], snap_ref.at[piece], snap_sems.at[i])
        for i, piece in enumerate(pieces)
    ]
    for copy in small + large:
        copy.start()
    row = lax.broadcasted_iota(jnp.int32, (rows, snaps), 0)
    time = lax.broadcasted_iota(jnp.int32, (rows, snaps), 1)
    for copy in small:
        copy.wait()
    start = jnp.zeros((rows, snaps), jnp.int32)
    for b in range(blocks):
        start = jnp.where(row // 2 == b, offsets_ref[b], start)
    shifted = time - start
    hann = 0.5 - 0.5 * cos_of_phase(shifted)
    inside = (shifted >= 0) & (shifted < NFFT)
    scales = jnp.broadcast_to(scales_ref[...].reshape(1, snaps), (rows, snaps))
    weight = jnp.where(inside, hann * scales * (1.0 / math.sqrt(NFFT)), 0.0)
    base = shifted[:, :NFFT].astype(jnp.float32)
    quarter = (row[:, :NFFT] % 2) * (NFFT // 4)
    repeats = -(-snaps // NFFT)

    def rows_of(f):
        freq = freq_ref[f].astype(jnp.float32)
        table = cos_of_phase((base * freq).astype(jnp.int32) + quarter)
        return jnp.concatenate([table] * repeats, 1)[:, :snaps] * weight

    for f in range(0, freqs, 2):
        pair = jnp.concatenate([rows_of(f), rows_of(f + 1)], 0)
        coef_ref[f * rows:(f + 2) * rows, :] = pair.astype(jnp.bfloat16)
    total = jnp.zeros(out_ref.shape[1:], jnp.float32)
    for copy, piece in zip(large, pieces):
        copy.wait()
        total += jnp.dot(
            coef_ref[:, piece], snap_ref[piece], preferred_element_type=jnp.float32
        )
    result = total.astype(jnp.bfloat16)
    for copy in range(out_ref.shape[0]):
        out_ref[copy] = result


def block_spectra(copies, snapshots, row_scales, block_offsets, freq_index):
    snaps, points = snapshots.shape
    rows = 2 * block_offsets.shape[0] * freq_index.shape[0]
    pieces = -(-snaps // PIECE)
    return pl.pallas_call(
        spectra_kernel,
        out_shape=jax.ShapeDtypeStruct((copies, rows, points), jnp.bfloat16),
        in_specs=[pl.BlockSpec(memory_space=pltpu.HBM)] * 4,
        out_specs=pl.BlockSpec(memory_space=pltpu.VMEM),
        scratch_shapes=[
            pltpu.VMEM((snaps, points), jnp.bfloat16),
            pltpu.VMEM((snaps,), jnp.float32),
            pltpu.SMEM(block_offsets.shape, jnp.int32),
            pltpu.SMEM(freq_index.shape, jnp.int32),
            pltpu.VMEM((rows, snaps), jnp.bfloat16),
            pltpu.SemaphoreType.DMA((3,)),
            pltpu.SemaphoreType.DMA((pieces,)),
        ],
        compiler_params=pltpu.CompilerParams(vmem_limit_bytes=60 * 2**20),
        name="spectra",
    )(snapshots, row_scales, block_offsets, freq_index)


def rotated(x, lane):
    axis = x.ndim - 1
    width = x.shape[axis]
    after = pltpu.roll(x, width - 1, axis)
    before = pltpu.roll(x, 1, axis)
    return jnp.where(lane % 2 == 0, -after, before)


def gram_rows(slabs, full_ref):
    width = full_ref.shape[0]
    full_ref[...] = sum(
        lax.dot_general(x, x, (((1,), (1,)), ((), ())), preferred_element_type=jnp.float32)
        for x in slabs
    )
    even = full_ref[pl.ds(0, width // 2, stride=2), :]
    odd = full_ref[pl.ds(1, width // 2, stride=2), :]
    lane = lax.broadcasted_iota(jnp.int32, odd.shape, 1)
    return even - rotated(odd, lane)


def gram_kernel(x_ref, out_ref, full_ref):
    out_ref[...] = gram_rows([x_ref[...]], full_ref)


def complex_gram(x):
    width = x.shape[0]
    return pl.pallas_call(
        gram_kernel,
        out_shape=jax.ShapeDtypeStruct((width // 2, width), jnp.float32),
        in_specs=[pl.BlockSpec(memory_space=pltpu.VMEM)],
        out_specs=pl.BlockSpec(memory_space=pltpu.VMEM),
        scratch_shapes=[pltpu.VMEM((width, width), jnp.float32)],
        compiler_params=pltpu.CompilerParams(vmem_limit_bytes=4 * 2**20),
        name="gram",
    )(x)


def eliminate(rows, panel):
    count = len(rows)
    shape = rows[0].shape
    sub = lax.broadcasted_iota(jnp.int32, shape, 0)
    lane = lax.broadcasted_iota(jnp.int32, shape, 1)

    def over_lanes(x, at):
        return jnp.broadcast_to(x[:, at:at + 1], shape)

    def over_rows(x, at):
        return jnp.broadcast_to(x[at:at + 1, :], shape)

    rows = list(rows)
    pivots = [jnp.ones(shape, jnp.float32) for _ in range(count)]
    for first in range(0, count * SUB, panel):
        own = first // SUB
        live = range(own, count)
        re = [{i: over_lanes(rows[i], 2 * (first + c)) for i in live} for c in range(panel)]
        im = [{i: over_lanes(rows[i], 2 * (first + c) + 1) for i in live} for c in range(panel)]
        head, turned = rows[own], rotated(rows[own], lane)
        for c in range(panel):
            at = (first + c) % SUB
            k = first + c
            pivot = over_rows(re[c][own], at)
            pivots[own] = jnp.where(sub == at, pivot, pivots[own])
            inverse = pl.reciprocal(pivot, approx=True)
            upper = {
                later: (over_rows(re[later][own], at), over_rows(im[later][own], at))
                for later in range(c + 1, panel)
            }
            for i in live:
                re[c][i] = re[c][i] * inverse
                im[c][i] = im[c][i] * inverse
                for later, (u_re, u_im) in upper.items():
                    re[later][i] = re[later][i] - (re[c][i] * u_re - im[c][i] * u_im)
                    im[later][i] = im[later][i] - (re[c][i] * u_im + im[c][i] * u_re)
            below = sub > at
            m_re = jnp.where(below, re[c][own], 0.0)
            m_im = jnp.where(below, im[c][own], 0.0)
            on_re, on_im = lane == 2 * k, lane == 2 * k + 1
            p = jnp.where(on_re, 1.0, jnp.where(on_im, 0.0, over_rows(head, at)))
            q = jnp.where(on_im, 1.0, jnp.where(on_re, 0.0, over_rows(turned, at)))
            cleared = below & (on_re | on_im)
            head = jnp.where(cleared, 0.0, head) - (m_re * p + m_im * q)
            turned = jnp.where(cleared, 0.0, turned) - (m_re * q - m_im * p)
        rows[own] = head
        if own + 1 == count:
            continue
        inside = (lane >= 2 * first) & (lane < 2 * (first + panel))
        rest = {i: jnp.where(inside, 0.0, rows[i]) for i in range(own + 1, count)}
        for c in range(panel):
            at = (first + c) % SUB
            k = first + c
            on_re, on_im = lane == 2 * k, lane == 2 * k + 1
            drop = (lane >= 2 * k) & (lane < 2 * (first + panel))
            p = jnp.where(on_re, 1.0, jnp.where(drop, 0.0, over_rows(head, at)))
            q = jnp.where(on_im, 1.0, jnp.where(drop, 0.0, over_rows(turned, at)))
            for i in rest:
                rest[i] = rest[i] - (re[c][i] * p + im[c][i] * q)
        for i in rest:
            rows[i] = rest[i]
    return rows, pivots


def modes_kernel(scale, slabs, x_ref, *refs):
    *given, modes_ref, factor_ref, basis_ref, points_ref = refs
    width = basis_ref.shape[0]
    size = width // 2
    count = size // SUB
    if given:
        gram = given[0][...]
        mine = x_ref[...]
    else:
        gram = gram_rows([x_ref[i * width:(i + 1) * width] for i in range(slabs)], basis_ref)
        own = lax.axis_index("space")
        mine = x_ref[pl.ds(pl.multiple_of(own * width, width), width)]
    points = jnp.transpose(mine)
    points_ref[...] = jnp.concatenate([points, points], 1)
    gram = gram * scale
    rows, pivots = eliminate([gram[i * SUB:(i + 1) * SUB] for i in range(count)], PANEL)
    shape = rows[0].shape
    sub = lax.broadcasted_iota(jnp.int32, shape, 0)
    lane = lax.broadcasted_iota(jnp.int32, shape, 1)
    pick = jnp.where(lane < size, 2 * lane, 2 * (lane - size) + 1)
    for i in range(count):
        own_rows = slice(i * SUB, (i + 1) * SUB)
        root = lax.rsqrt(pivots[i])
        diagonal = 2 * (i * SUB + sub)
        left = jnp.where(lane < diagonal, rows[i], jnp.where(lane == diagonal, 1.0, 0.0)) * root
        basis_ref[pl.ds(2 * i * SUB, SUB, stride=2), :] = left
        basis_ref[pl.ds(2 * i * SUB + 1, SUB, stride=2), :] = rotated(left, lane)
        right = jnp.where(lane > diagonal + 1, rows[i], jnp.where(lane == diagonal, pivots[i], 0.0))
        parts = jnp.take_along_axis(right * root, pick, axis=1)
        factor_ref[0, own_rows, :] = parts[:, :size]
        factor_ref[1, own_rows, :] = parts[:, size:]
    basis = basis_ref[...]
    high = basis.astype(jnp.bfloat16)
    low = (basis - high.astype(jnp.float32)).astype(jnp.bfloat16)
    modes_ref[...] = lax.dot_general(
        points_ref[...], jnp.concatenate([high, low], 1), (((1,), (1,)), ((), ())),
        preferred_element_type=jnp.float32,
    )


def modes_and_factor(x, grams, width, slabs, scale):
    points = x.shape[1]
    size = width // 2
    return pl.pallas_call(
        functools.partial(modes_kernel, scale, slabs),
        out_shape=(
            jax.ShapeDtypeStruct((points, width), jnp.float32),
            jax.ShapeDtypeStruct((2, size, size), jnp.float32),
        ),
        in_specs=[pl.BlockSpec(memory_space=pltpu.VMEM)] * (1 + len(grams)),
        out_specs=(pl.BlockSpec(memory_space=pltpu.VMEM),) * 2,
        scratch_shapes=[
            pltpu.VMEM((width, width), jnp.float32),
            pltpu.VMEM((points, 2 * width), jnp.bfloat16),
        ],
        compiler_params=pltpu.CompilerParams(vmem_limit_bytes=8 * 2**20),
        name="factor_and_modes",
    )(x, *grams)


def local(slabs, snapshots, row_scales, block_offsets, freq_index):
    freqs = freq_index.shape[0]
    points = snapshots.shape[1]
    width = 2 * block_offsets.shape[0] * lax.axis_size("blk")
    copies = slabs if slabs <= FEW_SLABS else 1
    spectra = block_spectra(copies, snapshots, row_scales, block_offsets, freq_index)
    chunks = spectra.reshape(copies * freqs, -1, points)
    swap = functools.partial(lax.all_to_all, split_axis=0, concat_axis=0, tiled=True)
    if copies == slabs:
        x = swap(chunks, ("space", "blk")).reshape(-1, points)
        grams = []
    else:
        x = swap(chunks, "blk").reshape(-1, points)
        grams = [lax.psum(complex_gram(x), "space")]
    modes, factor = modes_and_factor(x, grams, width, slabs, 1.0 / (points * slabs))
    return modes[None], factor[None]


def solution(mesh):
    return jax.shard_map(
        functools.partial(local, mesh.shape["space"]),
        mesh=mesh,
        in_specs=(P("blk", "space"), P("blk"), P("blk"), P()),
        out_specs=(P("blk", "space", None), P("blk", None, None, None)),
        check_vma=False,
    )
```

```python
import functools
import math

import jax
import jax.numpy as jnp
from jax import lax
from jax.experimental import pallas as pl
from jax.experimental.pallas import tpu as pltpu
from jax.sharding import PartitionSpec as P

NFFT = 512
PANEL = 8
SUB = 8
PIECE = 256
FEW_SLABS = 2
SIN_COEFS = (
    0.9999999765895043,
    -0.1666664763439475,
    0.008332899819203531,
    -0.0001980089750772882,
    2.5904879854375602e-06,
)


def cos_of_phase(phase):
    folded = jnp.abs((phase & (NFFT - 1)) - NFFT // 2) - NFFT // 4
    x = folded.astype(jnp.float32) * (2.0 * math.pi / NFFT)
    square = x * x
    total = jnp.full_like(x, SIN_COEFS[-1])
    for coef in SIN_COEFS[-2::-1]:
        total = total * square + coef
    return total * x


def spectra_kernel(
    snap_hbm, scales_hbm, offsets_hbm, freq_hbm, out_ref,
    snap_ref, scales_ref, offsets_ref, freq_ref, coef_ref, small_sems, snap_sems,
):
    snaps = snap_ref.shape[0]
    blocks = offsets_ref.shape[0]
    rows = 2 * blocks
    freqs = freq_ref.shape[0]
    small = [
        pltpu.make_async_copy(src, dst, small_sems.at[i])
        for i, (src, dst) in enumerate(
            ((offsets_hbm, offsets_ref), (freq_hbm, freq_ref), (scales_hbm, scales_ref))
        )
    ]
    pieces = [slice(at, min(at + PIECE, snaps)) for at in range(0, snaps, PIECE)]
    large = [
        pltpu.make_async_copy(snap_hbm.at[piece], snap_ref.at[piece], snap_sems.at[i])
        for i, piece in enumerate(pieces)
    ]
    for copy in small + large:
        copy.start()
    row = lax.broadcasted_iota(jnp.int32, (rows, snaps), 0)
    time = lax.broadcasted_iota(jnp.int32, (rows, snaps), 1)
    for copy in small:
        copy.wait()
    start = jnp.zeros((rows, snaps), jnp.int32)
    for b in range(blocks):
        start = jnp.where(row // 2 == b, offsets_ref[b], start)
    shifted = time - start
    hann = 0.5 - 0.5 * cos_of_phase(shifted)
    inside = (shifted >= 0) & (shifted < NFFT)
    scales = jnp.broadcast_to(scales_ref[...].reshape(1, snaps), (rows, snaps))
    weight = jnp.where(inside, hann * scales * (1.0 / math.sqrt(NFFT)), 0.0)
    base = shifted[:, :NFFT].astype(jnp.float32)
    quarter = (row[:, :NFFT] % 2) * (NFFT // 4)
    repeats = -(-snaps // NFFT)

    def rows_of(f):
        freq = freq_ref[f].astype(jnp.float32)
        table = cos_of_phase((base * freq).astype(jnp.int32) + quarter)
        return jnp.concatenate([table] * repeats, 1)[:, :snaps] * weight

    for f in range(0, freqs, 2):
        pair = jnp.concatenate([rows_of(f), rows_of(f + 1)], 0)
        coef_ref[f * rows:(f + 2) * rows, :] = pair.astype(jnp.bfloat16)
    total = jnp.zeros(out_ref.shape[1:], jnp.float32)
    for copy, piece in zip(large, pieces):
        copy.wait()
        total += jnp.dot(
            coef_ref[:, piece], snap_ref[piece], preferred_element_type=jnp.float32
        )
    result = total.astype(jnp.bfloat16)
    for copy in range(out_ref.shape[0]):
        out_ref[copy] = result


def block_spectra(copies, snapshots, row_scales, block_offsets, freq_index):
    snaps, points = snapshots.shape
    rows = 2 * block_offsets.shape[0] * freq_index.shape[0]
    pieces = -(-snaps // PIECE)
    return pl.pallas_call(
        spectra_kernel,
        out_shape=jax.ShapeDtypeStruct((copies, rows, points), jnp.bfloat16),
        in_specs=[pl.BlockSpec(memory_space=pltpu.HBM)] * 4,
        out_specs=pl.BlockSpec(memory_space=pltpu.VMEM),
        scratch_shapes=[
            pltpu.VMEM((snaps, points), jnp.bfloat16),
            pltpu.VMEM((snaps,), jnp.float32),
            pltpu.SMEM(block_offsets.shape, jnp.int32),
            pltpu.SMEM(freq_index.shape, jnp.int32),
            pltpu.VMEM((rows, snaps), jnp.bfloat16),
            pltpu.SemaphoreType.DMA((3,)),
            pltpu.SemaphoreType.DMA((pieces,)),
        ],
        compiler_params=pltpu.CompilerParams(vmem_limit_bytes=60 * 2**20),
        name="spectra",
    )(snapshots, row_scales, block_offsets, freq_index)


def rotated(x, lane):
    axis = x.ndim - 1
    width = x.shape[axis]
    after = pltpu.roll(x, width - 1, axis)
    before = pltpu.roll(x, 1, axis)
    return jnp.where(lane % 2 == 0, -after, before)


def gram_rows(slabs, full_ref):
    width = full_ref.shape[0]
    full_ref[...] = sum(
        lax.dot_general(x, x, (((1,), (1,)), ((), ())), preferred_element_type=jnp.float32)
        for x in slabs
    )
    even = full_ref[pl.ds(0, width // 2, stride=2), :]
    odd = full_ref[pl.ds(1, width // 2, stride=2), :]
    lane = lax.broadcasted_iota(jnp.int32, odd.shape, 1)
    return even - rotated(odd, lane)


def gram_kernel(x_ref, out_ref, full_ref):
    out_ref[...] = gram_rows([x_ref[...]], full_ref)


def complex_gram(x):
    width = x.shape[0]
    return pl.pallas_call(
        gram_kernel,
        out_shape=jax.ShapeDtypeStruct((width // 2, width), jnp.float32),
        in_specs=[pl.BlockSpec(memory_space=pltpu.VMEM)],
        out_specs=pl.BlockSpec(memory_space=pltpu.VMEM),
        scratch_shapes=[pltpu.VMEM((width, width), jnp.float32)],
        compiler_params=pltpu.CompilerParams(vmem_limit_bytes=4 * 2**20),
        name="gram",
    )(x)


def tree_sum(terms):
    while len(terms) > 1:
        terms = [sum(terms[i:i + 2]) for i in range(0, len(terms), 2)]
    return terms[0]


def eliminate(rows, panel):
    count = len(rows)
    shape = rows[0].shape
    sub = lax.broadcasted_iota(jnp.int32, shape, 0)
    lane = lax.broadcasted_iota(jnp.int32, shape, 1)

    def over_lanes(x, at):
        return jnp.broadcast_to(x[:, at:at + 1], shape)

    def over_rows(x, at):
        return jnp.broadcast_to(x[at:at + 1, :], shape)

    rows = list(rows)
    final = [None] * count
    pivots = [None] * count
    for first in range(0, count * SUB, panel):
        own = first // SUB
        head, turned = rows[own], rotated(rows[own], lane)
        if first % SUB == 0:
            final[own], pivots[own] = head, jnp.ones(shape, jnp.float32)
        columns = [2 * (first + c) for c in range(panel)]
        raw = {
            i: [(over_lanes(rows[i], at), over_lanes(rows[i], at + 1)) for at in columns]
            for i in range(own, count)
        }
        here = raw[own]
        for c in range(panel):
            at = (first + c) % SUB
            here_row = sub == at
            pivot = over_rows(here[c][0], at)
            inverse = pl.reciprocal(pivot, approx=True)
            m_re = jnp.where(here_row, -inverse, here[c][0] * inverse)
            m_im = jnp.where(here_row, 0.0, here[c][1] * inverse)
            if first % SUB:
                m_re = jnp.where(sub < first % SUB, 0.0, m_re)
                m_im = jnp.where(sub < first % SUB, 0.0, m_im)
            final[own] = jnp.where(here_row, head, final[own])
            pivots[own] = jnp.where(here_row, pivot, pivots[own])
            for later in range(c + 1, panel):
                re, im = here[later]
                u_re, u_im = over_rows(re, at), over_rows(im, at)
                here[later] = (
                    jnp.where(here_row, 0.0, re) - (m_re * u_re - m_im * u_im),
                    jnp.where(here_row, 0.0, im) - (m_re * u_im + m_im * u_re),
                )
            on_re, on_im = lane == columns[c], lane == columns[c] + 1
            p = jnp.where(on_re, 1.0, jnp.where(on_im, 0.0, over_rows(head, at)))
            q = jnp.where(on_im, 1.0, jnp.where(on_re, 0.0, over_rows(turned, at)))
            cleared = here_row | ((on_re | on_im) & (sub >= first % SUB))
            head = jnp.where(cleared, 0.0, head) - (m_re * p + m_im * q)
            turned = jnp.where(cleared, 0.0, turned) - (m_re * q - m_im * p)
        rows[own] = head
        inside = (lane >= columns[0]) & (lane < columns[0] + 2 * panel)
        solved = [
            (over_rows(head, (first + c) % SUB), over_rows(turned, (first + c) % SUB))
            for c in range(panel)
        ]
        for i in range(own + 1, count):
            rows[i] = jnp.where(inside, 0.0, rows[i]) - tree_sum(
                [re * p + im * q for (re, im), (p, q) in zip(raw[i], solved)]
            )
    return final, pivots


def modes_kernel(scale, slabs, x_ref, *refs):
    *given, modes_ref, factor_ref, basis_ref, points_ref = refs
    width = basis_ref.shape[0]
    size = width // 2
    count = size // SUB
    if given:
        gram = given[0][...]
        mine = x_ref[...]
    else:
        gram = gram_rows([x_ref[i * width:(i + 1) * width] for i in range(slabs)], basis_ref)
        own = lax.axis_index("space")
        mine = x_ref[pl.ds(pl.multiple_of(own * width, width), width)]
    points = jnp.transpose(mine)
    points_ref[...] = jnp.concatenate([points, points], 1)
    gram = gram * scale
    rows, pivots = eliminate([gram[i * SUB:(i + 1) * SUB] for i in range(count)], PANEL)
    shape = rows[0].shape
    sub = lax.broadcasted_iota(jnp.int32, shape, 0)
    lane = lax.broadcasted_iota(jnp.int32, shape, 1)
    pick = jnp.where(lane < size, 2 * lane, 2 * (lane - size) + 1)
    for i in range(count):
        own_rows = slice(i * SUB, (i + 1) * SUB)
        root = lax.rsqrt(pivots[i])
        diagonal = 2 * (i * SUB + sub)
        left = jnp.where(lane < diagonal, rows[i], jnp.where(lane == diagonal, 1.0, 0.0)) * root
        basis_ref[pl.ds(2 * i * SUB, SUB, stride=2), :] = left
        basis_ref[pl.ds(2 * i * SUB + 1, SUB, stride=2), :] = rotated(left, lane)
        right = jnp.where(lane > diagonal + 1, rows[i], jnp.where(lane == diagonal, pivots[i], 0.0))
        parts = jnp.take_along_axis(right * root, pick, axis=1)
        factor_ref[0, own_rows, :] = parts[:, :size]
        factor_ref[1, own_rows, :] = parts[:, size:]
    basis = basis_ref[...]
    high = basis.astype(jnp.bfloat16)
    low = (basis - high.astype(jnp.float32)).astype(jnp.bfloat16)
    modes_ref[...] = lax.dot_general(
        points_ref[...], jnp.concatenate([high, low], 1), (((1,), (1,)), ((), ())),
        preferred_element_type=jnp.float32,
    )


def modes_and_factor(x, grams, width, slabs, scale):
    points = x.shape[1]
    size = width // 2
    return pl.pallas_call(
        functools.partial(modes_kernel, scale, slabs),
        out_shape=(
            jax.ShapeDtypeStruct((points, width), jnp.float32),
            jax.ShapeDtypeStruct((2, size, size), jnp.float32),
        ),
        in_specs=[pl.BlockSpec(memory_space=pltpu.VMEM)] * (1 + len(grams)),
        out_specs=(pl.BlockSpec(memory_space=pltpu.VMEM),) * 2,
        scratch_shapes=[
            pltpu.VMEM((width, width), jnp.float32),
            pltpu.VMEM((points, 2 * width), jnp.bfloat16),
        ],
        compiler_params=pltpu.CompilerParams(vmem_limit_bytes=8 * 2**20),
        name="factor_and_modes",
    )(x, *grams)


def local(slabs, snapshots, row_scales, block_offsets, freq_index):
    freqs = freq_index.shape[0]
    points = snapshots.shape[1]
    width = 2 * block_offsets.shape[0] * lax.axis_size("blk")
    copies = slabs if slabs <= FEW_SLABS else 1
    spectra = block_spectra(copies, snapshots, row_scales, block_offsets, freq_index)
    chunks = spectra.reshape(copies * freqs, -1, points)
    swap = functools.partial(lax.all_to_all, split_axis=0, concat_axis=0, tiled=True)
    if copies == slabs:
        x = swap(chunks, ("space", "blk")).reshape(-1, points)
        grams = []
    else:
        x = swap(chunks, "blk").reshape(-1, points)
        grams = [lax.psum(complex_gram(x), "space")]
    modes, factor = modes_and_factor(x, grams, width, slabs, 1.0 / (points * slabs))
    return modes[None], factor[None]


def solution(mesh):
    return jax.shard_map(
        functools.partial(local, mesh.shape["space"]),
        mesh=mesh,
        in_specs=(P("blk", "space"), P("blk"), P("blk"), P()),
        out_specs=(P("blk", "space", None), P("blk", None, None, None)),
        check_vma=False,
    )
```

```python
import functools
import math

import jax
import jax.numpy as jnp
from jax import lax
from jax.experimental import pallas as pl
from jax.experimental.pallas import tpu as pltpu
from jax.sharding import PartitionSpec as P

NFFT = 512
PANEL = 8
SUB = 8
PIECE = 256
INNER = 4
SIN_COEFS = (
    0.9999999765895043,
    -0.1666664763439475,
    0.008332899819203531,
    -0.0001980089750772882,
    2.5904879854375602e-06,
)


def cos_of_phase(phase):
    folded = jnp.abs((phase & (NFFT - 1)) - NFFT // 2) - NFFT // 4
    x = folded.astype(jnp.float32) * (2.0 * math.pi / NFFT)
    square = x * x
    total = jnp.full_like(x, SIN_COEFS[-1])
    for coef in SIN_COEFS[-2::-1]:
        total = total * square + coef
    return total * x


def spectra_kernel(inner, snap_hbm, scales_hbm, offsets_hbm, freq_hbm, *refs):
    *out_refs, snap_ref, scales_ref, offsets_ref, freq_ref, coef_ref, small_sems, snap_sems = refs
    snaps = snap_ref.shape[0]
    blocks = offsets_ref.shape[0]
    rows = 2 * blocks
    freqs = freq_ref.shape[0]
    small = [
        pltpu.make_async_copy(src, dst, small_sems.at[i])
        for i, (src, dst) in enumerate(
            ((offsets_hbm, offsets_ref), (freq_hbm, freq_ref), (scales_hbm, scales_ref))
        )
    ]
    pieces = [slice(at, min(at + PIECE, snaps)) for at in range(0, snaps, PIECE)]
    large = [
        pltpu.make_async_copy(snap_hbm.at[piece], snap_ref.at[piece], snap_sems.at[i])
        for i, piece in enumerate(pieces)
    ]
    for copy in small + large:
        copy.start()
    row = lax.broadcasted_iota(jnp.int32, (rows, snaps), 0)
    time = lax.broadcasted_iota(jnp.int32, (rows, snaps), 1)
    for copy in small:
        copy.wait()
    start = jnp.zeros((rows, snaps), jnp.int32)
    for b in range(blocks):
        start = jnp.where(row // 2 == b, offsets_ref[b], start)
    shifted = time - start
    hann = 0.5 - 0.5 * cos_of_phase(shifted)
    inside = (shifted >= 0) & (shifted < NFFT)
    scales = jnp.broadcast_to(scales_ref[...].reshape(1, snaps), (rows, snaps))
    weight = jnp.where(inside, hann * scales * (1.0 / math.sqrt(NFFT)), 0.0)
    base = shifted[:, :NFFT].astype(jnp.float32)
    quarter = (row[:, :NFFT] % 2) * (NFFT // 4)
    repeats = -(-snaps // NFFT)

    def rows_of(g):
        f = g
        if len(out_refs) > 1:
            f = ((lax.axis_index("blk") // inner) ^ (g // inner)) * inner + g % inner
        freq = freq_ref[f].astype(jnp.float32)
        table = cos_of_phase((base * freq).astype(jnp.int32) + quarter)
        return jnp.concatenate([table] * repeats, 1)[:, :snaps] * weight

    for f in range(0, freqs, 2):
        pair = jnp.concatenate([rows_of(f), rows_of(f + 1)], 0)
        coef_ref[f * rows:(f + 2) * rows, :] = pair.astype(jnp.bfloat16)
    total = jnp.zeros(coef_ref.shape[:1] + snap_ref.shape[1:], jnp.float32)
    for copy, piece in zip(large, pieces):
        copy.wait()
        total += jnp.dot(
            coef_ref[:, piece], snap_ref[piece], preferred_element_type=jnp.float32
        )
    result = total.astype(jnp.bfloat16)
    each = result.shape[0] // len(out_refs)
    for i, out_ref in enumerate(out_refs):
        out_ref[...] = result[i * each:(i + 1) * each]


def block_spectra(parts, inner, snapshots, row_scales, block_offsets, freq_index):
    snaps, points = snapshots.shape
    rows = 2 * block_offsets.shape[0] * freq_index.shape[0]
    pieces = -(-snaps // PIECE)
    return pl.pallas_call(
        functools.partial(spectra_kernel, inner),
        out_shape=[jax.ShapeDtypeStruct((rows // parts, points), jnp.bfloat16)] * parts,
        in_specs=[pl.BlockSpec(memory_space=pltpu.HBM)] * 4,
        out_specs=[pl.BlockSpec(memory_space=pltpu.VMEM)] * parts,
        scratch_shapes=[
            pltpu.VMEM((snaps, points), jnp.bfloat16),
            pltpu.VMEM((snaps,), jnp.float32),
            pltpu.SMEM(block_offsets.shape, jnp.int32),
            pltpu.SMEM(freq_index.shape, jnp.int32),
            pltpu.VMEM((rows, snaps), jnp.bfloat16),
            pltpu.SemaphoreType.DMA((3,)),
            pltpu.SemaphoreType.DMA((pieces,)),
        ],
        compiler_params=pltpu.CompilerParams(vmem_limit_bytes=60 * 2**20),
        name="spectra",
    )(snapshots, row_scales, block_offsets, freq_index)


def regroup_kernel(*refs):
    outer = refs[-1].shape[0]
    in_refs, out_refs = refs[:outer], refs[outer:]
    inner = len(out_refs)
    place = lax.axis_index("blk")
    group, member = place // inner, place % inner
    for e, out_ref in enumerate(out_refs):
        for d, in_ref in enumerate(in_refs):
            out_ref[group ^ d] = in_ref[member ^ e]


def regroup(arrays):
    outer, inner = len(arrays), arrays[0].shape[0]
    shape = (outer,) + arrays[0].shape[1:]
    return pl.pallas_call(
        regroup_kernel,
        out_shape=[jax.ShapeDtypeStruct(shape, arrays[0].dtype)] * inner,
        in_specs=[pl.BlockSpec(memory_space=pltpu.VMEM)] * outer,
        out_specs=[pl.BlockSpec(memory_space=pltpu.VMEM)] * inner,
        compiler_params=pltpu.CompilerParams(vmem_limit_bytes=4 * 2**20),
        name="regroup",
    )(*arrays)


def rotated(x, lane):
    axis = x.ndim - 1
    width = x.shape[axis]
    after = pltpu.roll(x, width - 1, axis)
    before = pltpu.roll(x, 1, axis)
    return jnp.where(lane % 2 == 0, -after, before)


def gram_rows(slabs, full_ref):
    width = full_ref.shape[0]
    full_ref[...] = sum(
        lax.dot_general(x, x, (((1,), (1,)), ((), ())), preferred_element_type=jnp.float32)
        for x in slabs
    )
    even = full_ref[pl.ds(0, width // 2, stride=2), :]
    odd = full_ref[pl.ds(1, width // 2, stride=2), :]
    lane = lax.broadcasted_iota(jnp.int32, odd.shape, 1)
    return even - rotated(odd, lane)


def gram_kernel(x_ref, out_ref, full_ref):
    out_ref[...] = gram_rows([x_ref[...]], full_ref)


def complex_gram(x):
    width = x.shape[0]
    return pl.pallas_call(
        gram_kernel,
        out_shape=jax.ShapeDtypeStruct((width // 2, width), jnp.float32),
        in_specs=[pl.BlockSpec(memory_space=pltpu.VMEM)],
        out_specs=pl.BlockSpec(memory_space=pltpu.VMEM),
        scratch_shapes=[pltpu.VMEM((width, width), jnp.float32)],
        compiler_params=pltpu.CompilerParams(vmem_limit_bytes=4 * 2**20),
        name="gram",
    )(x)


def tree_sum(terms):
    while len(terms) > 1:
        terms = [sum(terms[i:i + 2]) for i in range(0, len(terms), 2)]
    return terms[0]


def eliminate(rows, panel):
    count = len(rows)
    shape = rows[0].shape
    sub = lax.broadcasted_iota(jnp.int32, shape, 0)
    lane = lax.broadcasted_iota(jnp.int32, shape, 1)

    def over_lanes(x, at):
        return jnp.broadcast_to(x[:, at:at + 1], shape)

    def over_rows(x, at):
        return jnp.broadcast_to(x[at:at + 1, :], shape)

    rows = list(rows)
    final = [None] * count
    pivots = [None] * count
    for first in range(0, count * SUB, panel):
        own = first // SUB
        head, turned = rows[own], rotated(rows[own], lane)
        if first % SUB == 0:
            final[own], pivots[own] = head, jnp.ones(shape, jnp.float32)
        columns = [2 * (first + c) for c in range(panel)]
        raw = {
            i: [(over_lanes(rows[i], at), over_lanes(rows[i], at + 1)) for at in columns]
            for i in range(own, count)
        }
        here = raw[own]
        for c in range(panel):
            at = (first + c) % SUB
            here_row = sub == at
            pivot = over_rows(here[c][0], at)
            inverse = pl.reciprocal(pivot, approx=True)
            m_re = jnp.where(here_row, -inverse, here[c][0] * inverse)
            m_im = jnp.where(here_row, 0.0, here[c][1] * inverse)
            if first % SUB:
                m_re = jnp.where(sub < first % SUB, 0.0, m_re)
                m_im = jnp.where(sub < first % SUB, 0.0, m_im)
            final[own] = jnp.where(here_row, head, final[own])
            pivots[own] = jnp.where(here_row, pivot, pivots[own])
            for later in range(c + 1, panel):
                re, im = here[later]
                u_re, u_im = over_rows(re, at), over_rows(im, at)
                here[later] = (
                    jnp.where(here_row, 0.0, re) - (m_re * u_re - m_im * u_im),
                    jnp.where(here_row, 0.0, im) - (m_re * u_im + m_im * u_re),
                )
            on_re, on_im = lane == columns[c], lane == columns[c] + 1
            p = jnp.where(on_re, 1.0, jnp.where(on_im, 0.0, over_rows(head, at)))
            q = jnp.where(on_im, 1.0, jnp.where(on_re, 0.0, over_rows(turned, at)))
            cleared = here_row | ((on_re | on_im) & (sub >= first % SUB))
            head = jnp.where(cleared, 0.0, head) - (m_re * p + m_im * q)
            turned = jnp.where(cleared, 0.0, turned) - (m_re * q - m_im * p)
        rows[own] = head
        inside = (lane >= columns[0]) & (lane < columns[0] + 2 * panel)
        solved = [
            (over_rows(head, (first + c) % SUB), over_rows(turned, (first + c) % SUB))
            for c in range(panel)
        ]
        for i in range(own + 1, count):
            rows[i] = jnp.where(inside, 0.0, rows[i]) - tree_sum(
                [re * p + im * q for (re, im), (p, q) in zip(raw[i], solved)]
            )
    return final, pivots


def gathered(refs, rows_ref):
    inner = len(refs)
    member = lax.axis_index("blk") % inner
    rows = refs[0].shape[1]
    for e, ref in enumerate(refs):
        for group in range(ref.shape[0]):
            at = pl.multiple_of((group * inner + (member ^ e)) * rows, rows)
            rows_ref[pl.ds(at, rows), :] = ref[group].astype(jnp.float32)
    return rows_ref[...].astype(jnp.bfloat16)


def modes_kernel(scale, slabs, *refs):
    *given, modes_ref, factor_ref, basis_ref, points_ref, rows_ref = refs
    width = basis_ref.shape[0]
    size = width // 2
    count = size // SUB
    if slabs:
        each = len(given) // slabs
        all_points = [
            gathered(given[i * each:(i + 1) * each], rows_ref.at[i]) for i in range(slabs)
        ]
        mine = all_points[0]
        gram = gram_rows(all_points, basis_ref)
    else:
        mine = given[0][...]
        gram = given[1][...]
    points = jnp.transpose(mine)
    points_ref[...] = jnp.concatenate([points, points], 1)
    gram = gram * scale
    rows, pivots = eliminate([gram[i * SUB:(i + 1) * SUB] for i in range(count)], PANEL)
    shape = rows[0].shape
    sub = lax.broadcasted_iota(jnp.int32, shape, 0)
    lane = lax.broadcasted_iota(jnp.int32, shape, 1)
    pick = jnp.where(lane < size, 2 * lane, 2 * (lane - size) + 1)
    for i in range(count):
        own_rows = slice(i * SUB, (i + 1) * SUB)
        root = lax.rsqrt(pivots[i])
        diagonal = 2 * (i * SUB + sub)
        left = jnp.where(lane < diagonal, rows[i], jnp.where(lane == diagonal, 1.0, 0.0)) * root
        basis_ref[pl.ds(2 * i * SUB, SUB, stride=2), :] = left
        basis_ref[pl.ds(2 * i * SUB + 1, SUB, stride=2), :] = rotated(left, lane)
        right = jnp.where(lane > diagonal + 1, rows[i], jnp.where(lane == diagonal, pivots[i], 0.0))
        parts = jnp.take_along_axis(right * root, pick, axis=1)
        factor_ref[0, own_rows, :] = parts[:, :size]
        factor_ref[1, own_rows, :] = parts[:, size:]
    basis = basis_ref[...]
    high = basis.astype(jnp.bfloat16)
    low = (basis - high.astype(jnp.float32)).astype(jnp.bfloat16)
    modes_ref[...] = lax.dot_general(
        points_ref[...], jnp.concatenate([high, low], 1), (((1,), (1,)), ((), ())),
        preferred_element_type=jnp.float32,
    )


def modes_and_factor(operands, width, points, slabs, scale):
    size = width // 2
    return pl.pallas_call(
        functools.partial(modes_kernel, scale, slabs),
        out_shape=(
            jax.ShapeDtypeStruct((points, width), jnp.float32),
            jax.ShapeDtypeStruct((2, size, size), jnp.float32),
        ),
        in_specs=[pl.BlockSpec(memory_space=pltpu.VMEM)] * len(operands),
        out_specs=(pl.BlockSpec(memory_space=pltpu.VMEM),) * 2,
        scratch_shapes=[
            pltpu.VMEM((width, width), jnp.float32),
            pltpu.VMEM((points, 2 * width), jnp.bfloat16),
            pltpu.VMEM((max(slabs, 1), width, points), jnp.float32),
        ],
        compiler_params=pltpu.CompilerParams(vmem_limit_bytes=8 * 2**20),
        name="factor_and_modes",
    )(*operands)


def local(slabs, owners, snapshots, row_scales, block_offsets, freq_index):
    freqs = freq_index.shape[0]
    points = snapshots.shape[1]
    rows = 2 * block_offsets.shape[0] * (freqs // owners)
    width = 2 * block_offsets.shape[0] * owners
    scale = 1.0 / (points * slabs)
    inputs = (snapshots, row_scales, block_offsets, freq_index)
    if slabs == 2 and freqs == owners and owners % INNER == 0:
        outer = owners // INNER
        spectra = block_spectra(outer, INNER, *inputs)
        near = [part.reshape(INNER, rows, points) for part in spectra]
        arrived = near[:1] + [
            lax.ppermute(near[d], "blk", [(i, i ^ (d * INNER)) for i in range(owners)])
            for d in range(1, outer)
        ]
        parts = list(regroup(arrived))
        both = ("space", "blk")
        other = [
            lax.ppermute(parts[e], both, [(i, (i + owners) % (2 * owners) ^ e) for i in range(2 * owners)])
            for e in range(INNER)
        ]
        own = parts[:1] + [
            lax.ppermute(parts[e], "blk", [(i, i ^ e) for i in range(owners)])
            for e in range(1, INNER)
        ]
        operands, slabs_here = own + other, 2
    else:
        chunks = block_spectra(1, 1, *inputs)[0].reshape(freqs, -1, points)
        x = lax.all_to_all(chunks, "blk", split_axis=0, concat_axis=0, tiled=True)
        x = x.reshape(-1, points)
        operands, slabs_here = [x, lax.psum(complex_gram(x), "space")], 0
    modes, factor = modes_and_factor(operands, width, points, slabs_here, scale)
    return modes[None], factor[None]


def solution(mesh):
    return jax.shard_map(
        functools.partial(local, mesh.shape["space"], mesh.shape["blk"]),
        mesh=mesh,
        in_specs=(P("blk", "space"), P("blk"), P("blk"), P()),
        out_specs=(P("blk", "space", None), P("blk", None, None, None)),
        check_vma=False,
    )
```

```python
import functools
import math

import jax
import jax.numpy as jnp
from jax import lax
from jax.experimental import pallas as pl
from jax.experimental.pallas import tpu as pltpu
from jax.sharding import PartitionSpec as P

NFFT = 512
PANEL = 8
SUB = 8
PIECE = 256
FEW_SLABS = 2
SIN_COEFS = (
    0.9999999765895043,
    -0.1666664763439475,
    0.008332899819203531,
    -0.0001980089750772882,
    2.5904879854375602e-06,
)


def cos_of_phase(phase):
    folded = jnp.abs((phase & (NFFT - 1)) - NFFT // 2) - NFFT // 4
    x = folded.astype(jnp.float32) * (2.0 * math.pi / NFFT)
    square = x * x
    total = jnp.full_like(x, SIN_COEFS[-1])
    for coef in SIN_COEFS[-2::-1]:
        total = total * square + coef
    return total * x


def spectra_kernel(
    snap_hbm, scales_hbm, offsets_hbm, freq_hbm, out_ref,
    snap_ref, scales_ref, offsets_ref, freq_ref, coef_ref, small_sems, snap_sems,
):
    snaps = snap_ref.shape[0]
    blocks = offsets_ref.shape[0]
    rows = 2 * blocks
    freqs = freq_ref.shape[0]
    small = [
        pltpu.make_async_copy(src, dst, small_sems.at[i])
        for i, (src, dst) in enumerate(
            ((offsets_hbm, offsets_ref), (freq_hbm, freq_ref), (scales_hbm, scales_ref))
        )
    ]
    pieces = [slice(at, min(at + PIECE, snaps)) for at in range(0, snaps, PIECE)]
    large = [
        pltpu.make_async_copy(snap_hbm.at[piece], snap_ref.at[piece], snap_sems.at[i])
        for i, piece in enumerate(pieces)
    ]
    for copy in small + large:
        copy.start()
    row = lax.broadcasted_iota(jnp.int32, (rows, snaps), 0)
    time = lax.broadcasted_iota(jnp.int32, (rows, snaps), 1)
    for copy in small:
        copy.wait()
    start = jnp.zeros((rows, snaps), jnp.int32)
    for b in range(blocks):
        start = jnp.where(row // 2 == b, offsets_ref[b], start)
    shifted = time - start
    hann = 0.5 - 0.5 * cos_of_phase(shifted)
    inside = (shifted >= 0) & (shifted < NFFT)
    scales = jnp.broadcast_to(scales_ref[...].reshape(1, snaps), (rows, snaps))
    weight = jnp.where(inside, hann * scales * (1.0 / math.sqrt(NFFT)), 0.0)
    base = shifted[:, :NFFT].astype(jnp.float32)
    quarter = (row[:, :NFFT] % 2) * (NFFT // 4)
    repeats = -(-snaps // NFFT)

    def rows_of(f):
        freq = freq_ref[f].astype(jnp.float32)
        table = cos_of_phase((base * freq).astype(jnp.int32) + quarter)
        return jnp.concatenate([table] * repeats, 1)[:, :snaps] * weight

    for f in range(0, freqs, 2):
        pair = jnp.concatenate([rows_of(f), rows_of(f + 1)], 0)
        coef_ref[f * rows:(f + 2) * rows, :] = pair.astype(jnp.bfloat16)
    total = jnp.zeros(out_ref.shape[1:], jnp.float32)
    for copy, piece in zip(large, pieces):
        copy.wait()
        total += jnp.dot(
            coef_ref[:, piece], snap_ref[piece], preferred_element_type=jnp.float32
        )
    result = total.astype(jnp.bfloat16)
    for copy in range(out_ref.shape[0]):
        out_ref[copy] = result


def block_spectra(copies, snapshots, row_scales, block_offsets, freq_index):
    snaps, points = snapshots.shape
    rows = 2 * block_offsets.shape[0] * freq_index.shape[0]
    pieces = -(-snaps // PIECE)
    return pl.pallas_call(
        spectra_kernel,
        out_shape=jax.ShapeDtypeStruct((copies, rows, points), jnp.bfloat16),
        in_specs=[pl.BlockSpec(memory_space=pltpu.HBM)] * 4,
        out_specs=pl.BlockSpec(memory_space=pltpu.VMEM),
        scratch_shapes=[
            pltpu.VMEM((snaps, points), jnp.bfloat16),
            pltpu.VMEM((snaps,), jnp.float32),
            pltpu.SMEM(block_offsets.shape, jnp.int32),
            pltpu.SMEM(freq_index.shape, jnp.int32),
            pltpu.VMEM((rows, snaps), jnp.bfloat16),
            pltpu.SemaphoreType.DMA((3,)),
            pltpu.SemaphoreType.DMA((pieces,)),
        ],
        compiler_params=pltpu.CompilerParams(vmem_limit_bytes=8 * 2**20),
        name="spectra",
    )(*(
        pltpu.with_memory_space_constraint(x, pltpu.HBM)
        for x in (snapshots, row_scales, block_offsets, freq_index)
    ))


def rotated(x, lane):
    axis = x.ndim - 1
    width = x.shape[axis]
    after = pltpu.roll(x, width - 1, axis)
    before = pltpu.roll(x, 1, axis)
    return jnp.where(lane % 2 == 0, -after, before)


def gram_rows(slabs, full_ref):
    width = full_ref.shape[0]
    full_ref[...] = sum(
        lax.dot_general(x, x, (((1,), (1,)), ((), ())), preferred_element_type=jnp.float32)
        for x in slabs
    )
    even = full_ref[pl.ds(0, width // 2, stride=2), :]
    odd = full_ref[pl.ds(1, width // 2, stride=2), :]
    lane = lax.broadcasted_iota(jnp.int32, odd.shape, 1)
    return even - rotated(odd, lane)


def gram_kernel(x_ref, out_ref, full_ref):
    out_ref[...] = gram_rows([x_ref[...]], full_ref)


def complex_gram(x):
    width = x.shape[0]
    return pl.pallas_call(
        gram_kernel,
        out_shape=jax.ShapeDtypeStruct((width // 2, width), jnp.float32),
        in_specs=[pl.BlockSpec(memory_space=pltpu.VMEM)],
        out_specs=pl.BlockSpec(memory_space=pltpu.VMEM),
        scratch_shapes=[pltpu.VMEM((width, width), jnp.float32)],
        compiler_params=pltpu.CompilerParams(vmem_limit_bytes=4 * 2**20),
        name="gram",
    )(x)


def tree_sum(terms):
    while len(terms) > 1:
        terms = [sum(terms[i:i + 2]) for i in range(0, len(terms), 2)]
    return terms[0]


def eliminate(rows, panel):
    count = len(rows)
    shape = rows[0].shape
    sub = lax.broadcasted_iota(jnp.int32, shape, 0)
    lane = lax.broadcasted_iota(jnp.int32, shape, 1)

    def over_lanes(x, at):
        return jnp.broadcast_to(x[:, at:at + 1], shape)

    def over_rows(x, at):
        return jnp.broadcast_to(x[at:at + 1, :], shape)

    rows = list(rows)
    final = [None] * count
    pivots = [None] * count
    for first in range(0, count * SUB, panel):
        own = first // SUB
        head, turned = rows[own], rotated(rows[own], lane)
        if first % SUB == 0:
            final[own], pivots[own] = head, jnp.ones(shape, jnp.float32)
        columns = [2 * (first + c) for c in range(panel)]
        raw = {
            i: [(over_lanes(rows[i], at), over_lanes(rows[i], at + 1)) for at in columns]
            for i in range(own, count)
        }
        here = raw[own]
        for c in range(panel):
            at = (first + c) % SUB
            here_row = sub == at
            pivot = over_rows(here[c][0], at)
            inverse = pl.reciprocal(pivot, approx=True)
            m_re = jnp.where(here_row, -inverse, here[c][0] * inverse)
            m_im = jnp.where(here_row, 0.0, here[c][1] * inverse)
            if first % SUB:
                m_re = jnp.where(sub < first % SUB, 0.0, m_re)
                m_im = jnp.where(sub < first % SUB, 0.0, m_im)
            final[own] = jnp.where(here_row, head, final[own])
            pivots[own] = jnp.where(here_row, pivot, pivots[own])
            for later in range(c + 1, panel):
                re, im = here[later]
                u_re, u_im = over_rows(re, at), over_rows(im, at)
                here[later] = (
                    jnp.where(here_row, 0.0, re) - (m_re * u_re - m_im * u_im),
                    jnp.where(here_row, 0.0, im) - (m_re * u_im + m_im * u_re),
                )
            on_re, on_im = lane == columns[c], lane == columns[c] + 1
            p = jnp.where(on_re, 1.0, jnp.where(on_im, 0.0, over_rows(head, at)))
            q = jnp.where(on_im, 1.0, jnp.where(on_re, 0.0, over_rows(turned, at)))
            cleared = here_row | ((on_re | on_im) & (sub >= first % SUB))
            head = jnp.where(cleared, 0.0, head) - (m_re * p + m_im * q)
            turned = jnp.where(cleared, 0.0, turned) - (m_re * q - m_im * p)
        rows[own] = head
        inside = (lane >= columns[0]) & (lane < columns[0] + 2 * panel)
        solved = [
            (over_rows(head, (first + c) % SUB), over_rows(turned, (first + c) % SUB))
            for c in range(panel)
        ]
        for i in range(own + 1, count):
            rows[i] = jnp.where(inside, 0.0, rows[i]) - tree_sum(
                [re * p + im * q for (re, im), (p, q) in zip(raw[i], solved)]
            )
    return final, pivots


def modes_kernel(scale, slabs, x_ref, *refs):
    *given, modes_ref, factor_ref, basis_ref, points_ref = refs
    width = basis_ref.shape[0]
    size = width // 2
    count = size // SUB
    if given:
        gram = given[0][...]
        mine = x_ref[...]
    else:
        gram = gram_rows([x_ref[i * width:(i + 1) * width] for i in range(slabs)], basis_ref)
        own = lax.axis_index("space")
        mine = x_ref[pl.ds(pl.multiple_of(own * width, width), width)]
    points = jnp.transpose(mine)
    points_ref[...] = jnp.concatenate([points, points], 1)
    gram = gram * scale
    rows, pivots = eliminate([gram[i * SUB:(i + 1) * SUB] for i in range(count)], PANEL)
    shape = rows[0].shape
    sub = lax.broadcasted_iota(jnp.int32, shape, 0)
    lane = lax.broadcasted_iota(jnp.int32, shape, 1)
    pick = jnp.where(lane < size, 2 * lane, 2 * (lane - size) + 1)
    for i in range(count):
        own_rows = slice(i * SUB, (i + 1) * SUB)
        root = lax.rsqrt(pivots[i])
        diagonal = 2 * (i * SUB + sub)
        left = jnp.where(lane < diagonal, rows[i], jnp.where(lane == diagonal, 1.0, 0.0)) * root
        basis_ref[pl.ds(2 * i * SUB, SUB, stride=2), :] = left
        basis_ref[pl.ds(2 * i * SUB + 1, SUB, stride=2), :] = rotated(left, lane)
        right = jnp.where(lane > diagonal + 1, rows[i], jnp.where(lane == diagonal, pivots[i], 0.0))
        parts = jnp.take_along_axis(right * root, pick, axis=1)
        factor_ref[0, own_rows, :] = parts[:, :size]
        factor_ref[1, own_rows, :] = parts[:, size:]
    basis = basis_ref[...]
    high = basis.astype(jnp.bfloat16)
    low = (basis - high.astype(jnp.float32)).astype(jnp.bfloat16)
    modes_ref[...] = lax.dot_general(
        points_ref[...], jnp.concatenate([high, low], 1), (((1,), (1,)), ((), ())),
        preferred_element_type=jnp.float32,
    )


def modes_and_factor(x, grams, width, slabs, scale):
    points = x.shape[1]
    size = width // 2
    return pl.pallas_call(
        functools.partial(modes_kernel, scale, slabs),
        out_shape=(
            jax.ShapeDtypeStruct((points, width), jnp.float32),
            jax.ShapeDtypeStruct((2, size, size), jnp.float32),
        ),
        in_specs=[pl.BlockSpec(memory_space=pltpu.VMEM)] * (1 + len(grams)),
        out_specs=(pl.BlockSpec(memory_space=pltpu.VMEM),) * 2,
        scratch_shapes=[
            pltpu.VMEM((width, width), jnp.float32),
            pltpu.VMEM((points, 2 * width), jnp.bfloat16),
        ],
        compiler_params=pltpu.CompilerParams(vmem_limit_bytes=8 * 2**20),
        name="factor_and_modes",
    )(x, *grams)


def local(slabs, snapshots, row_scales, block_offsets, freq_index):
    freqs = freq_index.shape[0]
    points = snapshots.shape[1]
    width = 2 * block_offsets.shape[0] * lax.axis_size("blk")
    copies = slabs if slabs <= FEW_SLABS else 1
    spectra = block_spectra(copies, snapshots, row_scales, block_offsets, freq_index)
    chunks = spectra.reshape(copies * freqs, -1, points)
    swap = functools.partial(lax.all_to_all, split_axis=0, concat_axis=0, tiled=True)
    if copies == slabs:
        x = swap(chunks, ("space", "blk")).reshape(-1, points)
        grams = []
    else:
        x = swap(chunks, "blk").reshape(-1, points)
        grams = [lax.psum(complex_gram(x), "space")]
    modes, factor = modes_and_factor(x, grams, width, slabs, 1.0 / (points * slabs))
    return modes[None], factor[None]


def solution(mesh):
    return jax.shard_map(
        functools.partial(local, mesh.shape["space"]),
        mesh=mesh,
        in_specs=(P("blk", "space"), P("blk"), P("blk"), P()),
        out_specs=(P("blk", "space", None), P("blk", None, None, None)),
        check_vma=False,
    )
```

```python
import functools
import math

import jax
import jax.numpy as jnp
from jax import lax
from jax.experimental import pallas as pl
from jax.experimental.pallas import tpu as pltpu
from jax.sharding import PartitionSpec as P

NFFT = 512
PANEL = 4
SUB = 8
PIECE = 256
FEW_SLABS = 2
SIN_COEFS = (
    0.9999999765895043,
    -0.1666664763439475,
    0.008332899819203531,
    -0.0001980089750772882,
    2.5904879854375602e-06,
)


def cos_of_phase(phase):
    folded = jnp.abs((phase & (NFFT - 1)) - NFFT // 2) - NFFT // 4
    x = folded.astype(jnp.float32) * (2.0 * math.pi / NFFT)
    square = x * x
    total = jnp.full_like(x, SIN_COEFS[-1])
    for coef in SIN_COEFS[-2::-1]:
        total = total * square + coef
    return total * x


def spectra_kernel(
    snap_hbm, scales_hbm, offsets_hbm, freq_hbm, out_ref,
    snap_ref, scales_ref, offsets_ref, freq_ref, coef_ref, small_sems, snap_sems,
):
    snaps = snap_ref.shape[0]
    blocks = offsets_ref.shape[0]
    rows = 2 * blocks
    freqs = freq_ref.shape[0]
    small = [
        pltpu.make_async_copy(src, dst, small_sems.at[i])
        for i, (src, dst) in enumerate(
            ((offsets_hbm, offsets_ref), (freq_hbm, freq_ref), (scales_hbm, scales_ref))
        )
    ]
    pieces = [slice(at, min(at + PIECE, snaps)) for at in range(0, snaps, PIECE)]
    large = [
        pltpu.make_async_copy(snap_hbm.at[piece], snap_ref.at[piece], snap_sems.at[i])
        for i, piece in enumerate(pieces)
    ]
    for copy in small + large:
        copy.start()
    row = lax.broadcasted_iota(jnp.int32, (rows, snaps), 0)
    time = lax.broadcasted_iota(jnp.int32, (rows, snaps), 1)
    for copy in small:
        copy.wait()
    start = jnp.zeros((rows, snaps), jnp.int32)
    for b in range(blocks):
        start = jnp.where(row // 2 == b, offsets_ref[b], start)
    shifted = time - start
    hann = 0.5 - 0.5 * cos_of_phase(shifted)
    inside = (shifted >= 0) & (shifted < NFFT)
    scales = jnp.broadcast_to(scales_ref[...].reshape(1, snaps), (rows, snaps))
    weight = jnp.where(inside, hann * scales * (1.0 / math.sqrt(NFFT)), 0.0)
    base = shifted[:, :NFFT].astype(jnp.float32)
    quarter = (row[:, :NFFT] % 2) * (NFFT // 4)
    repeats = -(-snaps // NFFT)

    def rows_of(f):
        freq = freq_ref[f].astype(jnp.float32)
        table = cos_of_phase((base * freq).astype(jnp.int32) + quarter)
        return jnp.concatenate([table] * repeats, 1)[:, :snaps] * weight

    for f in range(0, freqs, 2):
        pair = jnp.concatenate([rows_of(f), rows_of(f + 1)], 0)
        coef_ref[f * rows:(f + 2) * rows, :] = pair.astype(jnp.bfloat16)
    total = jnp.zeros(coef_ref.shape[:1] + snap_ref.shape[1:], jnp.float32)
    for copy, piece in zip(large, pieces):
        copy.wait()
        total += jnp.dot(
            coef_ref[:, piece], snap_ref[piece], preferred_element_type=jnp.float32
        )
    for f in range(freqs):
        one = total[f * rows:(f + 1) * rows]
        out_ref[f] = jnp.concatenate([one] * (out_ref.shape[1] // rows), 0).astype(jnp.bfloat16)


def block_spectra(copies, snapshots, row_scales, block_offsets, freq_index):
    snaps, points = snapshots.shape
    freqs = freq_index.shape[0]
    rows = 2 * block_offsets.shape[0]
    pieces = -(-snaps // PIECE)
    return pl.pallas_call(
        spectra_kernel,
        out_shape=jax.ShapeDtypeStruct((freqs, copies * rows, points), jnp.bfloat16),
        in_specs=[pl.BlockSpec(memory_space=pltpu.HBM)] * 4,
        out_specs=pl.BlockSpec(memory_space=pltpu.VMEM),
        scratch_shapes=[
            pltpu.VMEM((snaps, points), jnp.bfloat16),
            pltpu.VMEM((snaps,), jnp.float32),
            pltpu.SMEM(block_offsets.shape, jnp.int32),
            pltpu.SMEM(freq_index.shape, jnp.int32),
            pltpu.VMEM((freqs * rows, snaps), jnp.bfloat16),
            pltpu.SemaphoreType.DMA((3,)),
            pltpu.SemaphoreType.DMA((pieces,)),
        ],
        compiler_params=pltpu.CompilerParams(vmem_limit_bytes=8 * 2**20),
        name="spectra",
    )(*(
        pltpu.with_memory_space_constraint(x, pltpu.HBM)
        for x in (snapshots, row_scales, block_offsets, freq_index)
    ))


def rotated(x, lane):
    axis = x.ndim - 1
    width = x.shape[axis]
    after = pltpu.roll(x, width - 1, axis)
    before = pltpu.roll(x, 1, axis)
    return jnp.where(lane % 2 == 0, -after, before)


def gram_rows(slabs, full_ref):
    width = full_ref.shape[0]
    full_ref[...] = sum(
        lax.dot_general(x, x, (((1,), (1,)), ((), ())), preferred_element_type=jnp.float32)
        for x in slabs
    )
    even = full_ref[pl.ds(0, width // 2, stride=2), :]
    odd = full_ref[pl.ds(1, width // 2, stride=2), :]
    lane = lax.broadcasted_iota(jnp.int32, odd.shape, 1)
    return even - rotated(odd, lane)


def gram_kernel(x_ref, out_ref, full_ref):
    out_ref[...] = gram_rows([x_ref[...]], full_ref)


def complex_gram(x):
    width = x.shape[0]
    return pl.pallas_call(
        gram_kernel,
        out_shape=jax.ShapeDtypeStruct((width // 2, width), jnp.float32),
        in_specs=[pl.BlockSpec(memory_space=pltpu.VMEM)],
        out_specs=pl.BlockSpec(memory_space=pltpu.VMEM),
        scratch_shapes=[pltpu.VMEM((width, width), jnp.float32)],
        compiler_params=pltpu.CompilerParams(vmem_limit_bytes=4 * 2**20),
        name="gram",
    )(x)


def tree_sum(terms):
    while len(terms) > 1:
        terms = [sum(terms[i:i + 2]) for i in range(0, len(terms), 2)]
    return terms[0]


def eliminate(rows, panel):
    count = len(rows)
    shape = rows[0].shape
    sub = lax.broadcasted_iota(jnp.int32, shape, 0)
    lane = lax.broadcasted_iota(jnp.int32, shape, 1)

    def over_lanes(x, at):
        return jnp.broadcast_to(x[:, at:at + 1], shape)

    def over_rows(x, at):
        return jnp.broadcast_to(x[at:at + 1, :], shape)

    rows = list(rows)
    final = [None] * count
    pivots = [None] * count
    for first in range(0, count * SUB, panel):
        own = first // SUB
        head, turned = rows[own], rotated(rows[own], lane)
        if first % SUB == 0:
            final[own], pivots[own] = head, jnp.ones(shape, jnp.float32)
        columns = [2 * (first + c) for c in range(panel)]
        raw = {
            i: [(over_lanes(rows[i], at), over_lanes(rows[i], at + 1)) for at in columns]
            for i in range(own, count)
        }
        here = raw[own]
        for c in range(panel):
            at = (first + c) % SUB
            here_row = sub == at
            pivot = over_rows(here[c][0], at)
            inverse = pl.reciprocal(pivot, approx=True)
            m_re = jnp.where(here_row, -inverse, here[c][0] * inverse)
            m_im = jnp.where(here_row, 0.0, here[c][1] * inverse)
            if first % SUB:
                m_re = jnp.where(sub < first % SUB, 0.0, m_re)
                m_im = jnp.where(sub < first % SUB, 0.0, m_im)
            final[own] = jnp.where(here_row, head, final[own])
            pivots[own] = jnp.where(here_row, pivot, pivots[own])
            for later in range(c + 1, panel):
                re, im = here[later]
                u_re, u_im = over_rows(re, at), over_rows(im, at)
                here[later] = (
                    jnp.where(here_row, 0.0, re) - (m_re * u_re - m_im * u_im),
                    jnp.where(here_row, 0.0, im) - (m_re * u_im + m_im * u_re),
                )
            on_re, on_im = lane == columns[c], lane == columns[c] + 1
            p = jnp.where(on_re, 1.0, jnp.where(on_im, 0.0, over_rows(head, at)))
            q = jnp.where(on_im, 1.0, jnp.where(on_re, 0.0, over_rows(turned, at)))
            cleared = here_row | ((on_re | on_im) & (sub >= first % SUB))
            head = jnp.where(cleared, 0.0, head) - (m_re * p + m_im * q)
            turned = jnp.where(cleared, 0.0, turned) - (m_re * q - m_im * p)
        rows[own] = head
        inside = (lane >= columns[0]) & (lane < columns[0] + 2 * panel)
        solved = [
            (over_rows(head, (first + c) % SUB), over_rows(turned, (first + c) % SUB))
            for c in range(panel)
        ]
        for i in range(own + 1, count):
            rows[i] = jnp.where(inside, 0.0, rows[i]) - tree_sum(
                [re * p + im * q for (re, im), (p, q) in zip(raw[i], solved)]
            )
    return final, pivots


def modes_kernel(scale, slabs, rows, x_ref, *refs):
    *given, modes_ref, factor_ref, basis_ref, points_ref = refs
    width = basis_ref.shape[0]
    size = width // 2
    count = size // SUB
    if given:
        gram = given[0][...]
        mine = x_ref[...]
    else:
        points = x_ref.shape[1]
        both = x_ref[...].astype(jnp.float32).reshape(-1, slabs, rows, points)
        split = [both[:, i].reshape(width, points).astype(jnp.bfloat16) for i in range(slabs)]
        gram = gram_rows(split, basis_ref)
        own = lax.axis_index("space")
        mine = split[0]
        for i in range(1, slabs):
            mine = jnp.where(own == i, split[i], mine)
    points = jnp.transpose(mine)
    points_ref[...] = jnp.concatenate([points, points], 1)
    gram = gram * scale
    factored, pivots = eliminate([gram[i * SUB:(i + 1) * SUB] for i in range(count)], PANEL)
    shape = factored[0].shape
    sub = lax.broadcasted_iota(jnp.int32, shape, 0)
    lane = lax.broadcasted_iota(jnp.int32, shape, 1)
    pick = jnp.where(lane < size, 2 * lane, 2 * (lane - size) + 1)
    for i in range(count):
        own_rows = slice(i * SUB, (i + 1) * SUB)
        root = lax.rsqrt(pivots[i])
        diagonal = 2 * (i * SUB + sub)
        left = jnp.where(lane < diagonal, factored[i], jnp.where(lane == diagonal, 1.0, 0.0)) * root
        basis_ref[pl.ds(2 * i * SUB, SUB, stride=2), :] = left
        basis_ref[pl.ds(2 * i * SUB + 1, SUB, stride=2), :] = rotated(left, lane)
        right = jnp.where(lane > diagonal + 1, factored[i], jnp.where(lane == diagonal, pivots[i], 0.0))
        parts = jnp.take_along_axis(right * root, pick, axis=1)
        factor_ref[0, own_rows, :] = parts[:, :size]
        factor_ref[1, own_rows, :] = parts[:, size:]
    basis = basis_ref[...]
    high = basis.astype(jnp.bfloat16)
    low = (basis - high.astype(jnp.float32)).astype(jnp.bfloat16)
    modes_ref[...] = lax.dot_general(
        points_ref[...], jnp.concatenate([high, low], 1), (((1,), (1,)), ((), ())),
        preferred_element_type=jnp.float32,
    )


def modes_and_factor(x, grams, width, slabs, rows, scale):
    points = x.shape[1]
    size = width // 2
    return pl.pallas_call(
        functools.partial(modes_kernel, scale, slabs, rows),
        out_shape=(
            jax.ShapeDtypeStruct((points, width), jnp.float32),
            jax.ShapeDtypeStruct((2, size, size), jnp.float32),
        ),
        in_specs=[pl.BlockSpec(memory_space=pltpu.VMEM)] * (1 + len(grams)),
        out_specs=(pl.BlockSpec(memory_space=pltpu.VMEM),) * 2,
        scratch_shapes=[
            pltpu.VMEM((width, width), jnp.float32),
            pltpu.VMEM((points, 2 * width), jnp.bfloat16),
        ],
        compiler_params=pltpu.CompilerParams(vmem_limit_bytes=8 * 2**20),
        name="factor_and_modes",
    )(x, *grams)


def local(slabs, snapshots, row_scales, block_offsets, freq_index):
    freqs = freq_index.shape[0]
    points = snapshots.shape[1]
    width = 2 * block_offsets.shape[0] * lax.axis_size("blk")
    rows = 2 * block_offsets.shape[0]
    copies = slabs if slabs <= FEW_SLABS else 1
    spectra = block_spectra(copies, snapshots, row_scales, block_offsets, freq_index)
    chunks = spectra.reshape(copies * freqs, rows, points)
    swap = functools.partial(lax.all_to_all, split_axis=0, concat_axis=0, tiled=True)
    if copies == slabs:
        x = swap(chunks, ("blk", "space")).reshape(-1, points)
        grams = []
    else:
        x = swap(chunks, "blk").reshape(-1, points)
        grams = [lax.psum(complex_gram(x), "space")]
    modes, factor = modes_and_factor(x, grams, width, slabs, rows, 1.0 / (points * slabs))
    return modes[None], factor[None]


def solution(mesh):
    return jax.shard_map(
        functools.partial(local, mesh.shape["space"]),
        mesh=mesh,
        in_specs=(P("blk", "space"), P("blk"), P("blk"), P()),
        out_specs=(P("blk", "space", None), P("blk", None, None, None)),
        check_vma=False,
    )
```

```python
import functools
import math

import jax
import jax.numpy as jnp
from jax import lax
from jax.experimental import pallas as pl
from jax.experimental.pallas import tpu as pltpu
from jax.sharding import PartitionSpec as P

NFFT = 512
PANEL = 8
SUB = 8
PIECE = 256
FEW_SLABS = 2
SIN_COEFS = (
    0.9999999765895043,
    -0.1666664763439475,
    0.008332899819203531,
    -0.0001980089750772882,
    2.5904879854375602e-06,
)


def cos_of_phase(phase):
    folded = jnp.abs((phase & (NFFT - 1)) - NFFT // 2) - NFFT // 4
    x = folded.astype(jnp.float32) * (2.0 * math.pi / NFFT)
    square = x * x
    total = jnp.full_like(x, SIN_COEFS[-1])
    for coef in SIN_COEFS[-2::-1]:
        total = total * square + coef
    return total * x


def spectra_kernel(
    snap_hbm, scales_hbm, offsets_hbm, freq_hbm, out_ref,
    snap_ref, scales_ref, offsets_ref, freq_ref, coef_ref, small_sems, snap_sems,
):
    snaps = snap_ref.shape[0]
    blocks = offsets_ref.shape[0]
    rows = 2 * blocks
    freqs = freq_ref.shape[0]
    small = [
        pltpu.make_async_copy(src, dst, small_sems.at[i])
        for i, (src, dst) in enumerate(
            ((offsets_hbm, offsets_ref), (freq_hbm, freq_ref), (scales_hbm, scales_ref))
        )
    ]
    pieces = [slice(at, min(at + PIECE, snaps)) for at in range(0, snaps, PIECE)]
    large = [
        pltpu.make_async_copy(snap_hbm.at[piece], snap_ref.at[piece], snap_sems.at[i])
        for i, piece in enumerate(pieces)
    ]
    for copy in small + large:
        copy.start()
    row = lax.broadcasted_iota(jnp.int32, (rows, snaps), 0)
    time = lax.broadcasted_iota(jnp.int32, (rows, snaps), 1)
    for copy in small:
        copy.wait()
    start = jnp.zeros((rows, snaps), jnp.int32)
    for b in range(blocks):
        start = jnp.where(row // 2 == b, offsets_ref[b], start)
    shifted = time - start
    hann = 0.5 - 0.5 * cos_of_phase(shifted)
    inside = (shifted >= 0) & (shifted < NFFT)
    scales = jnp.broadcast_to(scales_ref[...].reshape(1, snaps), (rows, snaps))
    weight = jnp.where(inside, hann * scales * (1.0 / math.sqrt(NFFT)), 0.0)
    base = shifted[:, :NFFT].astype(jnp.float32)
    quarter = (row[:, :NFFT] % 2) * (NFFT // 4)
    repeats = -(-snaps // NFFT)

    def rows_of(f):
        freq = freq_ref[f].astype(jnp.float32)
        table = cos_of_phase((base * freq).astype(jnp.int32) + quarter)
        return jnp.concatenate([table] * repeats, 1)[:, :snaps] * weight

    for f in range(0, freqs, 2):
        pair = jnp.concatenate([rows_of(f), rows_of(f + 1)], 0)
        coef_ref[f * rows:(f + 2) * rows, :] = pair.astype(jnp.bfloat16)
    for copy in large:
        copy.wait()
    total = jnp.dot(coef_ref[...], snap_ref[...], preferred_element_type=jnp.float32)
    result = total.astype(jnp.bfloat16)
    for copy in range(out_ref.shape[0]):
        out_ref[copy] = result


def block_spectra(copies, snapshots, row_scales, block_offsets, freq_index):
    snaps, points = snapshots.shape
    rows = 2 * block_offsets.shape[0] * freq_index.shape[0]
    pieces = -(-snaps // PIECE)
    return pl.pallas_call(
        spectra_kernel,
        out_shape=jax.ShapeDtypeStruct((copies, rows, points), jnp.bfloat16),
        in_specs=[pl.BlockSpec(memory_space=pltpu.HBM)] * 4,
        out_specs=pl.BlockSpec(memory_space=pltpu.VMEM),
        scratch_shapes=[
            pltpu.VMEM((snaps, points), jnp.bfloat16),
            pltpu.VMEM((snaps,), jnp.float32),
            pltpu.SMEM(block_offsets.shape, jnp.int32),
            pltpu.SMEM(freq_index.shape, jnp.int32),
            pltpu.VMEM((rows, snaps), jnp.bfloat16),
            pltpu.SemaphoreType.DMA((3,)),
            pltpu.SemaphoreType.DMA((pieces,)),
        ],
        compiler_params=pltpu.CompilerParams(vmem_limit_bytes=8 * 2**20),
        name="spectra",
    )(*(
        pltpu.with_memory_space_constraint(x, pltpu.HBM)
        for x in (snapshots, row_scales, block_offsets, freq_index)
    ))


def rotated(x, lane):
    axis = x.ndim - 1
    width = x.shape[axis]
    after = pltpu.roll(x, width - 1, axis)
    before = pltpu.roll(x, 1, axis)
    return jnp.where(lane % 2 == 0, -after, before)


def gram_rows(slabs, full_ref):
    width = full_ref.shape[0]
    full_ref[...] = sum(
        lax.dot_general(x, x, (((1,), (1,)), ((), ())), preferred_element_type=jnp.float32)
        for x in slabs
    )
    even = full_ref[pl.ds(0, width // 2, stride=2), :]
    odd = full_ref[pl.ds(1, width // 2, stride=2), :]
    lane = lax.broadcasted_iota(jnp.int32, odd.shape, 1)
    return even - rotated(odd, lane)


def gram_kernel(x_ref, out_ref, full_ref):
    out_ref[...] = gram_rows([x_ref[...]], full_ref)


def complex_gram(x):
    width = x.shape[0]
    return pl.pallas_call(
        gram_kernel,
        out_shape=jax.ShapeDtypeStruct((width // 2, width), jnp.float32),
        in_specs=[pl.BlockSpec(memory_space=pltpu.VMEM)],
        out_specs=pl.BlockSpec(memory_space=pltpu.VMEM),
        scratch_shapes=[pltpu.VMEM((width, width), jnp.float32)],
        compiler_params=pltpu.CompilerParams(vmem_limit_bytes=4 * 2**20),
        name="gram",
    )(x)


def tree_sum(terms):
    while len(terms) > 1:
        terms = [sum(terms[i:i + 2]) for i in range(0, len(terms), 2)]
    return terms[0]


def eliminate(rows, panel):
    count = len(rows)
    shape = rows[0].shape
    sub = lax.broadcasted_iota(jnp.int32, shape, 0)
    lane = lax.broadcasted_iota(jnp.int32, shape, 1)

    def over_lanes(x, at):
        return jnp.broadcast_to(x[:, at:at + 1], shape)

    def over_rows(x, at):
        return jnp.broadcast_to(x[at:at + 1, :], shape)

    rows = list(rows)
    final = [None] * count
    pivots = [None] * count
    for first in range(0, count * SUB, panel):
        own = first // SUB
        head, turned = rows[own], rotated(rows[own], lane)
        if first % SUB == 0:
            final[own], pivots[own] = head, jnp.ones(shape, jnp.float32)
        columns = [2 * (first + c) for c in range(panel)]
        raw = {
            i: [(over_lanes(rows[i], at), over_lanes(rows[i], at + 1)) for at in columns]
            for i in range(own, count)
        }
        here = raw[own]
        pivot = over_rows(here[0][0], first % SUB)
        for c in range(panel):
            at = (first + c) % SUB
            here_row = sub == at
            inverse = pl.reciprocal(pivot, approx=True)
            m_re = jnp.where(here_row, -1.0, here[c][0])
            m_im = jnp.where(here_row, 0.0, here[c][1])
            if first % SUB:
                m_re = jnp.where(sub < first % SUB, 0.0, m_re)
                m_im = jnp.where(sub < first % SUB, 0.0, m_im)
            m_re, m_im = m_re * inverse, m_im * inverse
            final[own] = jnp.where(here_row, head, final[own])
            pivots[own] = jnp.where(here_row, pivot, pivots[own])
            for later in range(c + 1, panel):
                re, im = here[later]
                u_re, u_im = over_rows(re, at), over_rows(im, at)
                if later == c + 1:
                    loss = (u_re * inverse) * u_re + (u_im * inverse) * u_im
                    pivot = over_rows(re, at + 1) - loss
                here[later] = (
                    jnp.where(here_row, 0.0, re) - m_re * u_re + m_im * u_im,
                    jnp.where(here_row, 0.0, im) - m_re * u_im - m_im * u_re,
                )
            on_re, on_im = lane == columns[c], lane == columns[c] + 1
            on_pair = on_re | on_im
            p = jnp.where(on_pair, on_re.astype(jnp.float32), over_rows(head, at))
            q = jnp.where(on_pair, on_im.astype(jnp.float32), over_rows(turned, at))
            cleared = here_row | (on_pair & (sub >= first % SUB))
            head = jnp.where(cleared, 0.0, head) - (m_re * p + m_im * q)
            turned = jnp.where(cleared, 0.0, turned) - (m_re * q - m_im * p)
        rows[own] = head
        inside = (lane >= columns[0]) & (lane < columns[0] + 2 * panel)
        solved = [
            (over_rows(head, (first + c) % SUB), over_rows(turned, (first + c) % SUB))
            for c in range(panel)
        ]
        for i in range(own + 1, count):
            rows[i] = jnp.where(inside, 0.0, rows[i]) - tree_sum(
                [re * p + im * q for (re, im), (p, q) in zip(raw[i], solved)]
            )
    return final, pivots


def modes_kernel(scale, slabs, x_ref, *refs):
    *given, modes_ref, factor_ref, basis_ref, points_ref = refs
    width = basis_ref.shape[0]
    size = width // 2
    count = size // SUB
    if given:
        gram = given[0][...]
        mine = x_ref[...]
    else:
        gram = gram_rows([x_ref[i * width:(i + 1) * width] for i in range(slabs)], basis_ref)
        own = lax.axis_index("space")
        mine = x_ref[pl.ds(pl.multiple_of(own * width, width), width)]
    points = jnp.transpose(mine)
    points_ref[...] = jnp.concatenate([points, points], 1)
    gram = gram * scale
    rows, pivots = eliminate([gram[i * SUB:(i + 1) * SUB] for i in range(count)], PANEL)
    shape = rows[0].shape
    sub = lax.broadcasted_iota(jnp.int32, shape, 0)
    lane = lax.broadcasted_iota(jnp.int32, shape, 1)
    pick = jnp.where(lane < size, 2 * lane, 2 * (lane - size) + 1)
    for i in range(count):
        own_rows = slice(i * SUB, (i + 1) * SUB)
        root = lax.rsqrt(pivots[i])
        diagonal = 2 * (i * SUB + sub)
        left = jnp.where(lane < diagonal, rows[i], jnp.where(lane == diagonal, 1.0, 0.0)) * root
        basis_ref[pl.ds(2 * i * SUB, SUB, stride=2), :] = left
        basis_ref[pl.ds(2 * i * SUB + 1, SUB, stride=2), :] = rotated(left, lane)
        right = jnp.where(lane > diagonal + 1, rows[i], jnp.where(lane == diagonal, pivots[i], 0.0))
        parts = jnp.take_along_axis(right * root, pick, axis=1)
        factor_ref[0, own_rows, :] = parts[:, :size]
        factor_ref[1, own_rows, :] = parts[:, size:]
    basis = basis_ref[...]
    high = basis.astype(jnp.bfloat16)
    low = (basis - high.astype(jnp.float32)).astype(jnp.bfloat16)
    modes_ref[...] = lax.dot_general(
        points_ref[...], jnp.concatenate([high, low], 1), (((1,), (1,)), ((), ())),
        preferred_element_type=jnp.float32,
    )


def modes_and_factor(x, grams, width, slabs, scale):
    points = x.shape[1]
    size = width // 2
    return pl.pallas_call(
        functools.partial(modes_kernel, scale, slabs),
        out_shape=(
            jax.ShapeDtypeStruct((points, width), jnp.float32),
            jax.ShapeDtypeStruct((2, size, size), jnp.float32),
        ),
        in_specs=[pl.BlockSpec(memory_space=pltpu.VMEM)] * (1 + len(grams)),
        out_specs=(pl.BlockSpec(memory_space=pltpu.VMEM),) * 2,
        scratch_shapes=[
            pltpu.VMEM((width, width), jnp.float32),
            pltpu.VMEM((points, 2 * width), jnp.bfloat16),
        ],
        compiler_params=pltpu.CompilerParams(vmem_limit_bytes=8 * 2**20),
        name="factor_and_modes",
    )(x, *grams)


def local(slabs, snapshots, row_scales, block_offsets, freq_index):
    freqs = freq_index.shape[0]
    points = snapshots.shape[1]
    width = 2 * block_offsets.shape[0] * lax.axis_size("blk")
    copies = slabs if slabs <= FEW_SLABS else 1
    spectra = block_spectra(copies, snapshots, row_scales, block_offsets, freq_index)
    chunks = spectra.reshape(copies * freqs, -1, points)
    swap = functools.partial(lax.all_to_all, split_axis=0, concat_axis=0, tiled=True)
    if copies == slabs:
        x = swap(chunks, ("space", "blk")).reshape(-1, points)
        grams = []
    else:
        x = swap(chunks, "blk").reshape(-1, points)
        grams = [lax.psum(complex_gram(x), "space")]
    modes, factor = modes_and_factor(x, grams, width, slabs, 1.0 / (points * slabs))
    return modes[None], factor[None]


def solution(mesh):
    return jax.shard_map(
        functools.partial(local, mesh.shape["space"]),
        mesh=mesh,
        in_specs=(P("blk", "space"), P("blk"), P("blk"), P()),
        out_specs=(P("blk", "space", None), P("blk", None, None, None)),
        check_vma=False,
    )
```

```python
import functools
import math

import jax
import jax.numpy as jnp
from jax import lax
from jax.experimental import pallas as pl
from jax.experimental.pallas import tpu as pltpu
from jax.sharding import PartitionSpec as P

NFFT = 512
PANEL = 8
SUB = 8
PIECE = 256
PARTS = 4
FEW_SLABS = 2
SIN_COEFS = (
    0.9999999765895043,
    -0.1666664763439475,
    0.008332899819203531,
    -0.0001980089750772882,
    2.5904879854375602e-06,
)


def cos_of_phase(phase):
    folded = jnp.abs((phase & (NFFT - 1)) - NFFT // 2) - NFFT // 4
    x = folded.astype(jnp.float32) * (2.0 * math.pi / NFFT)
    square = x * x
    total = jnp.full_like(x, SIN_COEFS[-1])
    for coef in SIN_COEFS[-2::-1]:
        total = total * square + coef
    return total * x


def spectra_kernel(
    snap_hbm, scales_hbm, offsets_hbm, freq_hbm, out_ref,
    snap_ref, scales_ref, offsets_ref, freq_ref, coef_ref, small_sems, snap_sems,
):
    snaps = snap_ref.shape[0]
    blocks = offsets_ref.shape[0]
    rows = 2 * blocks
    freqs = freq_ref.shape[0]
    small = [
        pltpu.make_async_copy(src, dst, small_sems.at[i])
        for i, (src, dst) in enumerate(
            ((offsets_hbm, offsets_ref), (freq_hbm, freq_ref), (scales_hbm, scales_ref))
        )
    ]
    pieces = [slice(at, min(at + PIECE, snaps)) for at in range(0, snaps, PIECE)]
    large = [
        pltpu.make_async_copy(snap_hbm.at[piece], snap_ref.at[piece], snap_sems.at[i])
        for i, piece in enumerate(pieces)
    ]
    for copy in small + large:
        copy.start()
    row = lax.broadcasted_iota(jnp.int32, (rows, snaps), 0)
    time = lax.broadcasted_iota(jnp.int32, (rows, snaps), 1)
    for copy in small:
        copy.wait()
    start = jnp.zeros((rows, snaps), jnp.int32)
    for b in range(blocks):
        start = jnp.where(row // 2 == b, offsets_ref[b], start)
    shifted = time - start
    hann = 0.5 - 0.5 * cos_of_phase(shifted)
    inside = (shifted >= 0) & (shifted < NFFT)
    scales = jnp.broadcast_to(scales_ref[...].reshape(1, snaps), (rows, snaps))
    weight = jnp.where(inside, hann * scales * (1.0 / math.sqrt(NFFT)), 0.0)
    base = shifted[:, :NFFT].astype(jnp.float32)
    quarter = (row[:, :NFFT] % 2) * (NFFT // 4)
    repeats = -(-snaps // NFFT)

    def rows_of(f):
        freq = freq_ref[f].astype(jnp.float32)
        table = cos_of_phase((base * freq).astype(jnp.int32) + quarter)
        return jnp.concatenate([table] * repeats, 1)[:, :snaps] * weight

    for f in range(0, freqs, 2):
        pair = jnp.concatenate([rows_of(f), rows_of(f + 1)], 0)
        coef_ref[f * rows:(f + 2) * rows, :] = pair.astype(jnp.bfloat16)
    for copy in large:
        copy.wait()
    total = jnp.dot(coef_ref[...], snap_ref[...], preferred_element_type=jnp.float32)
    result = total.astype(jnp.bfloat16)
    for copy in range(out_ref.shape[0]):
        out_ref[copy] = result


def block_spectra(copies, snapshots, row_scales, block_offsets, freq_index):
    snaps, points = snapshots.shape
    rows = 2 * block_offsets.shape[0] * freq_index.shape[0]
    pieces = -(-snaps // PIECE)
    return pl.pallas_call(
        spectra_kernel,
        out_shape=jax.ShapeDtypeStruct((copies, rows, points), jnp.bfloat16),
        in_specs=[pl.BlockSpec(memory_space=pltpu.HBM)] * 4,
        out_specs=pl.BlockSpec(memory_space=pltpu.VMEM),
        scratch_shapes=[
            pltpu.VMEM((snaps, points), jnp.bfloat16),
            pltpu.VMEM((snaps,), jnp.float32),
            pltpu.SMEM(block_offsets.shape, jnp.int32),
            pltpu.SMEM(freq_index.shape, jnp.int32),
            pltpu.VMEM((rows, snaps), jnp.bfloat16),
            pltpu.SemaphoreType.DMA((3,)),
            pltpu.SemaphoreType.DMA((pieces,)),
        ],
        compiler_params=pltpu.CompilerParams(vmem_limit_bytes=8 * 2**20),
        name="spectra",
    )(*(
        pltpu.with_memory_space_constraint(x, pltpu.HBM)
        for x in (snapshots, row_scales, block_offsets, freq_index)
    ))


def rotated(x, lane):
    axis = x.ndim - 1
    width = x.shape[axis]
    after = pltpu.roll(x, width - 1, axis)
    before = pltpu.roll(x, 1, axis)
    return jnp.where(lane % 2 == 0, -after, before)


def gram_rows(slabs, full_ref):
    width = full_ref.shape[0]
    full_ref[...] = sum(
        lax.dot_general(x, x, (((1,), (1,)), ((), ())), preferred_element_type=jnp.float32)
        for x in slabs
    )
    even = full_ref[pl.ds(0, width // 2, stride=2), :]
    odd = full_ref[pl.ds(1, width // 2, stride=2), :]
    lane = lax.broadcasted_iota(jnp.int32, odd.shape, 1)
    return even - rotated(odd, lane)


def gram_kernel(x_ref, out_ref, full_ref):
    out_ref[...] = gram_rows([x_ref[...]], full_ref)


def complex_gram(x):
    width = x.shape[0]
    return pl.pallas_call(
        gram_kernel,
        out_shape=jax.ShapeDtypeStruct((width // 2, width), jnp.float32),
        in_specs=[pl.BlockSpec(memory_space=pltpu.VMEM)],
        out_specs=pl.BlockSpec(memory_space=pltpu.VMEM),
        scratch_shapes=[pltpu.VMEM((width, width), jnp.float32)],
        compiler_params=pltpu.CompilerParams(vmem_limit_bytes=4 * 2**20),
        name="gram",
    )(x)


def tree_sum(terms):
    while len(terms) > 1:
        terms = [sum(terms[i:i + 2]) for i in range(0, len(terms), 2)]
    return terms[0]


def eliminate(rows, panel):
    count = len(rows)
    shape = rows[0].shape
    sub = lax.broadcasted_iota(jnp.int32, shape, 0)
    lane = lax.broadcasted_iota(jnp.int32, shape, 1)

    def over_lanes(x, at):
        return jnp.broadcast_to(x[:, at:at + 1], shape)

    def over_rows(x, at):
        return jnp.broadcast_to(x[at:at + 1, :], shape)

    rows = list(rows)
    final = [None] * count
    final_turned = [None] * count
    pivots = [None] * count
    for first in range(0, count * SUB, panel):
        own = first // SUB
        head, turned = rows[own], rotated(rows[own], lane)
        if first % SUB == 0:
            final[own], final_turned[own] = head, turned
            pivots[own] = jnp.ones(shape, jnp.float32)
        columns = [2 * (first + c) for c in range(panel)]
        raw = {
            i: [(over_lanes(rows[i], at), over_lanes(rows[i], at + 1)) for at in columns]
            for i in range(own, count)
        }
        here = raw[own]
        pivot = over_rows(here[0][0], first % SUB)
        for c in range(panel):
            at = (first + c) % SUB
            here_row = sub == at
            inverse = pl.reciprocal(pivot, approx=True)
            m_re = jnp.where(here_row, -1.0, here[c][0])
            m_im = jnp.where(here_row, 0.0, here[c][1])
            if first % SUB:
                m_re = jnp.where(sub < first % SUB, 0.0, m_re)
                m_im = jnp.where(sub < first % SUB, 0.0, m_im)
            m_re, m_im = m_re * inverse, m_im * inverse
            final[own] = jnp.where(here_row, head, final[own])
            final_turned[own] = jnp.where(here_row, turned, final_turned[own])
            pivots[own] = jnp.where(here_row, pivot, pivots[own])
            for later in range(c + 1, panel):
                re, im = here[later]
                u_re, u_im = over_rows(re, at), over_rows(im, at)
                if later == c + 1:
                    loss = (u_re * inverse) * u_re + (u_im * inverse) * u_im
                    pivot = over_rows(re, at + 1) - loss
                here[later] = (
                    jnp.where(here_row, 0.0, re) - m_re * u_re + m_im * u_im,
                    jnp.where(here_row, 0.0, im) - m_re * u_im - m_im * u_re,
                )
            on_re, on_im = lane == columns[c], lane == columns[c] + 1
            on_pair = on_re | on_im
            p = jnp.where(on_pair, on_re.astype(jnp.float32), over_rows(head, at))
            q = jnp.where(on_pair, on_im.astype(jnp.float32), over_rows(turned, at))
            cleared = here_row | (on_pair & (sub >= first % SUB))
            head = jnp.where(cleared, 0.0, head) - (m_re * p + m_im * q)
            turned = jnp.where(cleared, 0.0, turned) - (m_re * q - m_im * p)
        rows[own] = head
        inside = (lane >= columns[0]) & (lane < columns[0] + 2 * panel)
        solved = [
            (over_rows(head, (first + c) % SUB), over_rows(turned, (first + c) % SUB))
            for c in range(panel)
        ]
        for i in range(own + 1, count):
            rows[i] = jnp.where(inside, 0.0, rows[i]) - tree_sum(
                [re * p + im * q for (re, im), (p, q) in zip(raw[i], solved)]
            )
    return final, final_turned, pivots


def modes_kernel(scale, slabs, x_ref, *refs):
    *given, modes_hbm, factor_hbm, basis_ref, points_ref, modes_ref, factor_ref, sems = refs
    width = basis_ref.shape[0]
    size = width // 2
    count = size // SUB
    if given:
        gram = given[0][...]
        mine = x_ref[...]
    else:
        gram = gram_rows([x_ref[i * width:(i + 1) * width] for i in range(slabs)], basis_ref)
        own = lax.axis_index("space")
        mine = x_ref[pl.ds(pl.multiple_of(own * width, width), width)]
    points = jnp.transpose(mine)
    points_ref[...] = jnp.concatenate([points, points], 1)
    gram = gram * scale
    rows, turned, pivots = eliminate([gram[i * SUB:(i + 1) * SUB] for i in range(count)], PANEL)
    shape = rows[0].shape
    sub = lax.broadcasted_iota(jnp.int32, shape, 0)
    lane = lax.broadcasted_iota(jnp.int32, shape, 1)
    pick = jnp.where(lane < size, 2 * lane, 2 * (lane - size) + 1)
    for i in range(count):
        own_rows = slice(i * SUB, (i + 1) * SUB)
        root = lax.rsqrt(pivots[i])
        diagonal = 2 * (i * SUB + sub)
        left = jnp.where(lane < diagonal, rows[i], (lane == diagonal).astype(jnp.float32))
        aside = jnp.where(lane < diagonal, turned[i], (lane == diagonal + 1).astype(jnp.float32))
        basis_ref[pl.ds(2 * i * SUB, SUB, stride=2), :] = left * root
        basis_ref[pl.ds(2 * i * SUB + 1, SUB, stride=2), :] = aside * root
        right = jnp.where(lane > diagonal + 1, rows[i], jnp.where(lane == diagonal, pivots[i], 0.0))
        parts = jnp.take_along_axis(right * root, pick, axis=1)
        factor_ref[0, own_rows, :] = parts[:, :size]
        factor_ref[1, own_rows, :] = parts[:, size:]
    copies = [pltpu.make_async_copy(factor_ref, factor_hbm, sems.at[0])]
    copies[0].start()
    basis = basis_ref[...]
    high = basis.astype(jnp.bfloat16)
    low = (basis - high.astype(jnp.float32)).astype(jnp.bfloat16)
    terms = jnp.concatenate([high, low], 1)
    each = modes_ref.shape[0] // PARTS
    for i in range(PARTS):
        part = slice(i * each, (i + 1) * each)
        modes_ref[part] = lax.dot_general(
            points_ref[part], terms, (((1,), (1,)), ((), ())),
            preferred_element_type=jnp.float32,
        )
        copies.append(pltpu.make_async_copy(modes_ref.at[part], modes_hbm.at[part], sems.at[1 + i]))
        copies[-1].start()
    for copy in copies:
        copy.wait()


def modes_and_factor(x, grams, width, slabs, scale):
    points = x.shape[1]
    size = width // 2
    return pl.pallas_call(
        functools.partial(modes_kernel, scale, slabs),
        out_shape=(
            jax.ShapeDtypeStruct((points, width), jnp.float32),
            jax.ShapeDtypeStruct((2, size, size), jnp.float32),
        ),
        in_specs=[pl.BlockSpec(memory_space=pltpu.VMEM)] * (1 + len(grams)),
        out_specs=(pl.BlockSpec(memory_space=pltpu.HBM),) * 2,
        scratch_shapes=[
            pltpu.VMEM((width, width), jnp.float32),
            pltpu.VMEM((points, 2 * width), jnp.bfloat16),
            pltpu.VMEM((points, width), jnp.float32),
            pltpu.VMEM((2, size, size), jnp.float32),
            pltpu.SemaphoreType.DMA((1 + PARTS,)),
        ],
        compiler_params=pltpu.CompilerParams(vmem_limit_bytes=8 * 2**20),
        name="factor_and_modes",
    )(x, *grams)


def local(slabs, snapshots, row_scales, block_offsets, freq_index):
    freqs = freq_index.shape[0]
    points = snapshots.shape[1]
    width = 2 * block_offsets.shape[0] * lax.axis_size("blk")
    copies = slabs if slabs <= FEW_SLABS else 1
    spectra = block_spectra(copies, snapshots, row_scales, block_offsets, freq_index)
    chunks = spectra.reshape(copies * freqs, -1, points)
    swap = functools.partial(lax.all_to_all, split_axis=0, concat_axis=0, tiled=True)
    if copies == slabs:
        x = swap(chunks, ("space", "blk")).reshape(-1, points)
        grams = []
    else:
        x = swap(chunks, "blk").reshape(-1, points)
        grams = [lax.psum(complex_gram(x), "space")]
    modes, factor = modes_and_factor(x, grams, width, slabs, 1.0 / (points * slabs))
    return modes[None], factor[None]


def solution(mesh):
    return jax.shard_map(
        functools.partial(local, mesh.shape["space"]),
        mesh=mesh,
        in_specs=(P("blk", "space"), P("blk"), P("blk"), P()),
        out_specs=(P("blk", "space", None), P("blk", None, None, None)),
        check_vma=False,
    )
```

```python
import functools
import math

import jax
import jax.numpy as jnp
from jax import lax
from jax.experimental import pallas as pl
from jax.experimental.pallas import tpu as pltpu
from jax.sharding import PartitionSpec as P

NFFT = 512
SUB = 8
PIECE = 256
PARTS = 4
FEW_SLABS = 2
SIN_COEFS = (
    0.9999999765895043,
    -0.1666664763439475,
    0.008332899819203531,
    -0.0001980089750772882,
    2.5904879854375602e-06,
)


def cos_of_phase(phase):
    folded = jnp.abs((phase & (NFFT - 1)) - NFFT // 2) - NFFT // 4
    x = folded.astype(jnp.float32) * (2.0 * math.pi / NFFT)
    square = x * x
    total = jnp.full_like(x, SIN_COEFS[-1])
    for coef in SIN_COEFS[-2::-1]:
        total = total * square + coef
    return total * x


def spectra_kernel(
    snap_hbm, scales_hbm, offsets_hbm, freq_hbm, out_ref,
    snap_ref, scales_ref, offsets_ref, freq_ref, coef_ref, small_sems, snap_sems,
):
    snaps = snap_ref.shape[0]
    blocks = offsets_ref.shape[0]
    rows = 2 * blocks
    freqs = freq_ref.shape[0]
    small = [
        pltpu.make_async_copy(src, dst, small_sems.at[i])
        for i, (src, dst) in enumerate(
            ((offsets_hbm, offsets_ref), (freq_hbm, freq_ref), (scales_hbm, scales_ref))
        )
    ]
    pieces = [slice(at, min(at + PIECE, snaps)) for at in range(0, snaps, PIECE)]
    large = [
        pltpu.make_async_copy(snap_hbm.at[piece], snap_ref.at[piece], snap_sems.at[i])
        for i, piece in enumerate(pieces)
    ]
    for copy in small + large:
        copy.start()
    row = lax.broadcasted_iota(jnp.int32, (rows, snaps), 0)
    time = lax.broadcasted_iota(jnp.int32, (rows, snaps), 1)
    for copy in small:
        copy.wait()
    start = jnp.zeros((rows, snaps), jnp.int32)
    for b in range(blocks):
        start = jnp.where(row // 2 == b, offsets_ref[b], start)
    shifted = time - start
    hann = 0.5 - 0.5 * cos_of_phase(shifted)
    inside = (shifted >= 0) & (shifted < NFFT)
    scales = jnp.broadcast_to(scales_ref[...].reshape(1, snaps), (rows, snaps))
    weight = jnp.where(inside, hann * scales * (1.0 / math.sqrt(NFFT)), 0.0)
    base = shifted[:, :NFFT].astype(jnp.float32)
    quarter = (row[:, :NFFT] % 2) * (NFFT // 4)
    repeats = -(-snaps // NFFT)

    def rows_of(f):
        freq = freq_ref[f].astype(jnp.float32)
        table = cos_of_phase((base * freq).astype(jnp.int32) + quarter)
        return jnp.concatenate([table] * repeats, 1)[:, :snaps] * weight

    for f in range(0, freqs, 2):
        pair = jnp.concatenate([rows_of(f), rows_of(f + 1)], 0)
        coef_ref[f * rows:(f + 2) * rows, :] = pair.astype(jnp.bfloat16)
    for copy in large:
        copy.wait()
    total = jnp.dot(coef_ref[...], snap_ref[...], preferred_element_type=jnp.float32)
    result = total.astype(jnp.bfloat16)
    for copy in range(out_ref.shape[0]):
        out_ref[copy] = result


def block_spectra(copies, snapshots, row_scales, block_offsets, freq_index):
    snaps, points = snapshots.shape
    rows = 2 * block_offsets.shape[0] * freq_index.shape[0]
    pieces = -(-snaps // PIECE)
    return pl.pallas_call(
        spectra_kernel,
        out_shape=jax.ShapeDtypeStruct((copies, rows, points), jnp.bfloat16),
        in_specs=[pl.BlockSpec(memory_space=pltpu.HBM)] * 4,
        out_specs=pl.BlockSpec(memory_space=pltpu.VMEM),
        scratch_shapes=[
            pltpu.VMEM((snaps, points), jnp.bfloat16),
            pltpu.VMEM((snaps,), jnp.float32),
            pltpu.SMEM(block_offsets.shape, jnp.int32),
            pltpu.SMEM(freq_index.shape, jnp.int32),
            pltpu.VMEM((rows, snaps), jnp.bfloat16),
            pltpu.SemaphoreType.DMA((3,)),
            pltpu.SemaphoreType.DMA((pieces,)),
        ],
        compiler_params=pltpu.CompilerParams(vmem_limit_bytes=8 * 2**20),
        name="spectra",
    )(*(
        pltpu.with_memory_space_constraint(x, pltpu.HBM)
        for x in (snapshots, row_scales, block_offsets, freq_index)
    ))


def rotated(x, lane):
    axis = x.ndim - 1
    width = x.shape[axis]
    after = pltpu.roll(x, width - 1, axis)
    before = pltpu.roll(x, 1, axis)
    return jnp.where(lane % 2 == 0, -after, before)


def gram_rows(slabs, full_ref):
    width = full_ref.shape[0]
    full_ref[...] = sum(
        lax.dot_general(x, x, (((1,), (1,)), ((), ())), preferred_element_type=jnp.float32)
        for x in slabs
    )
    even = full_ref[pl.ds(0, width // 2, stride=2), :]
    odd = full_ref[pl.ds(1, width // 2, stride=2), :]
    lane = lax.broadcasted_iota(jnp.int32, odd.shape, 1)
    return even - rotated(odd, lane)


def gram_kernel(x_ref, out_ref, full_ref):
    out_ref[...] = gram_rows([x_ref[...]], full_ref)


def complex_gram(x):
    width = x.shape[0]
    return pl.pallas_call(
        gram_kernel,
        out_shape=jax.ShapeDtypeStruct((width // 2, width), jnp.float32),
        in_specs=[pl.BlockSpec(memory_space=pltpu.VMEM)],
        out_specs=pl.BlockSpec(memory_space=pltpu.VMEM),
        scratch_shapes=[pltpu.VMEM((width, width), jnp.float32)],
        compiler_params=pltpu.CompilerParams(vmem_limit_bytes=4 * 2**20),
        name="gram",
    )(x)


def tree_sum(terms):
    while len(terms) > 1:
        terms = [sum(terms[i:i + 2]) for i in range(0, len(terms), 2)]
    return terms[0]


def times(a, b):
    return a[0] * b[0] - a[1] * b[1], a[0] * b[1] + a[1] * b[0]


def conj_times(a, b):
    return a[0] * b[0] + a[1] * b[1], a[0] * b[1] - a[1] * b[0]


def eliminate(rows):
    count = len(rows)
    shape = rows[0].shape
    sub = lax.broadcasted_iota(jnp.int32, shape, 0)
    lane = lax.broadcasted_iota(jnp.int32, shape, 1)

    def over_lanes(x, at):
        return jnp.broadcast_to(x[:, at:at + 1], shape)

    def over_rows(x, at):
        return jnp.broadcast_to(x[at:at + 1, :], shape)

    def entry(column, at):
        return over_rows(column[0], at), over_rows(column[1], at)

    rows = list(rows)
    final, final_turned, pivots = [], [], []
    for own in range(count):
        head, turned = rows[own], rotated(rows[own], lane)
        keep, keep_turned, keep_pivot = head, turned, jnp.ones(shape, jnp.float32)
        columns = [2 * (own * SUB + c) for c in range(SUB)]
        raw = {
            i: [(over_lanes(rows[i], at), over_lanes(rows[i], at + 1)) for at in columns]
            for i in range(own, count)
        }
        here = raw[own]
        ahead = over_rows(here[0][0], 0), over_rows(here[1][0], 1), entry(here[1], 0)
        for pair in range(0, SUB, 2):
            first, second, u = ahead
            square = u[0] * u[0] + u[1] * u[1]
            inverse = pl.reciprocal(first, approx=True)
            inverses = inverse, first * pl.reciprocal(first * second - square, approx=True)
            values = first, second - square * inverse
            uppers = [{c: entry(here[c], pair) for c in range(pair + 1, SUB)}, {}]
            for c in range(pair + 2, SUB):
                old, loss = entry(here[c], pair + 1), conj_times(u, uppers[0][c])
                uppers[1][c] = old[0] - loss[0] * inverse, old[1] - loss[1] * inverse
            if pair + 2 < SUB:
                one, two = pair + 2, pair + 3
                parts = [
                    (conj_times(up[one], up[one])[0], conj_times(up[two], up[two])[0], conj_times(up[one], up[two]))
                    for up in uppers
                ]
                next_u = entry(here[two], one)
                (a1, a2, au), (b1, b2, bu) = parts
                ahead = (
                    (over_rows(here[one][0], one) - a1 * inverse) - b1 * inverses[1],
                    (over_rows(here[two][0], two) - a2 * inverse) - b2 * inverses[1],
                    tuple(
                        (next_u[k] - au[k] * inverse) - bu[k] * inverses[1] for k in range(2)
                    ),
                )
            for c in (pair, pair + 1):
                here_row = sub == c
                m_re = jnp.where(here_row, -1.0, here[c][0]) * inverses[c - pair]
                m_im = jnp.where(here_row, 0.0, here[c][1]) * inverses[c - pair]
                keep = jnp.where(here_row, head, keep)
                keep_turned = jnp.where(here_row, turned, keep_turned)
                keep_pivot = jnp.where(here_row, values[c - pair], keep_pivot)
                for later, (u_re, u_im) in uppers[c - pair].items():
                    re, im = here[later]
                    here[later] = (
                        jnp.where(here_row, 0.0, re) - m_re * u_re + m_im * u_im,
                        jnp.where(here_row, 0.0, im) - m_re * u_im - m_im * u_re,
                    )
                on_re, on_im = lane == columns[c], lane == columns[c] + 1
                on_pair = on_re | on_im
                p = jnp.where(on_pair, on_re.astype(jnp.float32), over_rows(head, c))
                q = jnp.where(on_pair, on_im.astype(jnp.float32), over_rows(turned, c))
                cleared = here_row | on_pair
                head = jnp.where(cleared, 0.0, head) - (m_re * p + m_im * q)
                turned = jnp.where(cleared, 0.0, turned) - (m_re * q - m_im * p)
        final.append(keep)
        final_turned.append(keep_turned)
        pivots.append(keep_pivot)
        inside = (lane >= columns[0]) & (lane < columns[0] + 2 * SUB)
        solved = [(over_rows(head, c), over_rows(turned, c)) for c in range(SUB)]
        for i in range(own + 1, count):
            rows[i] = jnp.where(inside, 0.0, rows[i]) - tree_sum(
                [re * p + im * q for (re, im), (p, q) in zip(raw[i], solved)]
            )
    return final, final_turned, pivots


def unit_diagonal(rows):
    shape = rows[0].shape
    sub = lax.broadcasted_iota(jnp.int32, shape, 0)
    lane = lax.broadcasted_iota(jnp.int32, shape, 1)
    diagonals = [jnp.where(lane == 2 * (i * SUB + sub), row, 0.0) for i, row in enumerate(rows)]
    across = jnp.sum(tree_sum(diagonals), axis=0, keepdims=True)
    across = jnp.broadcast_to(across, shape)
    across = across + pltpu.roll(across, 1, 1)
    root = lax.rsqrt(across)
    scaled = [
        row * lax.rsqrt(jnp.sum(diagonal, axis=1, keepdims=True)) * root
        for row, diagonal in zip(rows, diagonals)
    ]
    return scaled, root, across * root


def modes_kernel(scale, slabs, x_ref, *refs):
    *given, modes_hbm, factor_hbm, basis_ref, points_ref, modes_ref, factor_ref, sems = refs
    width = basis_ref.shape[0]
    size = width // 2
    count = size // SUB
    if given:
        gram = given[0][...]
        mine = x_ref[...]
    else:
        gram = gram_rows([x_ref[i * width:(i + 1) * width] for i in range(slabs)], basis_ref)
        own = lax.axis_index("space")
        mine = x_ref[pl.ds(pl.multiple_of(own * width, width), width)]
    points = jnp.transpose(mine)
    points_ref[...] = jnp.concatenate([points, points], 1)
    rows, shrink, grow = unit_diagonal([gram[i * SUB:(i + 1) * SUB] for i in range(count)])
    shrink, grow = shrink * (1.0 / math.sqrt(scale)), grow * math.sqrt(scale)
    rows, turned, pivots = eliminate(rows)
    shape = rows[0].shape
    sub = lax.broadcasted_iota(jnp.int32, shape, 0)
    lane = lax.broadcasted_iota(jnp.int32, shape, 1)
    pick = jnp.where(lane < size, 2 * lane, 2 * (lane - size) + 1)
    for i in range(count):
        own_rows = slice(i * SUB, (i + 1) * SUB)
        root = lax.rsqrt(pivots[i])
        diagonal = 2 * (i * SUB + sub)
        left = jnp.where(lane < diagonal, rows[i], (lane == diagonal).astype(jnp.float32))
        aside = jnp.where(lane < diagonal, turned[i], (lane == diagonal + 1).astype(jnp.float32))
        basis_ref[pl.ds(2 * i * SUB, SUB, stride=2), :] = left * (root * shrink)
        basis_ref[pl.ds(2 * i * SUB + 1, SUB, stride=2), :] = aside * (root * shrink)
        right = jnp.where(lane > diagonal + 1, rows[i], jnp.where(lane == diagonal, pivots[i], 0.0))
        parts = jnp.take_along_axis(right * (root * grow), pick, axis=1)
        factor_ref[0, own_rows, :] = parts[:, :size]
        factor_ref[1, own_rows, :] = parts[:, size:]
    copies = [pltpu.make_async_copy(factor_ref, factor_hbm, sems.at[0])]
    copies[0].start()
    basis = basis_ref[...]
    high = basis.astype(jnp.bfloat16)
    low = (basis - high.astype(jnp.float32)).astype(jnp.bfloat16)
    terms = jnp.concatenate([high, low], 1)
    each = modes_ref.shape[0] // PARTS
    for i in range(PARTS):
        part = slice(i * each, (i + 1) * each)
        modes_ref[part] = lax.dot_general(
            points_ref[part], terms, (((1,), (1,)), ((), ())),
            preferred_element_type=jnp.float32,
        )
        copies.append(pltpu.make_async_copy(modes_ref.at[part], modes_hbm.at[part], sems.at[1 + i]))
        copies[-1].start()
    for copy in copies:
        copy.wait()


def modes_and_factor(x, grams, width, slabs, scale):
    points = x.shape[1]
    size = width // 2
    return pl.pallas_call(
        functools.partial(modes_kernel, scale, slabs),
        out_shape=(
            jax.ShapeDtypeStruct((points, width), jnp.float32),
            jax.ShapeDtypeStruct((2, size, size), jnp.float32),
        ),
        in_specs=[pl.BlockSpec(memory_space=pltpu.VMEM)] * (1 + len(grams)),
        out_specs=(pl.BlockSpec(memory_space=pltpu.HBM),) * 2,
        scratch_shapes=[
            pltpu.VMEM((width, width), jnp.float32),
            pltpu.VMEM((points, 2 * width), jnp.bfloat16),
            pltpu.VMEM((points, width), jnp.float32),
            pltpu.VMEM((2, size, size), jnp.float32),
            pltpu.SemaphoreType.DMA((1 + PARTS,)),
        ],
        compiler_params=pltpu.CompilerParams(vmem_limit_bytes=8 * 2**20),
        name="factor_and_modes",
    )(x, *grams)


def local(slabs, snapshots, row_scales, block_offsets, freq_index):
    freqs = freq_index.shape[0]
    points = snapshots.shape[1]
    width = 2 * block_offsets.shape[0] * lax.axis_size("blk")
    copies = slabs if slabs <= FEW_SLABS else 1
    spectra = block_spectra(copies, snapshots, row_scales, block_offsets, freq_index)
    chunks = spectra.reshape(copies * freqs, -1, points)
    swap = functools.partial(lax.all_to_all, split_axis=0, concat_axis=0, tiled=True)
    if copies == slabs:
        x = swap(chunks, ("space", "blk")).reshape(-1, points)
        grams = []
    else:
        x = swap(chunks, "blk").reshape(-1, points)
        grams = [lax.psum(complex_gram(x), "space")]
    modes, factor = modes_and_factor(x, grams, width, slabs, 1.0 / (points * slabs))
    return modes[None], factor[None]


def solution(mesh):
    return jax.shard_map(
        functools.partial(local, mesh.shape["space"]),
        mesh=mesh,
        in_specs=(P("blk", "space"), P("blk"), P("blk"), P()),
        out_specs=(P("blk", "space", None), P("blk", None, None, None)),
        check_vma=False,
    )
```

```python
import functools
import math

import jax
import jax.numpy as jnp
from jax import lax
from jax.experimental import pallas as pl
from jax.experimental.pallas import tpu as pltpu
from jax.sharding import PartitionSpec as P

NFFT = 512
SUB = 8
PIECE = 256
PARTS = 4
FEW_SLABS = 2
SIN_COEFS = (
    0.9999999765895043,
    -0.1666664763439475,
    0.008332899819203531,
    -0.0001980089750772882,
    2.5904879854375602e-06,
)


def cos_of_phase(phase):
    folded = jnp.abs((phase & (NFFT - 1)) - NFFT // 2) - NFFT // 4
    x = folded.astype(jnp.float32) * (2.0 * math.pi / NFFT)
    square = x * x
    total = jnp.full_like(x, SIN_COEFS[-1])
    for coef in SIN_COEFS[-2::-1]:
        total = total * square + coef
    return total * x


def spectra_kernel(
    snap_hbm, scales_hbm, offsets_hbm, freq_hbm, out_ref,
    snap_ref, scales_ref, offsets_ref, freq_ref, coef_ref, small_sems, snap_sems,
):
    snaps = snap_ref.shape[0]
    blocks = offsets_ref.shape[0]
    rows = 2 * blocks
    freqs = freq_ref.shape[0]
    small = [
        pltpu.make_async_copy(src, dst, small_sems.at[i])
        for i, (src, dst) in enumerate(
            ((offsets_hbm, offsets_ref), (freq_hbm, freq_ref), (scales_hbm, scales_ref))
        )
    ]
    pieces = [slice(at, min(at + PIECE, snaps)) for at in range(0, snaps, PIECE)]
    large = [
        pltpu.make_async_copy(snap_hbm.at[piece], snap_ref.at[piece], snap_sems.at[i])
        for i, piece in enumerate(pieces)
    ]
    for copy in small + large:
        copy.start()
    row = lax.broadcasted_iota(jnp.int32, (rows, snaps), 0)
    time = lax.broadcasted_iota(jnp.int32, (rows, snaps), 1)
    for copy in small:
        copy.wait()
    start = jnp.zeros((rows, snaps), jnp.int32)
    for b in range(blocks):
        start = jnp.where(row // 2 == b, offsets_ref[b], start)
    shifted = time - start
    hann = 0.5 - 0.5 * cos_of_phase(shifted)
    inside = (shifted >= 0) & (shifted < NFFT)
    scales = jnp.broadcast_to(scales_ref[...].reshape(1, snaps), (rows, snaps))
    weight = jnp.where(inside, hann * scales * (1.0 / math.sqrt(NFFT)), 0.0)
    base = shifted[:, :NFFT].astype(jnp.float32)
    quarter = (row[:, :NFFT] % 2) * (NFFT // 4)
    repeats = -(-snaps // NFFT)

    def rows_of(f):
        freq = freq_ref[f].astype(jnp.float32)
        table = cos_of_phase((base * freq).astype(jnp.int32) + quarter)
        return jnp.concatenate([table] * repeats, 1)[:, :snaps] * weight

    for f in range(0, freqs, 2):
        pair = jnp.concatenate([rows_of(f), rows_of(f + 1)], 0)
        coef_ref[f * rows:(f + 2) * rows, :] = pair.astype(jnp.bfloat16)
    for copy in large:
        copy.wait()
    total = jnp.dot(coef_ref[...], snap_ref[...], preferred_element_type=jnp.float32)
    result = total.astype(jnp.bfloat16)
    for copy in range(out_ref.shape[0]):
        out_ref[copy] = result


def block_spectra(copies, snapshots, row_scales, block_offsets, freq_index):
    snaps, points = snapshots.shape
    rows = 2 * block_offsets.shape[0] * freq_index.shape[0]
    pieces = -(-snaps // PIECE)
    return pl.pallas_call(
        spectra_kernel,
        out_shape=jax.ShapeDtypeStruct((copies, rows, points), jnp.bfloat16),
        in_specs=[pl.BlockSpec(memory_space=pltpu.HBM)] * 4,
        out_specs=pl.BlockSpec(memory_space=pltpu.VMEM),
        scratch_shapes=[
            pltpu.VMEM((snaps, points), jnp.bfloat16),
            pltpu.VMEM((snaps,), jnp.float32),
            pltpu.SMEM(block_offsets.shape, jnp.int32),
            pltpu.SMEM(freq_index.shape, jnp.int32),
            pltpu.VMEM((rows, snaps), jnp.bfloat16),
            pltpu.SemaphoreType.DMA((3,)),
            pltpu.SemaphoreType.DMA((pieces,)),
        ],
        compiler_params=pltpu.CompilerParams(vmem_limit_bytes=8 * 2**20),
        name="spectra",
    )(*(
        pltpu.with_memory_space_constraint(x, pltpu.HBM)
        for x in (snapshots, row_scales, block_offsets, freq_index)
    ))


def rotated(x, lane):
    axis = x.ndim - 1
    width = x.shape[axis]
    after = pltpu.roll(x, width - 1, axis)
    before = pltpu.roll(x, 1, axis)
    return jnp.where(lane % 2 == 0, -after, before)


def gram_rows(slabs, full_ref):
    width = full_ref.shape[0]
    full_ref[...] = sum(
        lax.dot_general(x, x, (((1,), (1,)), ((), ())), preferred_element_type=jnp.float32)
        for x in slabs
    )
    even = full_ref[pl.ds(0, width // 2, stride=2), :]
    odd = full_ref[pl.ds(1, width // 2, stride=2), :]
    lane = lax.broadcasted_iota(jnp.int32, odd.shape, 1)
    return even - rotated(odd, lane)


def gram_kernel(x_ref, out_ref, full_ref):
    out_ref[...] = gram_rows([x_ref[...]], full_ref)


def complex_gram(x):
    width = x.shape[0]
    return pl.pallas_call(
        gram_kernel,
        out_shape=jax.ShapeDtypeStruct((width // 2, width), jnp.float32),
        in_specs=[pl.BlockSpec(memory_space=pltpu.VMEM)],
        out_specs=pl.BlockSpec(memory_space=pltpu.VMEM),
        scratch_shapes=[pltpu.VMEM((width, width), jnp.float32)],
        compiler_params=pltpu.CompilerParams(vmem_limit_bytes=4 * 2**20),
        name="gram",
    )(x)


def tree_sum(terms):
    while len(terms) > 1:
        terms = [sum(terms[i:i + 2]) for i in range(0, len(terms), 2)]
    return terms[0]


def eliminate(rows, solved_ref):
    count = len(rows)
    shape = rows[0].shape
    sub = lax.broadcasted_iota(jnp.int32, shape, 0)
    lane = lax.broadcasted_iota(jnp.int32, shape, 1)

    def over_lanes(x, at):
        return jnp.broadcast_to(x[:, at:at + 1], shape)

    def over_rows(x, at):
        return jnp.broadcast_to(x[at:at + 1, :], shape)

    rows = list(rows)
    final, final_turned, pivots = [], [], []
    solved_ref[...] = jnp.zeros_like(solved_ref)
    for own in range(count):
        head, turned = rows[own], rotated(rows[own], lane)
        keep, keep_turned, keep_pivot = head, turned, jnp.ones(shape, jnp.float32)
        columns = [2 * (own * SUB + c) for c in range(SUB)]
        raw = {
            i: [(over_lanes(rows[i], at), over_lanes(rows[i], at + 1)) for at in columns]
            for i in range(own, min(own + 2, count))
        }
        here = raw[own]
        pivot = over_rows(here[0][0], 0)
        for c in range(SUB):
            here_row = sub == c
            inverse = pl.reciprocal(pivot, approx=True)
            m_re = jnp.where(here_row, -1.0, here[c][0]) * inverse
            m_im = jnp.where(here_row, 0.0, here[c][1]) * inverse
            keep = jnp.where(here_row, head, keep)
            keep_turned = jnp.where(here_row, turned, keep_turned)
            keep_pivot = jnp.where(here_row, pivot, keep_pivot)
            for later in range(c + 1, SUB):
                re, im = here[later]
                u_re, u_im = over_rows(re, c), over_rows(im, c)
                if later == c + 1:
                    loss = (u_re * inverse) * u_re + (u_im * inverse) * u_im
                    pivot = over_rows(re, c + 1) - loss
                here[later] = (
                    jnp.where(here_row, 0.0, re) - m_re * u_re + m_im * u_im,
                    jnp.where(here_row, 0.0, im) - m_re * u_im - m_im * u_re,
                )
            on_re, on_im = lane == columns[c], lane == columns[c] + 1
            on_pair = on_re | on_im
            p = jnp.where(on_pair, on_re.astype(jnp.float32), over_rows(head, c))
            q = jnp.where(on_pair, on_im.astype(jnp.float32), over_rows(turned, c))
            cleared = here_row | on_pair
            head = jnp.where(cleared, 0.0, head) - (m_re * p + m_im * q)
            turned = jnp.where(cleared, 0.0, turned) - (m_re * q - m_im * p)
        final.append(keep)
        final_turned.append(keep_turned)
        pivots.append(keep_pivot)
        if own + 1 == count:
            break
        inside = (lane >= columns[0]) & (lane < columns[0] + 2 * SUB)
        solved = [(over_rows(head, c), over_rows(turned, c)) for c in range(SUB)]
        rows[own + 1] = jnp.where(inside, 0.0, rows[own + 1]) - tree_sum(
            [re * p + im * q for (re, im), (p, q) in zip(raw[own + 1], solved)]
        )
        far = range(own + 2, count)
        if far:
            solved_ref[pl.ds(columns[0], SUB, stride=2), :] = head
            solved_ref[pl.ds(columns[0] + 1, SUB, stride=2), :] = turned
            losses = jnp.dot(
                jnp.concatenate([jnp.where(inside, rows[i], 0.0) for i in far], 0), solved_ref[...],
                precision=lax.Precision.HIGHEST, preferred_element_type=jnp.float32,
            )
            for at, i in enumerate(far):
                loss = losses[at * SUB:(at + 1) * SUB]
                rows[i] = jnp.where(inside, 0.0, rows[i]) - loss
    return final, final_turned, pivots


def modes_kernel(scale, slabs, x_ref, *refs):
    *given, modes_hbm, factor_hbm, basis_ref, solved_ref, points_ref, modes_ref, factor_ref, sems = refs
    width = basis_ref.shape[0]
    size = width // 2
    count = size // SUB
    if given:
        gram = given[0][...]
        mine = x_ref[...]
    else:
        gram = gram_rows([x_ref[i * width:(i + 1) * width] for i in range(slabs)], basis_ref)
        own = lax.axis_index("space")
        mine = x_ref[pl.ds(pl.multiple_of(own * width, width), width)]
    points = jnp.transpose(mine)
    points_ref[...] = jnp.concatenate([points, points], 1)
    gram = gram * scale
    rows, turned, pivots = eliminate([gram[i * SUB:(i + 1) * SUB] for i in range(count)], solved_ref)
    shape = rows[0].shape
    sub = lax.broadcasted_iota(jnp.int32, shape, 0)
    lane = lax.broadcasted_iota(jnp.int32, shape, 1)
    pick = jnp.where(lane < size, 2 * lane, 2 * (lane - size) + 1)
    for i in range(count):
        own_rows = slice(i * SUB, (i + 1) * SUB)
        root = lax.rsqrt(pivots[i])
        diagonal = 2 * (i * SUB + sub)
        left = jnp.where(lane < diagonal, rows[i], (lane == diagonal).astype(jnp.float32))
        aside = jnp.where(lane < diagonal, turned[i], (lane == diagonal + 1).astype(jnp.float32))
        basis_ref[pl.ds(2 * i * SUB, SUB, stride=2), :] = left * root
        basis_ref[pl.ds(2 * i * SUB + 1, SUB, stride=2), :] = aside * root
        right = jnp.where(lane > diagonal + 1, rows[i], jnp.where(lane == diagonal, pivots[i], 0.0))
        parts = jnp.take_along_axis(right * root, pick, axis=1)
        factor_ref[0, own_rows, :] = parts[:, :size]
        factor_ref[1, own_rows, :] = parts[:, size:]
    copies = [pltpu.make_async_copy(factor_ref, factor_hbm, sems.at[0])]
    copies[0].start()
    basis = basis_ref[...]
    high = basis.astype(jnp.bfloat16)
    low = (basis - high.astype(jnp.float32)).astype(jnp.bfloat16)
    terms = jnp.concatenate([high, low], 1)
    each = modes_ref.shape[0] // PARTS
    for i in range(PARTS):
        part = slice(i * each, (i + 1) * each)
        modes_ref[part] = lax.dot_general(
            points_ref[part], terms, (((1,), (1,)), ((), ())),
            preferred_element_type=jnp.float32,
        )
        copies.append(pltpu.make_async_copy(modes_ref.at[part], modes_hbm.at[part], sems.at[1 + i]))
        copies[-1].start()
    for copy in copies:
        copy.wait()


def modes_and_factor(x, grams, width, slabs, scale):
    points = x.shape[1]
    size = width // 2
    return pl.pallas_call(
        functools.partial(modes_kernel, scale, slabs),
        out_shape=(
            jax.ShapeDtypeStruct((points, width), jnp.float32),
            jax.ShapeDtypeStruct((2, size, size), jnp.float32),
        ),
        in_specs=[pl.BlockSpec(memory_space=pltpu.VMEM)] * (1 + len(grams)),
        out_specs=(pl.BlockSpec(memory_space=pltpu.HBM),) * 2,
        scratch_shapes=[
            pltpu.VMEM((width, width), jnp.float32),
            pltpu.VMEM((width, width), jnp.float32),
            pltpu.VMEM((points, 2 * width), jnp.bfloat16),
            pltpu.VMEM((points, width), jnp.float32),
            pltpu.VMEM((2, size, size), jnp.float32),
            pltpu.SemaphoreType.DMA((1 + PARTS,)),
        ],
        compiler_params=pltpu.CompilerParams(vmem_limit_bytes=8 * 2**20),
        name="factor_and_modes",
    )(x, *grams)


def local(slabs, snapshots, row_scales, block_offsets, freq_index):
    freqs = freq_index.shape[0]
    points = snapshots.shape[1]
    width = 2 * block_offsets.shape[0] * lax.axis_size("blk")
    copies = slabs if slabs <= FEW_SLABS else 1
    spectra = block_spectra(copies, snapshots, row_scales, block_offsets, freq_index)
    chunks = spectra.reshape(copies * freqs, -1, points)
    swap = functools.partial(lax.all_to_all, split_axis=0, concat_axis=0, tiled=True)
    if copies == slabs:
        x = swap(chunks, ("space", "blk")).reshape(-1, points)
        grams = []
    else:
        x = swap(chunks, "blk").reshape(-1, points)
        grams = [lax.psum(complex_gram(x), "space")]
    modes, factor = modes_and_factor(x, grams, width, slabs, 1.0 / (points * slabs))
    return modes[None], factor[None]


def solution(mesh):
    return jax.shard_map(
        functools.partial(local, mesh.shape["space"]),
        mesh=mesh,
        in_specs=(P("blk", "space"), P("blk"), P("blk"), P()),
        out_specs=(P("blk", "space", None), P("blk", None, None, None)),
        check_vma=False,
    )
```

```python
import functools
import math

import jax
import jax.numpy as jnp
from jax import lax
from jax.experimental import pallas as pl
from jax.experimental.pallas import tpu as pltpu
from jax.sharding import PartitionSpec as P

NFFT = 512
SUB = 8
PIECE = 256
PARTS = 4
FEW_SLABS = 2
SIN_COEFS = (
    0.9999999765895043,
    -0.1666664763439475,
    0.008332899819203531,
    -0.0001980089750772882,
    2.5904879854375602e-06,
)


def cos_of_phase(phase):
    folded = jnp.abs((phase & (NFFT - 1)) - NFFT // 2) - NFFT // 4
    x = folded.astype(jnp.float32) * (2.0 * math.pi / NFFT)
    square = x * x
    total = jnp.full_like(x, SIN_COEFS[-1])
    for coef in SIN_COEFS[-2::-1]:
        total = total * square + coef
    return total * x


def spectra_kernel(
    snap_hbm, scales_hbm, offsets_hbm, freq_hbm, out_ref,
    snap_ref, scales_ref, offsets_ref, freq_ref, coef_ref, small_sems, snap_sems,
):
    snaps = snap_ref.shape[0]
    blocks = offsets_ref.shape[0]
    rows = 2 * blocks
    freqs = freq_ref.shape[0]
    small = [
        pltpu.make_async_copy(src, dst, small_sems.at[i])
        for i, (src, dst) in enumerate(
            ((offsets_hbm, offsets_ref), (freq_hbm, freq_ref), (scales_hbm, scales_ref))
        )
    ]
    pieces = [slice(at, min(at + PIECE, snaps)) for at in range(0, snaps, PIECE)]
    large = [
        pltpu.make_async_copy(snap_hbm.at[piece], snap_ref.at[piece], snap_sems.at[i])
        for i, piece in enumerate(pieces)
    ]
    for copy in small + large:
        copy.start()
    row = lax.broadcasted_iota(jnp.int32, (rows, snaps), 0)
    time = lax.broadcasted_iota(jnp.int32, (rows, snaps), 1)
    for copy in small:
        copy.wait()
    start = jnp.zeros((rows, snaps), jnp.int32)
    for b in range(blocks):
        start = jnp.where(row // 2 == b, offsets_ref[b], start)
    shifted = time - start
    hann = 0.5 - 0.5 * cos_of_phase(shifted)
    inside = (shifted >= 0) & (shifted < NFFT)
    scales = jnp.broadcast_to(scales_ref[...].reshape(1, snaps), (rows, snaps))
    weight = jnp.where(inside, hann * scales * (1.0 / math.sqrt(NFFT)), 0.0)
    base = shifted[:, :NFFT].astype(jnp.float32)
    quarter = (row[:, :NFFT] % 2) * (NFFT // 4)
    repeats = -(-snaps // NFFT)

    def rows_of(f):
        freq = freq_ref[f].astype(jnp.float32)
        table = cos_of_phase((base * freq).astype(jnp.int32) + quarter)
        return jnp.concatenate([table] * repeats, 1)[:, :snaps] * weight

    for f in range(0, freqs, 2):
        pair = jnp.concatenate([rows_of(f), rows_of(f + 1)], 0)
        coef_ref[f * rows:(f + 2) * rows, :] = pair.astype(jnp.bfloat16)
    for copy in large:
        copy.wait()
    total = jnp.dot(coef_ref[...], snap_ref[...], preferred_element_type=jnp.float32)
    result = total.astype(jnp.bfloat16)
    for copy in range(out_ref.shape[0]):
        out_ref[copy] = result


def block_spectra(copies, snapshots, row_scales, block_offsets, freq_index):
    snaps, points = snapshots.shape
    rows = 2 * block_offsets.shape[0] * freq_index.shape[0]
    pieces = -(-snaps // PIECE)
    return pl.pallas_call(
        spectra_kernel,
        out_shape=jax.ShapeDtypeStruct((copies, rows, points), jnp.bfloat16),
        in_specs=[pl.BlockSpec(memory_space=pltpu.HBM)] * 4,
        out_specs=pl.BlockSpec(memory_space=pltpu.VMEM),
        scratch_shapes=[
            pltpu.VMEM((snaps, points), jnp.bfloat16),
            pltpu.VMEM((snaps,), jnp.float32),
            pltpu.SMEM(block_offsets.shape, jnp.int32),
            pltpu.SMEM(freq_index.shape, jnp.int32),
            pltpu.VMEM((rows, snaps), jnp.bfloat16),
            pltpu.SemaphoreType.DMA((3,)),
            pltpu.SemaphoreType.DMA((pieces,)),
        ],
        compiler_params=pltpu.CompilerParams(vmem_limit_bytes=8 * 2**20),
        name="spectra",
    )(*(
        pltpu.with_memory_space_constraint(x, pltpu.HBM)
        for x in (snapshots, row_scales, block_offsets, freq_index)
    ))


def rotated(x, lane):
    axis = x.ndim - 1
    width = x.shape[axis]
    after = pltpu.roll(x, width - 1, axis)
    before = pltpu.roll(x, 1, axis)
    return jnp.where(lane % 2 == 0, -after, before)


def gram_rows(slabs, full_ref):
    width = full_ref.shape[0]
    full_ref[...] = sum(
        lax.dot_general(x, x, (((1,), (1,)), ((), ())), preferred_element_type=jnp.float32)
        for x in slabs
    )
    even = full_ref[pl.ds(0, width // 2, stride=2), :]
    odd = full_ref[pl.ds(1, width // 2, stride=2), :]
    lane = lax.broadcasted_iota(jnp.int32, odd.shape, 1)
    return even - rotated(odd, lane)


def gram_kernel(x_ref, out_ref, full_ref):
    out_ref[...] = gram_rows([x_ref[...]], full_ref)


def complex_gram(x):
    width = x.shape[0]
    return pl.pallas_call(
        gram_kernel,
        out_shape=jax.ShapeDtypeStruct((width // 2, width), jnp.float32),
        in_specs=[pl.BlockSpec(memory_space=pltpu.VMEM)],
        out_specs=pl.BlockSpec(memory_space=pltpu.VMEM),
        scratch_shapes=[pltpu.VMEM((width, width), jnp.float32)],
        compiler_params=pltpu.CompilerParams(vmem_limit_bytes=4 * 2**20),
        name="gram",
    )(x)


def tree_sum(terms):
    while len(terms) > 1:
        terms = [sum(terms[i:i + 2]) for i in range(0, len(terms), 2)]
    return terms[0]


def eliminate(rows, solved_ref, step_ref):
    count = len(rows)
    shape = rows[0].shape
    sub = lax.broadcasted_iota(jnp.int32, shape, 0)
    lane = lax.broadcasted_iota(jnp.int32, shape, 1)

    def over_lanes(x, at):
        return jnp.broadcast_to(x[:, at:at + 1], shape)

    def over_rows(x, at):
        return jnp.broadcast_to(x[at:at + 1, :], shape)

    def row_of(ref, *at):
        return ref[(*at[:-1], pl.ds(at[-1], SUB, stride=0), slice(None))]

    rows = list(rows)
    final, final_turned, pivots = [], [], []
    for own in range(count):
        head, turned = rows[own], rotated(rows[own], lane)
        keep, keep_turned, keep_pivot = head, turned, jnp.ones(shape, jnp.float32)
        columns = [2 * (own * SUB + c) for c in range(SUB)]
        raw = {
            i: [(over_lanes(rows[i], at), over_lanes(rows[i], at + 1)) for at in columns]
            for i in range(own, min(own + 2, count))
        }
        here = raw[own]
        pivot = over_rows(here[0][0], 0)
        for c in range(SUB):
            here_row = sub == c
            inverse = pl.reciprocal(pivot, approx=True)
            m_re = jnp.where(here_row, -1.0, here[c][0]) * inverse
            m_im = jnp.where(here_row, 0.0, here[c][1]) * inverse
            keep = jnp.where(here_row, head, keep)
            keep_turned = jnp.where(here_row, turned, keep_turned)
            keep_pivot = jnp.where(here_row, pivot, keep_pivot)
            for later in range(c + 1, SUB):
                re, im = here[later]
                u_re, u_im = over_rows(re, c), over_rows(im, c)
                if later == c + 1:
                    loss = (u_re * inverse) * u_re + (u_im * inverse) * u_im
                    pivot = over_rows(re, c + 1) - loss
                here[later] = (
                    jnp.where(here_row, 0.0, re) - m_re * u_re + m_im * u_im,
                    jnp.where(here_row, 0.0, im) - m_re * u_im - m_im * u_re,
                )
            on_re, on_im = lane == columns[c], lane == columns[c] + 1
            on_pair = on_re | on_im
            step_ref[c, :SUB, :] = head
            step_ref[c, SUB:, :] = turned
            p = jnp.where(on_pair, on_re.astype(jnp.float32), row_of(step_ref, c, c))
            q = jnp.where(on_pair, on_im.astype(jnp.float32), row_of(step_ref, c, SUB + c))
            cleared = here_row | on_pair
            head = jnp.where(cleared, 0.0, head) - (m_re * p + m_im * q)
            turned = jnp.where(cleared, 0.0, turned) - (m_re * q - m_im * p)
        final.append(keep)
        final_turned.append(keep_turned)
        pivots.append(keep_pivot)
        if own + 1 == count:
            break
        inside = (lane >= columns[0]) & (lane < columns[0] + 2 * SUB)
        solved_ref[own, pl.ds(0, SUB, stride=2), :] = head
        solved_ref[own, pl.ds(1, SUB, stride=2), :] = turned
        solved = [(over_rows(head, c), over_rows(turned, c)) for c in range(SUB)]
        rows[own + 1] = jnp.where(inside, 0.0, rows[own + 1]) - tree_sum(
            [re * p + im * q for (re, im), (p, q) in zip(raw[own + 1], solved)]
        )
        far = range(own + 2, count)
        if far:
            below = jnp.concatenate([rows[i] for i in far], 0)
            losses = jnp.dot(
                below[:, columns[0]:columns[0] + 2 * SUB], solved_ref[own],
                precision=lax.Precision.HIGHEST, preferred_element_type=jnp.float32,
            )
            for at, i in enumerate(far):
                loss = losses[at * SUB:(at + 1) * SUB]
                rows[i] = jnp.where(inside, 0.0, rows[i]) - loss
    return final, final_turned, pivots


def modes_kernel(scale, slabs, x_ref, *refs):
    *given, modes_hbm, factor_hbm, basis_ref, solved_ref, step_ref, points_ref, modes_ref, factor_ref, sems = refs
    width = basis_ref.shape[0]
    size = width // 2
    count = size // SUB
    if given:
        gram = given[0][...]
        mine = x_ref[...]
    else:
        gram = gram_rows([x_ref[i * width:(i + 1) * width] for i in range(slabs)], basis_ref)
        own = lax.axis_index("space")
        mine = x_ref[pl.ds(pl.multiple_of(own * width, width), width)]
    points = jnp.transpose(mine)
    points_ref[...] = jnp.concatenate([points, points], 1)
    gram = gram * scale
    rows, turned, pivots = eliminate([gram[i * SUB:(i + 1) * SUB] for i in range(count)], solved_ref, step_ref)
    shape = rows[0].shape
    sub = lax.broadcasted_iota(jnp.int32, shape, 0)
    lane = lax.broadcasted_iota(jnp.int32, shape, 1)
    pick = jnp.where(lane < size, 2 * lane, 2 * (lane - size) + 1)
    for i in range(count):
        own_rows = slice(i * SUB, (i + 1) * SUB)
        root = lax.rsqrt(pivots[i])
        diagonal = 2 * (i * SUB + sub)
        left = jnp.where(lane < diagonal, rows[i], (lane == diagonal).astype(jnp.float32))
        aside = jnp.where(lane < diagonal, turned[i], (lane == diagonal + 1).astype(jnp.float32))
        basis_ref[pl.ds(2 * i * SUB, SUB, stride=2), :] = left * root
        basis_ref[pl.ds(2 * i * SUB + 1, SUB, stride=2), :] = aside * root
        right = jnp.where(lane > diagonal + 1, rows[i], jnp.where(lane == diagonal, pivots[i], 0.0))
        parts = jnp.take_along_axis(right * root, pick, axis=1)
        factor_ref[0, own_rows, :] = parts[:, :size]
        factor_ref[1, own_rows, :] = parts[:, size:]
    copies = [pltpu.make_async_copy(factor_ref, factor_hbm, sems.at[0])]
    copies[0].start()
    basis = basis_ref[...]
    high = basis.astype(jnp.bfloat16)
    low = (basis - high.astype(jnp.float32)).astype(jnp.bfloat16)
    terms = jnp.concatenate([high, low], 1)
    each = modes_ref.shape[0] // PARTS
    for i in range(PARTS):
        part = slice(i * each, (i + 1) * each)
        modes_ref[part] = lax.dot_general(
            points_ref[part], terms, (((1,), (1,)), ((), ())),
            preferred_element_type=jnp.float32,
        )
        copies.append(pltpu.make_async_copy(modes_ref.at[part], modes_hbm.at[part], sems.at[1 + i]))
        copies[-1].start()
    for copy in copies:
        copy.wait()


def modes_and_factor(x, grams, width, slabs, scale):
    points = x.shape[1]
    size = width // 2
    return pl.pallas_call(
        functools.partial(modes_kernel, scale, slabs),
        out_shape=(
            jax.ShapeDtypeStruct((points, width), jnp.float32),
            jax.ShapeDtypeStruct((2, size, size), jnp.float32),
        ),
        in_specs=[pl.BlockSpec(memory_space=pltpu.VMEM)] * (1 + len(grams)),
        out_specs=(pl.BlockSpec(memory_space=pltpu.HBM),) * 2,
        scratch_shapes=[
            pltpu.VMEM((width, width), jnp.float32),
            pltpu.VMEM((size // SUB, 2 * SUB, width), jnp.float32),
            pltpu.VMEM((SUB, 2 * SUB, width), jnp.float32),
            pltpu.VMEM((points, 2 * width), jnp.bfloat16),
            pltpu.VMEM((points, width), jnp.float32),
            pltpu.VMEM((2, size, size), jnp.float32),
            pltpu.SemaphoreType.DMA((1 + PARTS,)),
        ],
        compiler_params=pltpu.CompilerParams(vmem_limit_bytes=8 * 2**20),
        name="factor_and_modes",
    )(x, *grams)


def local(slabs, snapshots, row_scales, block_offsets, freq_index):
    freqs = freq_index.shape[0]
    points = snapshots.shape[1]
    width = 2 * block_offsets.shape[0] * lax.axis_size("blk")
    copies = slabs if slabs <= FEW_SLABS else 1
    spectra = block_spectra(copies, snapshots, row_scales, block_offsets, freq_index)
    chunks = spectra.reshape(copies * freqs, -1, points)
    swap = functools.partial(lax.all_to_all, split_axis=0, concat_axis=0, tiled=True)
    if copies == slabs:
        x = swap(chunks, ("space", "blk")).reshape(-1, points)
        grams = []
    else:
        x = swap(chunks, "blk").reshape(-1, points)
        grams = [lax.psum(complex_gram(x), "space")]
    modes, factor = modes_and_factor(x, grams, width, slabs, 1.0 / (points * slabs))
    return modes[None], factor[None]


def solution(mesh):
    return jax.shard_map(
        functools.partial(local, mesh.shape["space"]),
        mesh=mesh,
        in_specs=(P("blk", "space"), P("blk"), P("blk"), P()),
        out_specs=(P("blk", "space", None), P("blk", None, None, None)),
        check_vma=False,
    )
```

```python
import functools
import math

import jax
import jax.numpy as jnp
from jax import lax
from jax.experimental import pallas as pl
from jax.experimental.pallas import tpu as pltpu
from jax.sharding import PartitionSpec as P

NFFT = 512
SUB = 8
PIECE = 640
PARTS = 4
FEW_SLABS = 2
SIN_COEFS = (
    0.9999999765895043,
    -0.1666664763439475,
    0.008332899819203531,
    -0.0001980089750772882,
    2.5904879854375602e-06,
)


def cos_of_phase(phase):
    folded = jnp.abs((phase & (NFFT - 1)) - NFFT // 2) - NFFT // 4
    x = folded.astype(jnp.float32) * (2.0 * math.pi / NFFT)
    square = x * x
    total = jnp.full_like(x, SIN_COEFS[-1])
    for coef in SIN_COEFS[-2::-1]:
        total = total * square + coef
    return total * x


def spectra_kernel(
    snap_hbm, scales_hbm, offsets_hbm, freq_hbm, out_ref,
    snap_ref, scales_ref, offsets_ref, freq_ref, coef_ref, small_sems, snap_sems,
):
    snaps = snap_ref.shape[0]
    blocks = offsets_ref.shape[0]
    rows = 2 * blocks
    freqs = freq_ref.shape[0]
    small = [
        pltpu.make_async_copy(src, dst, small_sems.at[i])
        for i, (src, dst) in enumerate(
            ((offsets_hbm, offsets_ref), (freq_hbm, freq_ref), (scales_hbm, scales_ref))
        )
    ]
    pieces = [slice(at, min(at + PIECE, snaps)) for at in range(0, snaps, PIECE)]
    large = [
        pltpu.make_async_copy(snap_hbm.at[piece], snap_ref.at[piece], snap_sems.at[i])
        for i, piece in enumerate(pieces)
    ]
    for copy in small + large:
        copy.start()
    row = lax.broadcasted_iota(jnp.int32, (rows, snaps), 0)
    time = lax.broadcasted_iota(jnp.int32, (rows, snaps), 1)
    for copy in small:
        copy.wait()
    start = jnp.zeros((rows, snaps), jnp.int32)
    for b in range(blocks):
        start = jnp.where(row // 2 == b, offsets_ref[b], start)
    shifted = time - start
    hann = 0.5 - 0.5 * cos_of_phase(shifted)
    inside = (shifted >= 0) & (shifted < NFFT)
    scales = jnp.broadcast_to(scales_ref[...].reshape(1, snaps), (rows, snaps))
    weight = jnp.where(inside, hann * scales * (1.0 / math.sqrt(NFFT)), 0.0)
    quarter = NFFT // 4
    base = shifted[:, :quarter].astype(jnp.float32)
    turn = (row[:, :quarter] % 2) * quarter
    repeats = -(-snaps // NFFT)

    def rows_of(f):
        freq = freq_ref[f]
        phase = (base * freq.astype(jnp.float32)).astype(jnp.int32) + turn
        even, odd = cos_of_phase(phase), cos_of_phase(phase + quarter)
        tiles = [even]
        for j in range(1, 4):
            turns = (freq * j) & 3
            along = ((1 - (turns & 1)) * (1 - turns)).astype(jnp.float32)
            across = ((turns & 1) * (2 - turns)).astype(jnp.float32)
            tiles.append(even * along + odd * across)
        return jnp.concatenate(tiles * repeats, 1)[:, :snaps] * weight

    for f in range(0, freqs, 2):
        pair = jnp.concatenate([rows_of(f), rows_of(f + 1)], 0)
        coef_ref[f * rows:(f + 2) * rows, :] = pair.astype(jnp.bfloat16)
    for copy in large:
        copy.wait()
    total = jnp.dot(coef_ref[...], snap_ref[...], preferred_element_type=jnp.float32)
    result = total.astype(jnp.bfloat16)
    for copy in range(out_ref.shape[0]):
        out_ref[copy] = result


def block_spectra(copies, snapshots, row_scales, block_offsets, freq_index):
    snaps, points = snapshots.shape
    rows = 2 * block_offsets.shape[0] * freq_index.shape[0]
    pieces = -(-snaps // PIECE)
    return pl.pallas_call(
        spectra_kernel,
        out_shape=jax.ShapeDtypeStruct((copies, rows, points), jnp.bfloat16),
        in_specs=[pl.BlockSpec(memory_space=pltpu.HBM)] * 4,
        out_specs=pl.BlockSpec(memory_space=pltpu.VMEM),
        scratch_shapes=[
            pltpu.VMEM((snaps, points), jnp.bfloat16),
            pltpu.VMEM((snaps,), jnp.float32),
            pltpu.SMEM(block_offsets.shape, jnp.int32),
            pltpu.SMEM(freq_index.shape, jnp.int32),
            pltpu.VMEM((rows, snaps), jnp.bfloat16),
            pltpu.SemaphoreType.DMA((3,)),
            pltpu.SemaphoreType.DMA((pieces,)),
        ],
        compiler_params=pltpu.CompilerParams(vmem_limit_bytes=8 * 2**20),
        name="spectra",
    )(*(
        pltpu.with_memory_space_constraint(x, pltpu.HBM)
        for x in (snapshots, row_scales, block_offsets, freq_index)
    ))


def rotated(x, lane):
    axis = x.ndim - 1
    width = x.shape[axis]
    after = pltpu.roll(x, width - 1, axis)
    before = pltpu.roll(x, 1, axis)
    return jnp.where(lane % 2 == 0, -after, before)


def gram_rows(slabs, full_ref):
    width = full_ref.shape[0]
    full_ref[...] = sum(
        lax.dot_general(x, x, (((1,), (1,)), ((), ())), preferred_element_type=jnp.float32)
        for x in slabs
    )
    even = full_ref[pl.ds(0, width // 2, stride=2), :]
    odd = full_ref[pl.ds(1, width // 2, stride=2), :]
    lane = lax.broadcasted_iota(jnp.int32, odd.shape, 1)
    return even - rotated(odd, lane)


def gram_kernel(x_ref, out_ref, full_ref):
    out_ref[...] = gram_rows([x_ref[...]], full_ref)


def complex_gram(x):
    width = x.shape[0]
    return pl.pallas_call(
        gram_kernel,
        out_shape=jax.ShapeDtypeStruct((width // 2, width), jnp.float32),
        in_specs=[pl.BlockSpec(memory_space=pltpu.VMEM)],
        out_specs=pl.BlockSpec(memory_space=pltpu.VMEM),
        scratch_shapes=[pltpu.VMEM((width, width), jnp.float32)],
        compiler_params=pltpu.CompilerParams(vmem_limit_bytes=4 * 2**20),
        name="gram",
    )(x)


def tree_sum(terms):
    while len(terms) > 1:
        terms = [sum(terms[i:i + 2]) for i in range(0, len(terms), 2)]
    return terms[0]


def eliminate(rows, solved_ref, step_ref):
    count = len(rows)
    shape = rows[0].shape
    sub = lax.broadcasted_iota(jnp.int32, shape, 0)
    lane = lax.broadcasted_iota(jnp.int32, shape, 1)

    def over_lanes(x, at):
        return jnp.broadcast_to(x[:, at:at + 1], shape)

    def over_rows(x, at):
        return jnp.broadcast_to(x[at:at + 1, :], shape)

    def row_of(ref, *at):
        return ref[(*at[:-1], pl.ds(at[-1], SUB, stride=0), slice(None))]

    rows = list(rows)
    final, final_turned, pivots = [], [], []
    for own in range(count):
        head, turned = rows[own], rotated(rows[own], lane)
        keep, keep_turned, keep_pivot = head, turned, jnp.ones(shape, jnp.float32)
        columns = [2 * (own * SUB + c) for c in range(SUB)]
        raw = {
            i: [(over_lanes(rows[i], at), over_lanes(rows[i], at + 1)) for at in columns]
            for i in range(own, min(own + 2, count))
        }
        here = raw[own]
        pivot = over_rows(here[0][0], 0)
        for c in range(SUB):
            here_row = sub == c
            inverse = pl.reciprocal(pivot, approx=True)
            m_re = jnp.where(here_row, -1.0, here[c][0]) * inverse
            m_im = jnp.where(here_row, 0.0, here[c][1]) * inverse
            keep = jnp.where(here_row, head, keep)
            keep_turned = jnp.where(here_row, turned, keep_turned)
            keep_pivot = jnp.where(here_row, pivot, keep_pivot)
            for later in range(c + 1, SUB):
                re, im = here[later]
                u_re, u_im = over_rows(re, c), over_rows(im, c)
                if later == c + 1:
                    loss = (u_re * inverse) * u_re + (u_im * inverse) * u_im
                    pivot = over_rows(re, c + 1) - loss
                here[later] = (
                    jnp.where(here_row, 0.0, re) - m_re * u_re + m_im * u_im,
                    jnp.where(here_row, 0.0, im) - m_re * u_im - m_im * u_re,
                )
            on_re, on_im = lane == columns[c], lane == columns[c] + 1
            on_pair = on_re | on_im
            step_ref[c, :SUB, :] = head
            step_ref[c, SUB:, :] = turned
            p = jnp.where(on_pair, on_re.astype(jnp.float32), row_of(step_ref, c, c))
            q = jnp.where(on_pair, on_im.astype(jnp.float32), row_of(step_ref, c, SUB + c))
            cleared = here_row | on_pair
            head = jnp.where(cleared, 0.0, head) - (m_re * p + m_im * q)
            turned = jnp.where(cleared, 0.0, turned) - (m_re * q - m_im * p)
        final.append(keep)
        final_turned.append(keep_turned)
        pivots.append(keep_pivot)
        if own + 1 == count:
            break
        inside = (lane >= columns[0]) & (lane < columns[0] + 2 * SUB)
        solved_ref[own, pl.ds(0, SUB, stride=2), :] = head
        solved_ref[own, pl.ds(1, SUB, stride=2), :] = turned
        solved = [(over_rows(head, c), over_rows(turned, c)) for c in range(SUB)]
        rows[own + 1] = jnp.where(inside, 0.0, rows[own + 1]) - tree_sum(
            [re * p + im * q for (re, im), (p, q) in zip(raw[own + 1], solved)]
        )
        far = range(own + 2, count)
        if far:
            below = jnp.concatenate([rows[i] for i in far], 0)
            losses = jnp.dot(
                below[:, columns[0]:columns[0] + 2 * SUB], solved_ref[own],
                precision=lax.Precision.HIGHEST, preferred_element_type=jnp.float32,
            )
            for at, i in enumerate(far):
                loss = losses[at * SUB:(at + 1) * SUB]
                rows[i] = jnp.where(inside, 0.0, rows[i]) - loss
    return final, final_turned, pivots


def modes_kernel(scale, slabs, x_ref, *refs):
    *given, modes_hbm, factor_hbm, basis_ref, solved_ref, step_ref, points_ref, modes_ref, factor_ref, sems = refs
    width = basis_ref.shape[0]
    size = width // 2
    count = size // SUB
    if given:
        gram = given[0][...]
        mine = x_ref[...]
    else:
        gram = gram_rows([x_ref[i * width:(i + 1) * width] for i in range(slabs)], basis_ref)
        own = lax.axis_index("space")
        mine = x_ref[pl.ds(pl.multiple_of(own * width, width), width)]
    points = jnp.transpose(mine)
    points_ref[...] = jnp.concatenate([points, points], 1)
    gram = gram * scale
    rows, turned, pivots = eliminate([gram[i * SUB:(i + 1) * SUB] for i in range(count)], solved_ref, step_ref)
    shape = rows[0].shape
    sub = lax.broadcasted_iota(jnp.int32, shape, 0)
    lane = lax.broadcasted_iota(jnp.int32, shape, 1)
    pick = jnp.where(lane < size, 2 * lane, 2 * (lane - size) + 1)
    for i in range(count):
        own_rows = slice(i * SUB, (i + 1) * SUB)
        root = lax.rsqrt(pivots[i])
        diagonal = 2 * (i * SUB + sub)
        left = jnp.where(lane < diagonal, rows[i], (lane == diagonal).astype(jnp.float32))
        aside = jnp.where(lane < diagonal, turned[i], (lane == diagonal + 1).astype(jnp.float32))
        basis_ref[pl.ds(2 * i * SUB, SUB, stride=2), :] = left * root
        basis_ref[pl.ds(2 * i * SUB + 1, SUB, stride=2), :] = aside * root
        right = jnp.where(lane > diagonal + 1, rows[i], jnp.where(lane == diagonal, pivots[i], 0.0))
        parts = jnp.take_along_axis(right * root, pick, axis=1)
        factor_ref[0, own_rows, :] = parts[:, :size]
        factor_ref[1, own_rows, :] = parts[:, size:]
    copies = [pltpu.make_async_copy(factor_ref, factor_hbm, sems.at[0])]
    copies[0].start()
    basis = basis_ref[...]
    high = basis.astype(jnp.bfloat16)
    low = (basis - high.astype(jnp.float32)).astype(jnp.bfloat16)
    terms = jnp.concatenate([high, low], 1)
    each = modes_ref.shape[0] // PARTS
    for i in range(PARTS):
        part = slice(i * each, (i + 1) * each)
        modes_ref[part] = lax.dot_general(
            points_ref[part], terms, (((1,), (1,)), ((), ())),
            preferred_element_type=jnp.float32,
        )
        copies.append(pltpu.make_async_copy(modes_ref.at[part], modes_hbm.at[part], sems.at[1 + i]))
        copies[-1].start()
    for copy in copies:
        copy.wait()


def modes_and_factor(x, grams, width, slabs, scale):
    points = x.shape[1]
    size = width // 2
    return pl.pallas_call(
        functools.partial(modes_kernel, scale, slabs),
        out_shape=(
            jax.ShapeDtypeStruct((points, width), jnp.float32),
            jax.ShapeDtypeStruct((2, size, size), jnp.float32),
        ),
        in_specs=[pl.BlockSpec(memory_space=pltpu.VMEM)] * (1 + len(grams)),
        out_specs=(pl.BlockSpec(memory_space=pltpu.HBM),) * 2,
        scratch_shapes=[
            pltpu.VMEM((width, width), jnp.float32),
            pltpu.VMEM((size // SUB, 2 * SUB, width), jnp.float32),
            pltpu.VMEM((SUB, 2 * SUB, width), jnp.float32),
            pltpu.VMEM((points, 2 * width), jnp.bfloat16),
            pltpu.VMEM((points, width), jnp.float32),
            pltpu.VMEM((2, size, size), jnp.float32),
            pltpu.SemaphoreType.DMA((1 + PARTS,)),
        ],
        compiler_params=pltpu.CompilerParams(vmem_limit_bytes=8 * 2**20),
        name="factor_and_modes",
    )(x, *grams)


def local(slabs, snapshots, row_scales, block_offsets, freq_index):
    freqs = freq_index.shape[0]
    points = snapshots.shape[1]
    width = 2 * block_offsets.shape[0] * lax.axis_size("blk")
    copies = slabs if slabs <= FEW_SLABS else 1
    spectra = block_spectra(copies, snapshots, row_scales, block_offsets, freq_index)
    chunks = spectra.reshape(copies * freqs, -1, points)
    swap = functools.partial(lax.all_to_all, split_axis=0, concat_axis=0, tiled=True)
    if copies == slabs:
        x = swap(chunks, ("space", "blk")).reshape(-1, points)
        grams = []
    else:
        x = swap(chunks, "blk").reshape(-1, points)
        grams = [lax.psum(complex_gram(x), "space")]
    modes, factor = modes_and_factor(x, grams, width, slabs, 1.0 / (points * slabs))
    return modes[None], factor[None]


def solution(mesh):
    return jax.shard_map(
        functools.partial(local, mesh.shape["space"]),
        mesh=mesh,
        in_specs=(P("blk", "space"), P("blk"), P("blk"), P()),
        out_specs=(P("blk", "space", None), P("blk", None, None, None)),
        check_vma=False,
    )
```

```python
import functools
import math

import jax
import jax.numpy as jnp
from jax import lax
from jax.experimental import pallas as pl
from jax.experimental.pallas import tpu as pltpu
from jax.sharding import PartitionSpec as P

NFFT = 512
SUB = 8
PIECE = 768
PARTS = 4
FEW_SLABS = 2
SIN_COEFS = (
    0.9999999765895043,
    -0.1666664763439475,
    0.008332899819203531,
    -0.0001980089750772882,
    2.5904879854375602e-06,
)


def cos_of_phase(phase):
    folded = jnp.abs((phase & (NFFT - 1)) - NFFT // 2) - NFFT // 4
    x = folded.astype(jnp.float32) * (2.0 * math.pi / NFFT)
    square = x * x
    total = jnp.full_like(x, SIN_COEFS[-1])
    for coef in SIN_COEFS[-2::-1]:
        total = total * square + coef
    return total * x


def spectra_kernel(
    snap_hbm, scales_hbm, offsets_hbm, freq_hbm, out_ref,
    snap_ref, scales_ref, offsets_ref, freq_ref, coef_ref, small_sems, snap_sems,
):
    snaps = snap_ref.shape[0]
    blocks = offsets_ref.shape[0]
    rows = 2 * blocks
    freqs = freq_ref.shape[0]
    small = [
        pltpu.make_async_copy(src, dst, small_sems.at[i])
        for i, (src, dst) in enumerate(
            ((offsets_hbm, offsets_ref), (freq_hbm, freq_ref), (scales_hbm, scales_ref))
        )
    ]
    pieces = [slice(at, min(at + PIECE, snaps)) for at in range(0, snaps, PIECE)]
    large = [
        pltpu.make_async_copy(snap_hbm.at[piece], snap_ref.at[piece], snap_sems.at[i])
        for i, piece in enumerate(pieces)
    ]
    for copy in small + large:
        copy.start()
    row = lax.broadcasted_iota(jnp.int32, (rows, snaps), 0)
    time = lax.broadcasted_iota(jnp.int32, (rows, snaps), 1)
    for copy in small:
        copy.wait()
    start = jnp.zeros((rows, snaps), jnp.int32)
    for b in range(blocks):
        start = jnp.where(row // 2 == b, offsets_ref[b], start)
    shifted = time - start
    hann = 0.5 - 0.5 * cos_of_phase(shifted)
    inside = (shifted >= 0) & (shifted < NFFT)
    scales = jnp.broadcast_to(scales_ref[...].reshape(1, snaps), (rows, snaps))
    weight = jnp.where(inside, hann * scales * (1.0 / math.sqrt(NFFT)), 0.0)
    quarter = NFFT // 4
    base = shifted[:, :quarter].astype(jnp.float32)
    turn = (row[:, :quarter] % 2) * quarter
    repeats = -(-snaps // NFFT)

    def rows_of(f):
        freq = freq_ref[f]
        phase = (base * freq.astype(jnp.float32)).astype(jnp.int32) + turn
        even, odd = cos_of_phase(phase), cos_of_phase(phase + quarter)
        tiles = [even]
        for j in range(1, 4):
            turns = (freq * j) & 3
            along = ((1 - (turns & 1)) * (1 - turns)).astype(jnp.float32)
            across = ((turns & 1) * (2 - turns)).astype(jnp.float32)
            tiles.append(even * along + odd * across)
        return jnp.concatenate(tiles * repeats, 1)[:, :snaps] * weight

    for f in range(0, freqs, 2):
        pair = jnp.concatenate([rows_of(f), rows_of(f + 1)], 0)
        coef_ref[f * rows:(f + 2) * rows, :] = pair.astype(jnp.bfloat16)
    parts = []
    for copy, piece in zip(large, pieces):
        copy.wait()
        parts.append(
            jnp.dot(coef_ref[:, piece], snap_ref[piece], preferred_element_type=jnp.float32)
        )
    total = sum(parts[1:], parts[0])
    result = total.astype(jnp.bfloat16)
    for copy in range(out_ref.shape[0]):
        out_ref[copy] = result


def block_spectra(copies, snapshots, row_scales, block_offsets, freq_index):
    snaps, points = snapshots.shape
    rows = 2 * block_offsets.shape[0] * freq_index.shape[0]
    pieces = -(-snaps // PIECE)
    return pl.pallas_call(
        spectra_kernel,
        out_shape=jax.ShapeDtypeStruct((copies, rows, points), jnp.bfloat16),
        in_specs=[pl.BlockSpec(memory_space=pltpu.HBM)] * 4,
        out_specs=pl.BlockSpec(memory_space=pltpu.VMEM),
        scratch_shapes=[
            pltpu.VMEM((snaps, points), jnp.bfloat16),
            pltpu.VMEM((snaps,), jnp.float32),
            pltpu.SMEM(block_offsets.shape, jnp.int32),
            pltpu.SMEM(freq_index.shape, jnp.int32),
            pltpu.VMEM((rows, snaps), jnp.bfloat16),
            pltpu.SemaphoreType.DMA((3,)),
            pltpu.SemaphoreType.DMA((pieces,)),
        ],
        compiler_params=pltpu.CompilerParams(vmem_limit_bytes=8 * 2**20),
        name="spectra",
    )(*(
        pltpu.with_memory_space_constraint(x, pltpu.HBM)
        for x in (snapshots, row_scales, block_offsets, freq_index)
    ))


def rotated(x, lane):
    axis = x.ndim - 1
    width = x.shape[axis]
    after = pltpu.roll(x, width - 1, axis)
    before = pltpu.roll(x, 1, axis)
    return jnp.where(lane % 2 == 0, -after, before)


def gram_rows(slabs, full_ref):
    width = full_ref.shape[0]
    full_ref[...] = sum(
        lax.dot_general(x, x, (((1,), (1,)), ((), ())), preferred_element_type=jnp.float32)
        for x in slabs
    )
    even = full_ref[pl.ds(0, width // 2, stride=2), :]
    odd = full_ref[pl.ds(1, width // 2, stride=2), :]
    lane = lax.broadcasted_iota(jnp.int32, odd.shape, 1)
    return even - rotated(odd, lane)


def gram_kernel(x_ref, out_ref, full_ref):
    out_ref[...] = gram_rows([x_ref[...]], full_ref)


def complex_gram(x):
    width = x.shape[0]
    return pl.pallas_call(
        gram_kernel,
        out_shape=jax.ShapeDtypeStruct((width // 2, width), jnp.float32),
        in_specs=[pl.BlockSpec(memory_space=pltpu.VMEM)],
        out_specs=pl.BlockSpec(memory_space=pltpu.VMEM),
        scratch_shapes=[pltpu.VMEM((width, width), jnp.float32)],
        compiler_params=pltpu.CompilerParams(vmem_limit_bytes=4 * 2**20),
        name="gram",
    )(x)


def tree_sum(terms):
    while len(terms) > 1:
        terms = [sum(terms[i:i + 2]) for i in range(0, len(terms), 2)]
    return terms[0]


def conj_times(a, b):
    return a[0] * b[0] + a[1] * b[1], a[0] * b[1] - a[1] * b[0]


def eliminate(rows, solved_ref, step_ref):
    count = len(rows)
    shape = rows[0].shape
    sub = lax.broadcasted_iota(jnp.int32, shape, 0)
    lane = lax.broadcasted_iota(jnp.int32, shape, 1)

    def over_lanes(x, at):
        return jnp.broadcast_to(x[:, at:at + 1], shape)

    def over_rows(x, at):
        return jnp.broadcast_to(x[at:at + 1, :], shape)

    def entry(column, at):
        return over_rows(column[0], at), over_rows(column[1], at)

    def row_of(ref, *at):
        return ref[(*at[:-1], pl.ds(at[-1], SUB, stride=0), slice(None))]

    rows = list(rows)
    final, final_turned, pivots = [], [], []
    for own in range(count):
        head, turned = rows[own], rotated(rows[own], lane)
        keep, keep_turned, keep_pivot = head, turned, jnp.ones(shape, jnp.float32)
        columns = [2 * (own * SUB + c) for c in range(SUB)]
        raw = {
            i: [(over_lanes(rows[i], at), over_lanes(rows[i], at + 1)) for at in columns]
            for i in range(own, min(own + 2, count))
        }
        here = raw[own]
        ahead = over_rows(here[0][0], 0), over_rows(here[1][0], 1), entry(here[1], 0)
        for c in range(SUB):
            here_row = sub == c
            if c % 2 == 0:
                first, second, u = ahead
                square = conj_times(u, u)[0]
                inverse = pl.reciprocal(first, approx=True)
                inverses = inverse, first * pl.reciprocal(first * second - square, approx=True)
                values = first, second - square * inverse
                uppers = [{k: entry(here[k], c) for k in range(c + 1, SUB)}, {}]
                for k in range(c + 2, SUB):
                    old, loss = entry(here[k], c + 1), conj_times(u, uppers[0][k])
                    uppers[1][k] = old[0] - loss[0] * inverse, old[1] - loss[1] * inverse
                if c + 2 < SUB:
                    one, two = c + 2, c + 3
                    next_u = entry(here[two], one)
                    (a1, a2, au), (b1, b2, bu) = [
                        (conj_times(up[one], up[one])[0], conj_times(up[two], up[two])[0], conj_times(up[one], up[two]))
                        for up in uppers
                    ]
                    ahead = (
                        (over_rows(here[one][0], one) - a1 * inverse) - b1 * inverses[1],
                        (over_rows(here[two][0], two) - a2 * inverse) - b2 * inverses[1],
                        tuple(
                            (next_u[k] - au[k] * inverse) - bu[k] * inverses[1] for k in range(2)
                        ),
                    )
            m_re = jnp.where(here_row, -1.0, here[c][0]) * inverses[c % 2]
            m_im = jnp.where(here_row, 0.0, here[c][1]) * inverses[c % 2]
            keep = jnp.where(here_row, head, keep)
            keep_turned = jnp.where(here_row, turned, keep_turned)
            keep_pivot = jnp.where(here_row, values[c % 2], keep_pivot)
            for later, (u_re, u_im) in uppers[c % 2].items():
                re, im = here[later]
                here[later] = (
                    jnp.where(here_row, 0.0, re) - m_re * u_re + m_im * u_im,
                    jnp.where(here_row, 0.0, im) - m_re * u_im - m_im * u_re,
                )
            on_re, on_im = lane == columns[c], lane == columns[c] + 1
            on_pair = on_re | on_im
            step_ref[c, :SUB, :] = head
            step_ref[c, SUB:, :] = turned
            p = jnp.where(on_pair, on_re.astype(jnp.float32), row_of(step_ref, c, c))
            q = jnp.where(on_pair, on_im.astype(jnp.float32), row_of(step_ref, c, SUB + c))
            cleared = here_row | on_pair
            head = jnp.where(cleared, 0.0, head) - (m_re * p + m_im * q)
            turned = jnp.where(cleared, 0.0, turned) - (m_re * q - m_im * p)
        final.append(keep)
        final_turned.append(keep_turned)
        pivots.append(keep_pivot)
        if own + 1 == count:
            break
        inside = (lane >= columns[0]) & (lane < columns[0] + 2 * SUB)
        solved_ref[own, pl.ds(0, SUB, stride=2), :] = head
        solved_ref[own, pl.ds(1, SUB, stride=2), :] = turned
        solved = [(over_rows(head, c), over_rows(turned, c)) for c in range(SUB)]
        rows[own + 1] = jnp.where(inside, 0.0, rows[own + 1]) - tree_sum(
            [re * p + im * q for (re, im), (p, q) in zip(raw[own + 1], solved)]
        )
        far = range(own + 2, count)
        if far:
            below = jnp.concatenate([rows[i] for i in far], 0)
            losses = jnp.dot(
                below[:, columns[0]:columns[0] + 2 * SUB], solved_ref[own],
                precision=lax.Precision.HIGHEST, preferred_element_type=jnp.float32,
            )
            for at, i in enumerate(far):
                loss = losses[at * SUB:(at + 1) * SUB]
                rows[i] = jnp.where(inside, 0.0, rows[i]) - loss
    return final, final_turned, pivots


def unit_diagonal(rows):
    shape = rows[0].shape
    sub = lax.broadcasted_iota(jnp.int32, shape, 0)
    lane = lax.broadcasted_iota(jnp.int32, shape, 1)
    diagonals = [jnp.where(lane == 2 * (i * SUB + sub), row, 0.0) for i, row in enumerate(rows)]
    across = jnp.sum(tree_sum(diagonals), axis=0, keepdims=True)
    across = jnp.broadcast_to(across, shape)
    across = across + pltpu.roll(across, 1, 1)
    root = lax.rsqrt(across)
    scaled = [
        row * lax.rsqrt(jnp.sum(diagonal, axis=1, keepdims=True)) * root
        for row, diagonal in zip(rows, diagonals)
    ]
    return scaled, root, across * root


def modes_kernel(scale, slabs, x_ref, *refs):
    *given, modes_hbm, factor_hbm, basis_ref, solved_ref, step_ref, points_ref, modes_ref, factor_ref, sems = refs
    width = basis_ref.shape[0]
    size = width // 2
    count = size // SUB
    if given:
        gram = given[0][...]
        mine = x_ref[...]
    else:
        gram = gram_rows([x_ref[i * width:(i + 1) * width] for i in range(slabs)], basis_ref)
        own = lax.axis_index("space")
        mine = x_ref[pl.ds(pl.multiple_of(own * width, width), width)]
    points = jnp.transpose(mine)
    points_ref[...] = jnp.concatenate([points, points], 1)
    rows, shrink, grow = unit_diagonal([gram[i * SUB:(i + 1) * SUB] for i in range(count)])
    shrink, grow = shrink * (1.0 / math.sqrt(scale)), grow * math.sqrt(scale)
    rows, turned, pivots = eliminate(rows, solved_ref, step_ref)
    shape = rows[0].shape
    sub = lax.broadcasted_iota(jnp.int32, shape, 0)
    lane = lax.broadcasted_iota(jnp.int32, shape, 1)
    pick = jnp.where(lane < size, 2 * lane, 2 * (lane - size) + 1)
    for i in range(count):
        own_rows = slice(i * SUB, (i + 1) * SUB)
        root = lax.rsqrt(pivots[i])
        diagonal = 2 * (i * SUB + sub)
        left = jnp.where(lane < diagonal, rows[i], (lane == diagonal).astype(jnp.float32))
        aside = jnp.where(lane < diagonal, turned[i], (lane == diagonal + 1).astype(jnp.float32))
        basis_ref[pl.ds(2 * i * SUB, SUB, stride=2), :] = left * (root * shrink)
        basis_ref[pl.ds(2 * i * SUB + 1, SUB, stride=2), :] = aside * (root * shrink)
        right = jnp.where(lane > diagonal + 1, rows[i], jnp.where(lane == diagonal, pivots[i], 0.0))
        parts = jnp.take_along_axis(right * (root * grow), pick, axis=1)
        factor_ref[0, own_rows, :] = parts[:, :size]
        factor_ref[1, own_rows, :] = parts[:, size:]
    copies = [pltpu.make_async_copy(factor_ref, factor_hbm, sems.at[0])]
    copies[0].start()
    basis = basis_ref[...]
    high = basis.astype(jnp.bfloat16)
    low = (basis - high.astype(jnp.float32)).astype(jnp.bfloat16)
    terms = jnp.concatenate([high, low], 1)
    each = modes_ref.shape[0] // PARTS
    for i in range(PARTS):
        part = slice(i * each, (i + 1) * each)
        modes_ref[part] = lax.dot_general(
            points_ref[part], terms, (((1,), (1,)), ((), ())),
            preferred_element_type=jnp.float32,
        )
        copies.append(pltpu.make_async_copy(modes_ref.at[part], modes_hbm.at[part], sems.at[1 + i]))
        copies[-1].start()
    for copy in copies:
        copy.wait()


def modes_and_factor(x, grams, width, slabs, scale):
    points = x.shape[1]
    size = width // 2
    return pl.pallas_call(
        functools.partial(modes_kernel, scale, slabs),
        out_shape=(
            jax.ShapeDtypeStruct((points, width), jnp.float32),
            jax.ShapeDtypeStruct((2, size, size), jnp.float32),
        ),
        in_specs=[pl.BlockSpec(memory_space=pltpu.VMEM)] * (1 + len(grams)),
        out_specs=(pl.BlockSpec(memory_space=pltpu.HBM),) * 2,
        scratch_shapes=[
            pltpu.VMEM((width, width), jnp.float32),
            pltpu.VMEM((size // SUB, 2 * SUB, width), jnp.float32),
            pltpu.VMEM((SUB, 2 * SUB, width), jnp.float32),
            pltpu.VMEM((points, 2 * width), jnp.bfloat16),
            pltpu.VMEM((points, width), jnp.float32),
            pltpu.VMEM((2, size, size), jnp.float32),
            pltpu.SemaphoreType.DMA((1 + PARTS,)),
        ],
        compiler_params=pltpu.CompilerParams(vmem_limit_bytes=8 * 2**20),
        name="factor_and_modes",
    )(x, *grams)


def local(slabs, snapshots, row_scales, block_offsets, freq_index):
    freqs = freq_index.shape[0]
    points = snapshots.shape[1]
    width = 2 * block_offsets.shape[0] * lax.axis_size("blk")
    copies = slabs if slabs <= FEW_SLABS else 1
    spectra = block_spectra(copies, snapshots, row_scales, block_offsets, freq_index)
    chunks = spectra.reshape(copies * freqs, -1, points)
    swap = functools.partial(lax.all_to_all, split_axis=0, concat_axis=0, tiled=True)
    if copies == slabs:
        x = swap(chunks, ("space", "blk")).reshape(-1, points)
        grams = []
    else:
        x = swap(chunks, "blk").reshape(-1, points)
        grams = [lax.psum(complex_gram(x), "space")]
    modes, factor = modes_and_factor(x, grams, width, slabs, 1.0 / (points * slabs))
    return modes[None], factor[None]


def solution(mesh):
    return jax.shard_map(
        functools.partial(local, mesh.shape["space"]),
        mesh=mesh,
        in_specs=(P("blk", "space"), P("blk"), P("blk"), P()),
        out_specs=(P("blk", "space", None), P("blk", None, None, None)),
        check_vma=False,
    )
```

```python
import functools
import math

import jax
import jax.numpy as jnp
from jax import lax
from jax.experimental import pallas as pl
from jax.experimental.pallas import tpu as pltpu
from jax.sharding import PartitionSpec as P

NFFT = 512
SUB = 8
PIECE = 640
PARTS = 4
FEW_SLABS = 2
SIN_COEFS = (
    0.9999999765895043,
    -0.1666664763439475,
    0.008332899819203531,
    -0.0001980089750772882,
    2.5904879854375602e-06,
)


def cos_of_phase(phase):
    folded = jnp.abs((phase & (NFFT - 1)) - NFFT // 2) - NFFT // 4
    x = folded.astype(jnp.float32) * (2.0 * math.pi / NFFT)
    square = x * x
    total = jnp.full_like(x, SIN_COEFS[-1])
    for coef in SIN_COEFS[-2::-1]:
        total = total * square + coef
    return total * x


def spectra_kernel(
    snap_hbm, scales_hbm, offsets_hbm, freq_hbm, out_ref,
    snap_ref, scales_ref, offsets_ref, freq_ref, coef_ref, small_sems, snap_sems,
):
    snaps = snap_ref.shape[0]
    blocks = offsets_ref.shape[0]
    rows = 2 * blocks
    freqs = freq_ref.shape[0]
    small = [
        pltpu.make_async_copy(src, dst, small_sems.at[i])
        for i, (src, dst) in enumerate(
            ((offsets_hbm, offsets_ref), (freq_hbm, freq_ref), (scales_hbm, scales_ref))
        )
    ]
    pieces = [slice(at, min(at + PIECE, snaps)) for at in range(0, snaps, PIECE)]
    large = [
        pltpu.make_async_copy(snap_hbm.at[piece], snap_ref.at[piece], snap_sems.at[i])
        for i, piece in enumerate(pieces)
    ]
    for copy in small + large:
        copy.start()
    row = lax.broadcasted_iota(jnp.int32, (rows, snaps), 0)
    time = lax.broadcasted_iota(jnp.int32, (rows, snaps), 1)
    for copy in small:
        copy.wait()
    start = jnp.zeros((rows, snaps), jnp.int32)
    for b in range(blocks):
        start = jnp.where(row // 2 == b, offsets_ref[b], start)
    shifted = time - start
    hann = 0.5 - 0.5 * cos_of_phase(shifted)
    inside = (shifted >= 0) & (shifted < NFFT)
    scales = jnp.broadcast_to(scales_ref[...].reshape(1, snaps), (rows, snaps))
    weight = jnp.where(inside, hann * scales * (1.0 / math.sqrt(NFFT)), 0.0)
    quarter = NFFT // 4
    base = shifted[:, :quarter].astype(jnp.float32)
    turn = (row[:, :quarter] % 2) * quarter
    repeats = -(-snaps // NFFT)

    def rows_of(f):
        freq = freq_ref[f]
        phase = (base * freq.astype(jnp.float32)).astype(jnp.int32) + turn
        even, odd = cos_of_phase(phase), cos_of_phase(phase + quarter)
        tiles = [even]
        for j in range(1, 4):
            turns = (freq * j) & 3
            along = ((1 - (turns & 1)) * (1 - turns)).astype(jnp.float32)
            across = ((turns & 1) * (2 - turns)).astype(jnp.float32)
            tiles.append(even * along + odd * across)
        return jnp.concatenate(tiles * repeats, 1)[:, :snaps] * weight

    for f in range(0, freqs, 2):
        pair = jnp.concatenate([rows_of(f), rows_of(f + 1)], 0)
        coef_ref[f * rows:(f + 2) * rows, :] = pair.astype(jnp.bfloat16)
    for copy in large:
        copy.wait()
    total = jnp.dot(coef_ref[...], snap_ref[...], preferred_element_type=jnp.float32)
    result = total.astype(jnp.bfloat16)
    for copy in range(out_ref.shape[0]):
        out_ref[copy] = result


def block_spectra(copies, snapshots, row_scales, block_offsets, freq_index):
    snaps, points = snapshots.shape
    rows = 2 * block_offsets.shape[0] * freq_index.shape[0]
    pieces = -(-snaps // PIECE)
    return pl.pallas_call(
        spectra_kernel,
        out_shape=jax.ShapeDtypeStruct((copies, rows, points), jnp.bfloat16),
        in_specs=[pl.BlockSpec(memory_space=pltpu.HBM)] * 4,
        out_specs=pl.BlockSpec(memory_space=pltpu.VMEM),
        scratch_shapes=[
            pltpu.VMEM((snaps, points), jnp.bfloat16),
            pltpu.VMEM((snaps,), jnp.float32),
            pltpu.SMEM(block_offsets.shape, jnp.int32),
            pltpu.SMEM(freq_index.shape, jnp.int32),
            pltpu.VMEM((rows, snaps), jnp.bfloat16),
            pltpu.SemaphoreType.DMA((3,)),
            pltpu.SemaphoreType.DMA((pieces,)),
        ],
        compiler_params=pltpu.CompilerParams(vmem_limit_bytes=8 * 2**20),
        name="spectra",
    )(*(
        pltpu.with_memory_space_constraint(x, pltpu.HBM)
        for x in (snapshots, row_scales, block_offsets, freq_index)
    ))


def rotated(x, lane):
    axis = x.ndim - 1
    width = x.shape[axis]
    after = pltpu.roll(x, width - 1, axis)
    before = pltpu.roll(x, 1, axis)
    return jnp.where(lane % 2 == 0, -after, before)


def gram_rows(slabs, full_ref):
    width = full_ref.shape[0]
    full_ref[...] = sum(
        lax.dot_general(x, x, (((1,), (1,)), ((), ())), preferred_element_type=jnp.float32)
        for x in slabs
    )
    even = full_ref[pl.ds(0, width // 2, stride=2), :]
    odd = full_ref[pl.ds(1, width // 2, stride=2), :]
    lane = lax.broadcasted_iota(jnp.int32, odd.shape, 1)
    return even - rotated(odd, lane)


def gram_kernel(x_ref, out_ref, full_ref):
    out_ref[...] = gram_rows([x_ref[...]], full_ref)


def complex_gram(x):
    width = x.shape[0]
    return pl.pallas_call(
        gram_kernel,
        out_shape=jax.ShapeDtypeStruct((width // 2, width), jnp.float32),
        in_specs=[pl.BlockSpec(memory_space=pltpu.VMEM)],
        out_specs=pl.BlockSpec(memory_space=pltpu.VMEM),
        scratch_shapes=[pltpu.VMEM((width, width), jnp.float32)],
        compiler_params=pltpu.CompilerParams(vmem_limit_bytes=4 * 2**20),
        name="gram",
    )(x)


def tree_sum(terms):
    while len(terms) > 1:
        terms = [sum(terms[i:i + 2]) for i in range(0, len(terms), 2)]
    return terms[0]


def three_terms(x):
    high = x.astype(jnp.bfloat16)
    rest = x - high.astype(jnp.float32)
    middle = rest.astype(jnp.bfloat16)
    return high, middle, (rest - middle.astype(jnp.float32)).astype(jnp.bfloat16)


def parts_apart(x, lane):
    size = x.shape[1] // 2
    return jnp.take_along_axis(x, jnp.where(lane < size, 2 * lane, 2 * (lane - size) + 1), axis=1)


def eliminate(rows, step_ref):
    count = len(rows)
    shape = rows[0].shape
    sub = lax.broadcasted_iota(jnp.int32, shape, 0)
    lane = lax.broadcasted_iota(jnp.int32, shape, 1)

    def over_lanes(x, at):
        return jnp.broadcast_to(x[:, at:at + 1], shape)

    def over_rows(x, at):
        return jnp.broadcast_to(x[at:at + 1, :], shape)

    def row_of(ref, *at):
        return ref[(*at[:-1], pl.ds(at[-1], SUB, stride=0), slice(None))]

    rows = list(rows)
    final, final_turned, pivots = [], [], []
    for own in range(count):
        head, turned = rows[own], rotated(rows[own], lane)
        keep, keep_turned, keep_pivot = head, turned, jnp.ones(shape, jnp.float32)
        columns = [2 * (own * SUB + c) for c in range(SUB)]
        raw = {
            i: [(over_lanes(rows[i], at), over_lanes(rows[i], at + 1)) for at in columns]
            for i in range(own, min(own + 2, count))
        }
        apart = parts_apart(head, lane)
        high, middle, low = three_terms(
            jnp.concatenate([apart, -pltpu.roll(apart, shape[1] // 2, 1)], 0)
        )
        columns_below = jnp.concatenate([high, high, middle, high, middle, low], 0)
        here = raw[own]
        pivot = over_rows(here[0][0], 0)
        for c in range(SUB):
            here_row = sub == c
            inverse = pl.reciprocal(pivot, approx=True)
            m_re = jnp.where(here_row, -1.0, here[c][0]) * inverse
            m_im = jnp.where(here_row, 0.0, here[c][1]) * inverse
            keep = jnp.where(here_row, head, keep)
            keep_turned = jnp.where(here_row, turned, keep_turned)
            keep_pivot = jnp.where(here_row, pivot, keep_pivot)
            for later in range(c + 1, SUB):
                re, im = here[later]
                u_re, u_im = over_rows(re, c), over_rows(im, c)
                if later == c + 1:
                    loss = (u_re * inverse) * u_re + (u_im * inverse) * u_im
                    pivot = over_rows(re, c + 1) - loss
                here[later] = (
                    jnp.where(here_row, 0.0, re) - m_re * u_re + m_im * u_im,
                    jnp.where(here_row, 0.0, im) - m_re * u_im - m_im * u_re,
                )
            on_re, on_im = lane == columns[c], lane == columns[c] + 1
            on_pair = on_re | on_im
            step_ref[c, :SUB, :] = head
            step_ref[c, SUB:, :] = turned
            p = jnp.where(on_pair, on_re.astype(jnp.float32), row_of(step_ref, c, c))
            q = jnp.where(on_pair, on_im.astype(jnp.float32), row_of(step_ref, c, SUB + c))
            cleared = here_row | on_pair
            head = jnp.where(cleared, 0.0, head) - (m_re * p + m_im * q)
            turned = jnp.where(cleared, 0.0, turned) - (m_re * q - m_im * p)
        final.append(keep)
        final_turned.append(keep_turned)
        pivots.append(keep_pivot)
        if own + 1 == count:
            break
        inside = (lane >= columns[0]) & (lane < columns[0] + 2 * SUB)
        solved = [(over_rows(head, c), over_rows(turned, c)) for c in range(SUB)]
        rows[own + 1] = jnp.where(inside, 0.0, rows[own + 1]) - tree_sum(
            [re * p + im * q for (re, im), (p, q) in zip(raw[own + 1], solved)]
        )
        far = range(own + 2, count)
        if far:
            high, middle, low = three_terms(jnp.concatenate([head, turned], 0))
            losses = lax.dot_general(
                columns_below, jnp.concatenate([high, middle, high, low, middle, high], 0),
                (((0,), (0,)), ((), ())), preferred_element_type=jnp.float32,
            )
            for i in far:
                rows[i] = jnp.where(inside, 0.0, rows[i]) - losses[i * SUB:(i + 1) * SUB]
    return final, final_turned, pivots


def modes_kernel(scale, slabs, x_ref, *refs):
    *given, modes_hbm, factor_hbm, basis_ref, step_ref, points_ref, modes_ref, factor_ref, sems = refs
    width = basis_ref.shape[0]
    size = width // 2
    count = size // SUB
    if given:
        gram = given[0][...]
        mine = x_ref[...]
    else:
        gram = gram_rows([x_ref[i * width:(i + 1) * width] for i in range(slabs)], basis_ref)
        own = lax.axis_index("space")
        mine = x_ref[pl.ds(pl.multiple_of(own * width, width), width)]
    points = jnp.transpose(mine)
    points_ref[...] = jnp.concatenate([points, points], 1)
    gram = gram * scale
    rows, turned, pivots = eliminate([gram[i * SUB:(i + 1) * SUB] for i in range(count)], step_ref)
    shape = rows[0].shape
    sub = lax.broadcasted_iota(jnp.int32, shape, 0)
    lane = lax.broadcasted_iota(jnp.int32, shape, 1)
    for i in range(count):
        own_rows = slice(i * SUB, (i + 1) * SUB)
        root = lax.rsqrt(pivots[i])
        diagonal = 2 * (i * SUB + sub)
        left = jnp.where(lane < diagonal, rows[i], (lane == diagonal).astype(jnp.float32))
        aside = jnp.where(lane < diagonal, turned[i], (lane == diagonal + 1).astype(jnp.float32))
        basis_ref[pl.ds(2 * i * SUB, SUB, stride=2), :] = left * root
        basis_ref[pl.ds(2 * i * SUB + 1, SUB, stride=2), :] = aside * root
        right = jnp.where(lane > diagonal + 1, rows[i], jnp.where(lane == diagonal, pivots[i], 0.0))
        parts = parts_apart(right * root, lane)
        factor_ref[0, own_rows, :] = parts[:, :size]
        factor_ref[1, own_rows, :] = parts[:, size:]
    copies = [pltpu.make_async_copy(factor_ref, factor_hbm, sems.at[0])]
    copies[0].start()
    basis = basis_ref[...]
    high = basis.astype(jnp.bfloat16)
    low = (basis - high.astype(jnp.float32)).astype(jnp.bfloat16)
    terms = jnp.concatenate([high, low], 1)
    each = modes_ref.shape[0] // PARTS
    for i in range(PARTS):
        part = slice(i * each, (i + 1) * each)
        modes_ref[part] = lax.dot_general(
            points_ref[part], terms, (((1,), (1,)), ((), ())),
            preferred_element_type=jnp.float32,
        )
        copies.append(pltpu.make_async_copy(modes_ref.at[part], modes_hbm.at[part], sems.at[1 + i]))
        copies[-1].start()
    for copy in copies:
        copy.wait()


def modes_and_factor(x, grams, width, slabs, scale):
    points = x.shape[1]
    size = width // 2
    return pl.pallas_call(
        functools.partial(modes_kernel, scale, slabs),
        out_shape=(
            jax.ShapeDtypeStruct((points, width), jnp.float32),
            jax.ShapeDtypeStruct((2, size, size), jnp.float32),
        ),
        in_specs=[pl.BlockSpec(memory_space=pltpu.VMEM)] * (1 + len(grams)),
        out_specs=(pl.BlockSpec(memory_space=pltpu.HBM),) * 2,
        scratch_shapes=[
            pltpu.VMEM((width, width), jnp.float32),
            pltpu.VMEM((SUB, 2 * SUB, width), jnp.float32),
            pltpu.VMEM((points, 2 * width), jnp.bfloat16),
            pltpu.VMEM((points, width), jnp.float32),
            pltpu.VMEM((2, size, size), jnp.float32),
            pltpu.SemaphoreType.DMA((1 + PARTS,)),
        ],
        compiler_params=pltpu.CompilerParams(vmem_limit_bytes=8 * 2**20),
        name="factor_and_modes",
    )(x, *grams)


def local(slabs, snapshots, row_scales, block_offsets, freq_index):
    freqs = freq_index.shape[0]
    points = snapshots.shape[1]
    width = 2 * block_offsets.shape[0] * lax.axis_size("blk")
    copies = slabs if slabs <= FEW_SLABS else 1
    spectra = block_spectra(copies, snapshots, row_scales, block_offsets, freq_index)
    chunks = spectra.reshape(copies * freqs, -1, points)
    swap = functools.partial(lax.all_to_all, split_axis=0, concat_axis=0, tiled=True)
    if copies == slabs:
        x = swap(chunks, ("space", "blk")).reshape(-1, points)
        grams = []
    else:
        x = swap(chunks, "blk").reshape(-1, points)
        grams = [lax.psum(complex_gram(x), "space")]
    modes, factor = modes_and_factor(x, grams, width, slabs, 1.0 / (points * slabs))
    return modes[None], factor[None]


def solution(mesh):
    return jax.shard_map(
        functools.partial(local, mesh.shape["space"]),
        mesh=mesh,
        in_specs=(P("blk", "space"), P("blk"), P("blk"), P()),
        out_specs=(P("blk", "space", None), P("blk", None, None, None)),
        check_vma=False,
    )
```

```python
import functools
import math

import jax
import jax.numpy as jnp
from jax import lax
from jax.experimental import pallas as pl
from jax.experimental.pallas import tpu as pltpu
from jax.sharding import PartitionSpec as P

NFFT = 512
SUB = 8
PIECE = 640
PARTS = 4
FEW_SLABS = 2
SIN_COEFS = (
    0.9999999765895043,
    -0.1666664763439475,
    0.008332899819203531,
    -0.0001980089750772882,
    2.5904879854375602e-06,
)


def cos_of_phase(phase):
    folded = jnp.abs((phase & (NFFT - 1)) - NFFT // 2) - NFFT // 4
    x = folded.astype(jnp.float32) * (2.0 * math.pi / NFFT)
    square = x * x
    total = jnp.full_like(x, SIN_COEFS[-1])
    for coef in SIN_COEFS[-2::-1]:
        total = total * square + coef
    return total * x


def spectra_kernel(
    snap_hbm, scales_hbm, offsets_hbm, freq_hbm, out_ref,
    snap_ref, scales_ref, offsets_ref, freq_ref, coef_ref, small_sems, snap_sems,
):
    snaps = snap_ref.shape[0]
    blocks = offsets_ref.shape[0]
    rows = 2 * blocks
    freqs = freq_ref.shape[0]
    small = [
        pltpu.make_async_copy(src, dst, small_sems.at[i])
        for i, (src, dst) in enumerate(
            ((offsets_hbm, offsets_ref), (freq_hbm, freq_ref), (scales_hbm, scales_ref))
        )
    ]
    pieces = [slice(at, min(at + PIECE, snaps)) for at in range(0, snaps, PIECE)]
    large = [
        pltpu.make_async_copy(snap_hbm.at[piece], snap_ref.at[piece], snap_sems.at[i])
        for i, piece in enumerate(pieces)
    ]
    for copy in small + large:
        copy.start()
    row = lax.broadcasted_iota(jnp.int32, (rows, snaps), 0)
    time = lax.broadcasted_iota(jnp.int32, (rows, snaps), 1)
    for copy in small:
        copy.wait()
    start = jnp.zeros((rows, snaps), jnp.int32)
    for b in range(blocks):
        start = jnp.where(row // 2 == b, offsets_ref[b], start)
    shifted = time - start
    hann = 0.5 - 0.5 * cos_of_phase(shifted)
    inside = (shifted >= 0) & (shifted < NFFT)
    scales = jnp.broadcast_to(scales_ref[...].reshape(1, snaps), (rows, snaps))
    weight = jnp.where(inside, hann * scales * (1.0 / math.sqrt(NFFT)), 0.0)
    quarter = NFFT // 4
    base = shifted[:, :quarter].astype(jnp.float32)
    turn = (row[:, :quarter] % 2) * quarter
    repeats = -(-snaps // NFFT)

    def rows_of(f):
        freq = freq_ref[f]
        phase = (base * freq.astype(jnp.float32)).astype(jnp.int32) + turn
        even, odd = cos_of_phase(phase), cos_of_phase(phase + quarter)
        tiles = [even]
        for j in range(1, 4):
            turns = (freq * j) & 3
            along = ((1 - (turns & 1)) * (1 - turns)).astype(jnp.float32)
            across = ((turns & 1) * (2 - turns)).astype(jnp.float32)
            tiles.append(even * along + odd * across)
        return jnp.concatenate(tiles * repeats, 1)[:, :snaps] * weight

    for f in range(0, freqs, 2):
        pair = jnp.concatenate([rows_of(f), rows_of(f + 1)], 0)
        coef_ref[f * rows:(f + 2) * rows, :] = pair.astype(jnp.bfloat16)
    for copy in large:
        copy.wait()
    total = jnp.dot(coef_ref[...], snap_ref[...], preferred_element_type=jnp.float32)
    result = total.astype(jnp.bfloat16)
    for copy in range(out_ref.shape[0]):
        out_ref[copy] = result


def block_spectra(copies, snapshots, row_scales, block_offsets, freq_index):
    snaps, points = snapshots.shape
    rows = 2 * block_offsets.shape[0] * freq_index.shape[0]
    pieces = -(-snaps // PIECE)
    return pl.pallas_call(
        spectra_kernel,
        out_shape=jax.ShapeDtypeStruct((copies, rows, points), jnp.bfloat16),
        in_specs=[pl.BlockSpec(memory_space=pltpu.HBM)] * 4,
        out_specs=pl.BlockSpec(memory_space=pltpu.VMEM),
        scratch_shapes=[
            pltpu.VMEM((snaps, points), jnp.bfloat16),
            pltpu.VMEM((snaps,), jnp.float32),
            pltpu.SMEM(block_offsets.shape, jnp.int32),
            pltpu.SMEM(freq_index.shape, jnp.int32),
            pltpu.VMEM((rows, snaps), jnp.bfloat16),
            pltpu.SemaphoreType.DMA((3,)),
            pltpu.SemaphoreType.DMA((pieces,)),
        ],
        compiler_params=pltpu.CompilerParams(vmem_limit_bytes=8 * 2**20),
        name="spectra",
    )(*(
        pltpu.with_memory_space_constraint(x, pltpu.HBM)
        for x in (snapshots, row_scales, block_offsets, freq_index)
    ))


def rotated(x, lane):
    axis = x.ndim - 1
    width = x.shape[axis]
    after = pltpu.roll(x, width - 1, axis)
    before = pltpu.roll(x, 1, axis)
    return jnp.where(lane % 2 == 0, -after, before)


def gram_rows(slabs, full_ref):
    width = full_ref.shape[0]
    full_ref[...] = sum(
        lax.dot_general(x, x, (((1,), (1,)), ((), ())), preferred_element_type=jnp.float32)
        for x in slabs
    )
    even = full_ref[pl.ds(0, width // 2, stride=2), :]
    odd = full_ref[pl.ds(1, width // 2, stride=2), :]
    lane = lax.broadcasted_iota(jnp.int32, odd.shape, 1)
    return even - rotated(odd, lane)


def gram_kernel(x_ref, out_ref, full_ref):
    out_ref[...] = gram_rows([x_ref[...]], full_ref)


def complex_gram(x):
    width = x.shape[0]
    return pl.pallas_call(
        gram_kernel,
        out_shape=jax.ShapeDtypeStruct((width // 2, width), jnp.float32),
        in_specs=[pl.BlockSpec(memory_space=pltpu.VMEM)],
        out_specs=pl.BlockSpec(memory_space=pltpu.VMEM),
        scratch_shapes=[pltpu.VMEM((width, width), jnp.float32)],
        compiler_params=pltpu.CompilerParams(vmem_limit_bytes=4 * 2**20),
        name="gram",
    )(x)


def tree_sum(terms):
    while len(terms) > 1:
        terms = [sum(terms[i:i + 2]) for i in range(0, len(terms), 2)]
    return terms[0]


def eliminate(rows, solved_ref, step_ref, column_ref):
    count = len(rows)
    shape = rows[0].shape
    sub = lax.broadcasted_iota(jnp.int32, shape, 0)
    lane = lax.broadcasted_iota(jnp.int32, shape, 1)

    def over_lanes(x, at):
        return jnp.broadcast_to(x[:, at:at + 1], shape)

    def over_rows(x, at):
        return jnp.broadcast_to(x[at:at + 1, :], shape)

    def row_of(ref, *at):
        return ref[(*at[:-1], pl.ds(at[-1], SUB, stride=0), slice(None))]

    rows = list(rows)
    solved_ref[...] = jnp.zeros_like(solved_ref)
    final, final_turned, pivots = [], [], []
    for own in range(count):
        head, turned = rows[own], rotated(rows[own], lane)
        keep, keep_turned, keep_pivot = head, turned, jnp.ones(shape, jnp.float32)
        columns = [2 * (own * SUB + c) for c in range(SUB)]
        raw = {
            i: [(over_lanes(rows[i], at), over_lanes(rows[i], at + 1)) for at in columns]
            for i in range(own, min(own + 2, count))
        }
        here = raw[own]
        pivot = over_rows(here[0][0], 0)
        for c in range(SUB):
            here_row = sub == c
            inverse = pl.reciprocal(pivot, approx=True)
            m_re = jnp.where(here_row, -1.0, here[c][0]) * inverse
            m_im = jnp.where(here_row, 0.0, here[c][1]) * inverse
            keep = jnp.where(here_row, head, keep)
            keep_turned = jnp.where(here_row, turned, keep_turned)
            keep_pivot = jnp.where(here_row, pivot, keep_pivot)
            for later in range(c + 1, SUB):
                re, im = here[later]
                column_ref[c, later, :SUB, :] = re
                column_ref[c, later, SUB:, :] = im
                u_re, u_im = row_of(column_ref, c, later, c), row_of(column_ref, c, later, SUB + c)
                if later == c + 1:
                    loss = (u_re * inverse) * u_re + (u_im * inverse) * u_im
                    pivot = row_of(column_ref, c, later, c + 1) - loss
                here[later] = (
                    jnp.where(here_row, 0.0, re) - m_re * u_re + m_im * u_im,
                    jnp.where(here_row, 0.0, im) - m_re * u_im - m_im * u_re,
                )
            on_re, on_im = lane == columns[c], lane == columns[c] + 1
            on_pair = on_re | on_im
            step_ref[c, :SUB, :] = head
            step_ref[c, SUB:, :] = turned
            p = jnp.where(on_pair, on_re.astype(jnp.float32), row_of(step_ref, c, c))
            q = jnp.where(on_pair, on_im.astype(jnp.float32), row_of(step_ref, c, SUB + c))
            cleared = here_row | on_pair
            head = jnp.where(cleared, 0.0, head) - (m_re * p + m_im * q)
            turned = jnp.where(cleared, 0.0, turned) - (m_re * q - m_im * p)
        final.append(keep)
        final_turned.append(keep_turned)
        pivots.append(keep_pivot)
        if own + 1 == count:
            break
        inside = (lane >= columns[0]) & (lane < columns[0] + 2 * SUB)
        solved_ref[pl.ds(columns[0], SUB, stride=2), :] = head
        solved_ref[pl.ds(columns[0] + 1, SUB, stride=2), :] = turned
        solved = [(row_of(solved_ref, at), row_of(solved_ref, at + 1)) for at in columns]
        rows[own + 1] = jnp.where(inside, 0.0, rows[own + 1]) - tree_sum(
            [re * p + im * q for (re, im), (p, q) in zip(raw[own + 1], solved)]
        )
        far = range(own + 2, count)
        if far:
            losses = jnp.dot(
                jnp.concatenate([jnp.where(inside, rows[i], 0.0) for i in far], 0), solved_ref[...],
                precision=lax.Precision.HIGHEST, preferred_element_type=jnp.float32,
            )
            for at, i in enumerate(far):
                loss = losses[at * SUB:(at + 1) * SUB]
                rows[i] = jnp.where(inside, 0.0, rows[i]) - loss
    return final, final_turned, pivots


def modes_kernel(scale, slabs, x_ref, *refs):
    *given, modes_hbm, factor_hbm, basis_ref, solved_ref, step_ref, column_ref = refs[:-4]
    points_ref, modes_ref, factor_ref, sems = refs[-4:]
    width = basis_ref.shape[0]
    size = width // 2
    count = size // SUB
    if given:
        gram = given[0][...]
        mine = x_ref[...]
    else:
        gram = gram_rows([x_ref[i * width:(i + 1) * width] for i in range(slabs)], basis_ref)
        own = lax.axis_index("space")
        mine = x_ref[pl.ds(pl.multiple_of(own * width, width), width)]
    points = jnp.transpose(mine)
    points_ref[...] = jnp.concatenate([points, points], 1)
    gram = gram * scale
    rows, turned, pivots = eliminate([gram[i * SUB:(i + 1) * SUB] for i in range(count)], solved_ref, step_ref, column_ref)
    shape = rows[0].shape
    sub = lax.broadcasted_iota(jnp.int32, shape, 0)
    lane = lax.broadcasted_iota(jnp.int32, shape, 1)
    pick = jnp.where(lane < size, 2 * lane, 2 * (lane - size) + 1)
    for i in range(count):
        own_rows = slice(i * SUB, (i + 1) * SUB)
        root = lax.rsqrt(pivots[i])
        diagonal = 2 * (i * SUB + sub)
        left = jnp.where(lane < diagonal, rows[i], (lane == diagonal).astype(jnp.float32))
        aside = jnp.where(lane < diagonal, turned[i], (lane == diagonal + 1).astype(jnp.float32))
        basis_ref[pl.ds(2 * i * SUB, SUB, stride=2), :] = left * root
        basis_ref[pl.ds(2 * i * SUB + 1, SUB, stride=2), :] = aside * root
        right = jnp.where(lane > diagonal + 1, rows[i], jnp.where(lane == diagonal, pivots[i], 0.0))
        parts = jnp.take_along_axis(right * root, pick, axis=1)
        factor_ref[0, own_rows, :] = parts[:, :size]
        factor_ref[1, own_rows, :] = parts[:, size:]
    copies = [pltpu.make_async_copy(factor_ref, factor_hbm, sems.at[0])]
    copies[0].start()
    basis = basis_ref[...]
    high = basis.astype(jnp.bfloat16)
    low = (basis - high.astype(jnp.float32)).astype(jnp.bfloat16)
    terms = jnp.concatenate([high, low], 1)
    each = modes_ref.shape[0] // PARTS
    for i in range(PARTS):
        part = slice(i * each, (i + 1) * each)
        modes_ref[part] = lax.dot_general(
            points_ref[part], terms, (((1,), (1,)), ((), ())),
            preferred_element_type=jnp.float32,
        )
        copies.append(pltpu.make_async_copy(modes_ref.at[part], modes_hbm.at[part], sems.at[1 + i]))
        copies[-1].start()
    for copy in copies:
        copy.wait()


def modes_and_factor(x, grams, width, slabs, scale):
    points = x.shape[1]
    size = width // 2
    return pl.pallas_call(
        functools.partial(modes_kernel, scale, slabs),
        out_shape=(
            jax.ShapeDtypeStruct((points, width), jnp.float32),
            jax.ShapeDtypeStruct((2, size, size), jnp.float32),
        ),
        in_specs=[pl.BlockSpec(memory_space=pltpu.VMEM)] * (1 + len(grams)),
        out_specs=(pl.BlockSpec(memory_space=pltpu.HBM),) * 2,
        scratch_shapes=[
            pltpu.VMEM((width, width), jnp.float32),
            pltpu.VMEM((width, width), jnp.float32),
            pltpu.VMEM((SUB, 2 * SUB, width), jnp.float32),
            pltpu.VMEM((SUB, SUB, 2 * SUB, width), jnp.float32),
            pltpu.VMEM((points, 2 * width), jnp.bfloat16),
            pltpu.VMEM((points, width), jnp.float32),
            pltpu.VMEM((2, size, size), jnp.float32),
            pltpu.SemaphoreType.DMA((1 + PARTS,)),
        ],
        compiler_params=pltpu.CompilerParams(vmem_limit_bytes=8 * 2**20),
        name="factor_and_modes",
    )(x, *grams)


def local(slabs, snapshots, row_scales, block_offsets, freq_index):
    freqs = freq_index.shape[0]
    points = snapshots.shape[1]
    width = 2 * block_offsets.shape[0] * lax.axis_size("blk")
    copies = slabs if slabs <= FEW_SLABS else 1
    spectra = block_spectra(copies, snapshots, row_scales, block_offsets, freq_index)
    chunks = spectra.reshape(copies * freqs, -1, points)
    swap = functools.partial(lax.all_to_all, split_axis=0, concat_axis=0, tiled=True)
    if copies == slabs:
        x = swap(chunks, ("space", "blk")).reshape(-1, points)
        grams = []
    else:
        x = swap(chunks, "blk").reshape(-1, points)
        grams = [lax.psum(complex_gram(x), "space")]
    modes, factor = modes_and_factor(x, grams, width, slabs, 1.0 / (points * slabs))
    return modes[None], factor[None]


def solution(mesh):
    return jax.shard_map(
        functools.partial(local, mesh.shape["space"]),
        mesh=mesh,
        in_specs=(P("blk", "space"), P("blk"), P("blk"), P()),
        out_specs=(P("blk", "space", None), P("blk", None, None, None)),
        check_vma=False,
    )
```

```python
import functools
import math

import jax
import jax.numpy as jnp
from jax import lax
from jax.experimental import pallas as pl
from jax.experimental.pallas import tpu as pltpu
from jax.sharding import PartitionSpec as P

NFFT = 512
SUB = 8
PIECE = 640
PARTS = 4
FEW_SLABS = 2
SIN_COEFS = (
    0.9999999765895043,
    -0.1666664763439475,
    0.008332899819203531,
    -0.0001980089750772882,
    2.5904879854375602e-06,
)


def cos_of_phase(phase):
    folded = jnp.abs((phase & (NFFT - 1)) - NFFT // 2) - NFFT // 4
    x = folded.astype(jnp.float32) * (2.0 * math.pi / NFFT)
    square = x * x
    total = jnp.full_like(x, SIN_COEFS[-1])
    for coef in SIN_COEFS[-2::-1]:
        total = total * square + coef
    return total * x


def spectra_kernel(
    snap_hbm, scales_hbm, offsets_hbm, freq_hbm, out_ref,
    snap_ref, scales_ref, offsets_ref, freq_ref, coef_ref, small_sems, snap_sems,
):
    snaps = snap_ref.shape[0]
    blocks = offsets_ref.shape[0]
    rows = 2 * blocks
    freqs = freq_ref.shape[0]
    small = [
        pltpu.make_async_copy(src, dst, small_sems.at[i])
        for i, (src, dst) in enumerate(
            ((offsets_hbm, offsets_ref), (freq_hbm, freq_ref), (scales_hbm, scales_ref))
        )
    ]
    pieces = [slice(at, min(at + PIECE, snaps)) for at in range(0, snaps, PIECE)]
    large = [
        pltpu.make_async_copy(snap_hbm.at[piece], snap_ref.at[piece], snap_sems.at[i])
        for i, piece in enumerate(pieces)
    ]
    for copy in small + large:
        copy.start()
    row = lax.broadcasted_iota(jnp.int32, (rows, snaps), 0)
    time = lax.broadcasted_iota(jnp.int32, (rows, snaps), 1)
    for copy in small:
        copy.wait()
    start = jnp.zeros((rows, snaps), jnp.int32)
    for b in range(blocks):
        start = jnp.where(row // 2 == b, offsets_ref[b], start)
    shifted = time - start
    hann = 0.5 - 0.5 * cos_of_phase(shifted)
    inside = (shifted >= 0) & (shifted < NFFT)
    scales = jnp.broadcast_to(scales_ref[...].reshape(1, snaps), (rows, snaps))
    weight = jnp.where(inside, hann * scales * (1.0 / math.sqrt(NFFT)), 0.0)
    quarter = NFFT // 4
    base = shifted[:, :quarter].astype(jnp.float32)
    turn = (row[:, :quarter] % 2) * quarter
    repeats = -(-snaps // NFFT)

    def rows_of(f):
        freq = freq_ref[f]
        phase = (base * freq.astype(jnp.float32)).astype(jnp.int32) + turn
        even, odd = cos_of_phase(phase), cos_of_phase(phase + quarter)
        tiles = [even]
        for j in range(1, 4):
            turns = (freq * j) & 3
            along = ((1 - (turns & 1)) * (1 - turns)).astype(jnp.float32)
            across = ((turns & 1) * (2 - turns)).astype(jnp.float32)
            tiles.append(even * along + odd * across)
        return jnp.concatenate(tiles * repeats, 1)[:, :snaps] * weight

    for f in range(0, freqs, 2):
        pair = jnp.concatenate([rows_of(f), rows_of(f + 1)], 0)
        coef_ref[f * rows:(f + 2) * rows, :] = pair.astype(jnp.bfloat16)
    for copy in large:
        copy.wait()
    total = jnp.dot(coef_ref[...], snap_ref[...], preferred_element_type=jnp.float32)
    result = total.astype(jnp.bfloat16)
    for copy in range(out_ref.shape[0]):
        out_ref[copy] = result


def block_spectra(copies, snapshots, row_scales, block_offsets, freq_index):
    snaps, points = snapshots.shape
    rows = 2 * block_offsets.shape[0] * freq_index.shape[0]
    pieces = -(-snaps // PIECE)
    return pl.pallas_call(
        spectra_kernel,
        out_shape=jax.ShapeDtypeStruct((copies, rows, points), jnp.bfloat16),
        in_specs=[pl.BlockSpec(memory_space=pltpu.HBM)] * 4,
        out_specs=pl.BlockSpec(memory_space=pltpu.VMEM),
        scratch_shapes=[
            pltpu.VMEM((snaps, points), jnp.bfloat16),
            pltpu.VMEM((snaps,), jnp.float32),
            pltpu.SMEM(block_offsets.shape, jnp.int32),
            pltpu.SMEM(freq_index.shape, jnp.int32),
            pltpu.VMEM((rows, snaps), jnp.bfloat16),
            pltpu.SemaphoreType.DMA((3,)),
            pltpu.SemaphoreType.DMA((pieces,)),
        ],
        compiler_params=pltpu.CompilerParams(vmem_limit_bytes=8 * 2**20),
        name="spectra",
    )(*(
        pltpu.with_memory_space_constraint(x, pltpu.HBM)
        for x in (snapshots, row_scales, block_offsets, freq_index)
    ))


def rotated(x, lane):
    axis = x.ndim - 1
    width = x.shape[axis]
    after = pltpu.roll(x, width - 1, axis)
    before = pltpu.roll(x, 1, axis)
    return jnp.where(lane % 2 == 0, -after, before)


def gram_rows(slabs, full_ref):
    width = full_ref.shape[0]
    full_ref[...] = sum(
        lax.dot_general(x, x, (((1,), (1,)), ((), ())), preferred_element_type=jnp.float32)
        for x in slabs
    )
    even = full_ref[pl.ds(0, width // 2, stride=2), :]
    odd = full_ref[pl.ds(1, width // 2, stride=2), :]
    lane = lax.broadcasted_iota(jnp.int32, odd.shape, 1)
    return even - rotated(odd, lane)


def gram_kernel(x_ref, out_ref, full_ref):
    out_ref[...] = gram_rows([x_ref[...]], full_ref)


def complex_gram(x):
    width = x.shape[0]
    return pl.pallas_call(
        gram_kernel,
        out_shape=jax.ShapeDtypeStruct((width // 2, width), jnp.float32),
        in_specs=[pl.BlockSpec(memory_space=pltpu.VMEM)],
        out_specs=pl.BlockSpec(memory_space=pltpu.VMEM),
        scratch_shapes=[pltpu.VMEM((width, width), jnp.float32)],
        compiler_params=pltpu.CompilerParams(vmem_limit_bytes=4 * 2**20),
        name="gram",
    )(x)


def tree_sum(terms):
    while len(terms) > 1:
        terms = [sum(terms[i:i + 2]) for i in range(0, len(terms), 2)]
    return terms[0]


def eliminate(rows_ref, final_ref, turned_ref, pivots_ref, solved_ref):
    size = final_ref.shape[0]
    width = final_ref.shape[1]
    shape = (SUB, width)
    sub = lax.broadcasted_iota(jnp.int32, shape, 0)
    lane = lax.broadcasted_iota(jnp.int32, shape, 1)
    all_rows = lax.broadcasted_iota(jnp.int32, (size, width), 0)
    all_lanes = lax.broadcasted_iota(jnp.int32, (size, width), 1)
    solved_ref[...] = jnp.zeros_like(solved_ref)

    def over_lanes(x, at):
        return jnp.broadcast_to(x[:, at:at + 1], shape)

    def over_rows(x, at):
        return jnp.broadcast_to(x[at:at + 1, :], shape)

    def block_at(i):
        return pl.ds(pl.multiple_of(i * SUB, SUB), SUB)

    def columns_of(x, start):
        moved = pltpu.roll(x, lax.rem(width - start, width), 1)
        return [(over_lanes(moved, 2 * c), over_lanes(moved, 2 * c + 1)) for c in range(SUB)]

    def panel(own, carry):
        start = own * 2 * SUB
        before = start - 2 * SUB
        head = rows_ref[block_at(own), :]
        every = rows_ref[:size, :]
        inside = (all_rows >= (own + 1) * SUB) & (all_lanes >= before) & (all_lanes < start)
        losses = jnp.dot(
            jnp.where(inside, every, 0.0), solved_ref[...],
            precision=lax.Precision.HIGHEST, preferred_element_type=jnp.float32,
        )
        rows_ref[:size, :] = jnp.where(inside, 0.0, every) - losses
        turned = rotated(head, lane)
        here = columns_of(head, start)
        keep, keep_turned, keep_pivot = head, turned, jnp.ones(shape, jnp.float32)
        pivot = over_rows(here[0][0], 0)
        for c in range(SUB):
            here_row = sub == c
            inverse = pl.reciprocal(pivot, approx=True)
            m_re = jnp.where(here_row, -1.0, here[c][0]) * inverse
            m_im = jnp.where(here_row, 0.0, here[c][1]) * inverse
            keep = jnp.where(here_row, head, keep)
            keep_turned = jnp.where(here_row, turned, keep_turned)
            keep_pivot = jnp.where(here_row, pivot, keep_pivot)
            for later in range(c + 1, SUB):
                re, im = here[later]
                u_re, u_im = over_rows(re, c), over_rows(im, c)
                if later == c + 1:
                    loss = (u_re * inverse) * u_re + (u_im * inverse) * u_im
                    pivot = over_rows(re, c + 1) - loss
                here[later] = (
                    jnp.where(here_row, 0.0, re) - m_re * u_re + m_im * u_im,
                    jnp.where(here_row, 0.0, im) - m_re * u_im - m_im * u_re,
                )
            on_re, on_im = lane == start + 2 * c, lane == start + 2 * c + 1
            on_pair = on_re | on_im
            p = jnp.where(on_pair, on_re.astype(jnp.float32), over_rows(head, c))
            q = jnp.where(on_pair, on_im.astype(jnp.float32), over_rows(turned, c))
            cleared = here_row | on_pair
            head = jnp.where(cleared, 0.0, head) - (m_re * p + m_im * q)
            turned = jnp.where(cleared, 0.0, turned) - (m_re * q - m_im * p)
        final_ref[block_at(own), :] = keep
        turned_ref[block_at(own), :] = keep_turned
        pivots_ref[block_at(own), :] = keep_pivot
        solved_ref[pl.ds(pl.multiple_of(start, 2 * SUB), SUB, stride=2), :] = head
        solved_ref[pl.ds(pl.multiple_of(start, 2 * SUB) + 1, SUB, stride=2), :] = turned
        following = rows_ref[block_at(own + 1), :]
        raw = columns_of(following, start)
        within = (lane >= start) & (lane < start + 2 * SUB)
        rows_ref[block_at(own + 1), :] = jnp.where(within, 0.0, following) - tree_sum(
            [re * over_rows(head, c) + im * over_rows(turned, c) for c, (re, im) in enumerate(raw)]
        )
        return carry

    lax.fori_loop(0, size // SUB, panel, 0)


def modes_kernel(scale, slabs, x_ref, *refs):
    *given, modes_hbm, factor_hbm, basis_ref, rows_ref, final_ref, turned_ref, pivots_ref = refs[:-5]
    solved_ref, points_ref, modes_ref, factor_ref, sems = refs[-5:]
    width = basis_ref.shape[0]
    size = width // 2
    count = size // SUB
    if given:
        gram = given[0][...]
        mine = x_ref[...]
    else:
        gram = gram_rows([x_ref[i * width:(i + 1) * width] for i in range(slabs)], basis_ref)
        own = lax.axis_index("space")
        mine = x_ref[pl.ds(pl.multiple_of(own * width, width), width)]
    points = jnp.transpose(mine)
    points_ref[...] = jnp.concatenate([points, points], 1)
    rows_ref[:size, :] = gram * scale
    rows_ref[size:, :] = jnp.zeros((SUB, width), jnp.float32)
    eliminate(rows_ref, final_ref, turned_ref, pivots_ref, solved_ref)
    rows, turned, pivots = [
        [ref[i * SUB:(i + 1) * SUB, :] for i in range(count)] for ref in (final_ref, turned_ref, pivots_ref)
    ]
    shape = rows[0].shape
    sub = lax.broadcasted_iota(jnp.int32, shape, 0)
    lane = lax.broadcasted_iota(jnp.int32, shape, 1)
    pick = jnp.where(lane < size, 2 * lane, 2 * (lane - size) + 1)
    for i in range(count):
        own_rows = slice(i * SUB, (i + 1) * SUB)
        root = lax.rsqrt(pivots[i])
        diagonal = 2 * (i * SUB + sub)
        left = jnp.where(lane < diagonal, rows[i], (lane == diagonal).astype(jnp.float32))
        aside = jnp.where(lane < diagonal, turned[i], (lane == diagonal + 1).astype(jnp.float32))
        basis_ref[pl.ds(2 * i * SUB, SUB, stride=2), :] = left * root
        basis_ref[pl.ds(2 * i * SUB + 1, SUB, stride=2), :] = aside * root
        right = jnp.where(lane > diagonal + 1, rows[i], jnp.where(lane == diagonal, pivots[i], 0.0))
        parts = jnp.take_along_axis(right * root, pick, axis=1)
        factor_ref[0, own_rows, :] = parts[:, :size]
        factor_ref[1, own_rows, :] = parts[:, size:]
    copies = [pltpu.make_async_copy(factor_ref, factor_hbm, sems.at[0])]
    copies[0].start()
    basis = basis_ref[...]
    high = basis.astype(jnp.bfloat16)
    low = (basis - high.astype(jnp.float32)).astype(jnp.bfloat16)
    terms = jnp.concatenate([high, low], 1)
    each = modes_ref.shape[0] // PARTS
    for i in range(PARTS):
        part = slice(i * each, (i + 1) * each)
        modes_ref[part] = lax.dot_general(
            points_ref[part], terms, (((1,), (1,)), ((), ())),
            preferred_element_type=jnp.float32,
        )
        copies.append(pltpu.make_async_copy(modes_ref.at[part], modes_hbm.at[part], sems.at[1 + i]))
        copies[-1].start()
    for copy in copies:
        copy.wait()


def modes_and_factor(x, grams, width, slabs, scale):
    points = x.shape[1]
    size = width // 2
    return pl.pallas_call(
        functools.partial(modes_kernel, scale, slabs),
        out_shape=(
            jax.ShapeDtypeStruct((points, width), jnp.float32),
            jax.ShapeDtypeStruct((2, size, size), jnp.float32),
        ),
        in_specs=[pl.BlockSpec(memory_space=pltpu.VMEM)] * (1 + len(grams)),
        out_specs=(pl.BlockSpec(memory_space=pltpu.HBM),) * 2,
        scratch_shapes=[
            pltpu.VMEM((width, width), jnp.float32),
            pltpu.VMEM((size + SUB, width), jnp.float32),
            pltpu.VMEM((size, width), jnp.float32),
            pltpu.VMEM((size, width), jnp.float32),
            pltpu.VMEM((size, width), jnp.float32),
            pltpu.VMEM((width, width), jnp.float32),
            pltpu.VMEM((points, 2 * width), jnp.bfloat16),
            pltpu.VMEM((points, width), jnp.float32),
            pltpu.VMEM((2, size, size), jnp.float32),
            pltpu.SemaphoreType.DMA((1 + PARTS,)),
        ],
        compiler_params=pltpu.CompilerParams(vmem_limit_bytes=8 * 2**20),
        name="factor_and_modes",
    )(x, *grams)


def local(slabs, snapshots, row_scales, block_offsets, freq_index):
    freqs = freq_index.shape[0]
    points = snapshots.shape[1]
    width = 2 * block_offsets.shape[0] * lax.axis_size("blk")
    copies = slabs if slabs <= FEW_SLABS else 1
    spectra = block_spectra(copies, snapshots, row_scales, block_offsets, freq_index)
    chunks = spectra.reshape(copies * freqs, -1, points)
    swap = functools.partial(lax.all_to_all, split_axis=0, concat_axis=0, tiled=True)
    if copies == slabs:
        x = swap(chunks, ("space", "blk")).reshape(-1, points)
        grams = []
    else:
        x = swap(chunks, "blk").reshape(-1, points)
        grams = [lax.psum(complex_gram(x), "space")]
    modes, factor = modes_and_factor(x, grams, width, slabs, 1.0 / (points * slabs))
    return modes[None], factor[None]


def solution(mesh):
    return jax.shard_map(
        functools.partial(local, mesh.shape["space"]),
        mesh=mesh,
        in_specs=(P("blk", "space"), P("blk"), P("blk"), P()),
        out_specs=(P("blk", "space", None), P("blk", None, None, None)),
        check_vma=False,
    )
```

```python
import functools
import math

import jax
import jax.numpy as jnp
from jax import lax
from jax.experimental import pallas as pl
from jax.experimental.pallas import tpu as pltpu
from jax.sharding import PartitionSpec as P

NFFT = 512
SUB = 8
NEAR = 2
PIECE = 640
PARTS = 4
FEW_SLABS = 2
SIN_COEFS = (
    0.9999999765895043,
    -0.1666664763439475,
    0.008332899819203531,
    -0.0001980089750772882,
    2.5904879854375602e-06,
)


def cos_of_phase(phase):
    folded = jnp.abs((phase & (NFFT - 1)) - NFFT // 2) - NFFT // 4
    x = folded.astype(jnp.float32) * (2.0 * math.pi / NFFT)
    square = x * x
    total = jnp.full_like(x, SIN_COEFS[-1])
    for coef in SIN_COEFS[-2::-1]:
        total = total * square + coef
    return total * x


def spectra_kernel(
    snap_hbm, scales_hbm, offsets_hbm, freq_hbm, out_ref,
    snap_ref, scales_ref, offsets_ref, freq_ref, coef_ref, small_sems, snap_sems,
):
    snaps = snap_ref.shape[0]
    blocks = offsets_ref.shape[0]
    rows = 2 * blocks
    freqs = freq_ref.shape[0]
    small = [
        pltpu.make_async_copy(src, dst, small_sems.at[i])
        for i, (src, dst) in enumerate(
            ((offsets_hbm, offsets_ref), (freq_hbm, freq_ref), (scales_hbm, scales_ref))
        )
    ]
    pieces = [slice(at, min(at + PIECE, snaps)) for at in range(0, snaps, PIECE)]
    large = [
        pltpu.make_async_copy(snap_hbm.at[piece], snap_ref.at[piece], snap_sems.at[i])
        for i, piece in enumerate(pieces)
    ]
    for copy in small + large:
        copy.start()
    row = lax.broadcasted_iota(jnp.int32, (rows, snaps), 0)
    time = lax.broadcasted_iota(jnp.int32, (rows, snaps), 1)
    for copy in small:
        copy.wait()
    start = jnp.zeros((rows, snaps), jnp.int32)
    for b in range(blocks):
        start = jnp.where(row // 2 == b, offsets_ref[b], start)
    shifted = time - start
    hann = 0.5 - 0.5 * cos_of_phase(shifted)
    inside = (shifted >= 0) & (shifted < NFFT)
    scales = jnp.broadcast_to(scales_ref[...].reshape(1, snaps), (rows, snaps))
    weight = jnp.where(inside, hann * scales * (1.0 / math.sqrt(NFFT)), 0.0)
    quarter = NFFT // 4
    base = shifted[:, :quarter].astype(jnp.float32)
    turn = (row[:, :quarter] % 2) * quarter
    repeats = -(-snaps // NFFT)

    def rows_of(f):
        freq = freq_ref[f]
        phase = (base * freq.astype(jnp.float32)).astype(jnp.int32) + turn
        even, odd = cos_of_phase(phase), cos_of_phase(phase + quarter)
        tiles = [even]
        for j in range(1, 4):
            turns = (freq * j) & 3
            along = ((1 - (turns & 1)) * (1 - turns)).astype(jnp.float32)
            across = ((turns & 1) * (2 - turns)).astype(jnp.float32)
            tiles.append(even * along + odd * across)
        return jnp.concatenate(tiles * repeats, 1)[:, :snaps] * weight

    for f in range(0, freqs, 2):
        pair = jnp.concatenate([rows_of(f), rows_of(f + 1)], 0)
        coef_ref[f * rows:(f + 2) * rows, :] = pair.astype(jnp.bfloat16)
    for copy in large:
        copy.wait()
    total = jnp.dot(coef_ref[...], snap_ref[...], preferred_element_type=jnp.float32)
    result = total.astype(jnp.bfloat16)
    for copy in range(out_ref.shape[0]):
        out_ref[copy] = result


def block_spectra(copies, snapshots, row_scales, block_offsets, freq_index):
    snaps, points = snapshots.shape
    rows = 2 * block_offsets.shape[0] * freq_index.shape[0]
    pieces = -(-snaps // PIECE)
    return pl.pallas_call(
        spectra_kernel,
        out_shape=jax.ShapeDtypeStruct((copies, rows, points), jnp.bfloat16),
        in_specs=[pl.BlockSpec(memory_space=pltpu.HBM)] * 4,
        out_specs=pl.BlockSpec(memory_space=pltpu.VMEM),
        scratch_shapes=[
            pltpu.VMEM((snaps, points), jnp.bfloat16),
            pltpu.VMEM((snaps,), jnp.float32),
            pltpu.SMEM(block_offsets.shape, jnp.int32),
            pltpu.SMEM(freq_index.shape, jnp.int32),
            pltpu.VMEM((rows, snaps), jnp.bfloat16),
            pltpu.SemaphoreType.DMA((3,)),
            pltpu.SemaphoreType.DMA((pieces,)),
        ],
        compiler_params=pltpu.CompilerParams(vmem_limit_bytes=8 * 2**20),
        name="spectra",
    )(*(
        pltpu.with_memory_space_constraint(x, pltpu.HBM)
        for x in (snapshots, row_scales, block_offsets, freq_index)
    ))


def rotated(x, lane):
    axis = x.ndim - 1
    width = x.shape[axis]
    after = pltpu.roll(x, width - 1, axis)
    before = pltpu.roll(x, 1, axis)
    return jnp.where(lane % 2 == 0, -after, before)


def gram_rows(slabs, full_ref):
    width = full_ref.shape[0]
    full_ref[...] = sum(
        lax.dot_general(x, x, (((1,), (1,)), ((), ())), preferred_element_type=jnp.float32)
        for x in slabs
    )
    even = full_ref[pl.ds(0, width // 2, stride=2), :]
    odd = full_ref[pl.ds(1, width // 2, stride=2), :]
    lane = lax.broadcasted_iota(jnp.int32, odd.shape, 1)
    return even - rotated(odd, lane)


def gram_kernel(x_ref, out_ref, full_ref):
    out_ref[...] = gram_rows([x_ref[...]], full_ref)


def complex_gram(x):
    width = x.shape[0]
    return pl.pallas_call(
        gram_kernel,
        out_shape=jax.ShapeDtypeStruct((width // 2, width), jnp.float32),
        in_specs=[pl.BlockSpec(memory_space=pltpu.VMEM)],
        out_specs=pl.BlockSpec(memory_space=pltpu.VMEM),
        scratch_shapes=[pltpu.VMEM((width, width), jnp.float32)],
        compiler_params=pltpu.CompilerParams(vmem_limit_bytes=4 * 2**20),
        name="gram",
    )(x)


def tree_sum(terms):
    while len(terms) > 1:
        terms = [sum(terms[i:i + 2]) for i in range(0, len(terms), 2)]
    return terms[0]


def eliminate(rows, solved_ref, step_ref, done_ref):
    count = len(rows)
    shape = rows[0].shape
    sub = lax.broadcasted_iota(jnp.int32, shape, 0)
    lane = lax.broadcasted_iota(jnp.int32, shape, 1)

    def over_lanes(x, at):
        return jnp.broadcast_to(x[:, at:at + 1], shape)

    def over_rows(x, at):
        return jnp.broadcast_to(x[at:at + 1, :], shape)

    def row_of(ref, *at):
        return ref[(*at[:-1], pl.ds(at[-1], SUB, stride=0), slice(None))]

    rows = list(rows)
    final, final_turned, pivots = [], [], []
    for own in range(count):
        head, turned = rows[own], rotated(rows[own], lane)
        done = slice(own * SUB, (own + 1) * SUB)
        columns = [2 * (own * SUB + c) for c in range(SUB)]
        raw = {
            i: [(over_lanes(rows[i], at), over_lanes(rows[i], at + 1)) for at in columns]
            for i in range(own, min(own + 1 + NEAR, count))
        }
        here = raw[own]
        pivot = over_rows(here[0][0], 0)
        for c in range(SUB):
            here_row = sub == c
            inverse = pl.reciprocal(pivot, approx=True)
            m_re = jnp.where(here_row, -1.0, here[c][0]) * inverse
            m_im = jnp.where(here_row, 0.0, here[c][1]) * inverse
            done_row = slice(own * SUB + c, own * SUB + c + 1)
            for place, value in enumerate((head, turned, pivot)):
                done_ref[place, done_row, :] = value[c:c + 1]
            for later in range(c + 1, SUB):
                re, im = here[later]
                u_re, u_im = over_rows(re, c), over_rows(im, c)
                if later == c + 1:
                    loss = (u_re * inverse) * u_re + (u_im * inverse) * u_im
                    pivot = over_rows(re, c + 1) - loss
                here[later] = (
                    jnp.where(here_row, 0.0, re) - m_re * u_re + m_im * u_im,
                    jnp.where(here_row, 0.0, im) - m_re * u_im - m_im * u_re,
                )
            on_re, on_im = lane == columns[c], lane == columns[c] + 1
            on_pair = on_re | on_im
            step_ref[c, :SUB, :] = head
            step_ref[c, SUB:, :] = turned
            p = jnp.where(on_pair, on_re.astype(jnp.float32), row_of(step_ref, c, c))
            q = jnp.where(on_pair, on_im.astype(jnp.float32), row_of(step_ref, c, SUB + c))
            cleared = here_row | on_pair
            head = jnp.where(cleared, 0.0, head) - (m_re * p + m_im * q)
            turned = jnp.where(cleared, 0.0, turned) - (m_re * q - m_im * p)
        final.append(done_ref[0, done, :])
        final_turned.append(done_ref[1, done, :])
        pivots.append(done_ref[2, done, :])
        if own + 1 == count:
            break
        inside = (lane >= columns[0]) & (lane < columns[0] + 2 * SUB)
        solved_ref[own, pl.ds(0, SUB, stride=2), :] = head
        solved_ref[own, pl.ds(1, SUB, stride=2), :] = turned
        solved = [(over_rows(head, c), over_rows(turned, c)) for c in range(SUB)]
        for i in range(own + 1, min(own + 1 + NEAR, count)):
            rows[i] = jnp.where(inside, 0.0, rows[i]) - tree_sum(
                [re * p + im * q for (re, im), (p, q) in zip(raw[i], solved)]
            )
        far = range(own + 1 + NEAR, count)
        if far:
            below = jnp.concatenate([rows[i] for i in far], 0)
            losses = jnp.dot(
                below[:, columns[0]:columns[0] + 2 * SUB], solved_ref[own],
                precision=lax.Precision.HIGHEST, preferred_element_type=jnp.float32,
            )
            for at, i in enumerate(far):
                loss = losses[at * SUB:(at + 1) * SUB]
                rows[i] = jnp.where(inside, 0.0, rows[i]) - loss
    return final, final_turned, pivots


def modes_kernel(scale, slabs, x_ref, *refs):
    *given, modes_hbm, factor_hbm, basis_ref, solved_ref, step_ref, done_ref = refs[:-4]
    points_ref, modes_ref, factor_ref, sems = refs[-4:]
    width = basis_ref.shape[0]
    size = width // 2
    count = size // SUB
    if given:
        gram = given[0][...]
        mine = x_ref[...]
    else:
        gram = gram_rows([x_ref[i * width:(i + 1) * width] for i in range(slabs)], basis_ref)
        own = lax.axis_index("space")
        mine = x_ref[pl.ds(pl.multiple_of(own * width, width), width)]
    points = jnp.transpose(mine)
    points_ref[...] = jnp.concatenate([points, points], 1)
    gram = gram * scale
    rows, turned, pivots = eliminate([gram[i * SUB:(i + 1) * SUB] for i in range(count)], solved_ref, step_ref, done_ref)
    shape = rows[0].shape
    sub = lax.broadcasted_iota(jnp.int32, shape, 0)
    lane = lax.broadcasted_iota(jnp.int32, shape, 1)
    pick = jnp.where(lane < size, 2 * lane, 2 * (lane - size) + 1)
    for i in range(count):
        own_rows = slice(i * SUB, (i + 1) * SUB)
        root = lax.rsqrt(pivots[i])
        diagonal = 2 * (i * SUB + sub)
        left = jnp.where(lane < diagonal, rows[i], (lane == diagonal).astype(jnp.float32))
        aside = jnp.where(lane < diagonal, turned[i], (lane == diagonal + 1).astype(jnp.float32))
        basis_ref[pl.ds(2 * i * SUB, SUB, stride=2), :] = left * root
        basis_ref[pl.ds(2 * i * SUB + 1, SUB, stride=2), :] = aside * root
        right = jnp.where(lane > diagonal + 1, rows[i], jnp.where(lane == diagonal, pivots[i], 0.0))
        parts = jnp.take_along_axis(right * root, pick, axis=1)
        factor_ref[0, own_rows, :] = parts[:, :size]
        factor_ref[1, own_rows, :] = parts[:, size:]
    copies = [pltpu.make_async_copy(factor_ref, factor_hbm, sems.at[0])]
    copies[0].start()
    basis = basis_ref[...]
    high = basis.astype(jnp.bfloat16)
    low = (basis - high.astype(jnp.float32)).astype(jnp.bfloat16)
    terms = jnp.concatenate([high, low], 1)
    each = modes_ref.shape[0] // PARTS
    for i in range(PARTS):
        part = slice(i * each, (i + 1) * each)
        modes_ref[part] = lax.dot_general(
            points_ref[part], terms, (((1,), (1,)), ((), ())),
            preferred_element_type=jnp.float32,
        )
        copies.append(pltpu.make_async_copy(modes_ref.at[part], modes_hbm.at[part], sems.at[1 + i]))
        copies[-1].start()
    for copy in copies:
        copy.wait()


def modes_and_factor(x, grams, width, slabs, scale):
    points = x.shape[1]
    size = width // 2
    return pl.pallas_call(
        functools.partial(modes_kernel, scale, slabs),
        out_shape=(
            jax.ShapeDtypeStruct((points, width), jnp.float32),
            jax.ShapeDtypeStruct((2, size, size), jnp.float32),
        ),
        in_specs=[pl.BlockSpec(memory_space=pltpu.VMEM)] * (1 + len(grams)),
        out_specs=(pl.BlockSpec(memory_space=pltpu.HBM),) * 2,
        scratch_shapes=[
            pltpu.VMEM((width, width), jnp.float32),
            pltpu.VMEM((size // SUB, 2 * SUB, width), jnp.float32),
            pltpu.VMEM((SUB, 2 * SUB, width), jnp.float32),
            pltpu.VMEM((3, size, width), jnp.float32),
            pltpu.VMEM((points, 2 * width), jnp.bfloat16),
            pltpu.VMEM((points, width), jnp.float32),
            pltpu.VMEM((2, size, size), jnp.float32),
            pltpu.SemaphoreType.DMA((1 + PARTS,)),
        ],
        compiler_params=pltpu.CompilerParams(vmem_limit_bytes=8 * 2**20),
        name="factor_and_modes",
    )(x, *grams)


def local(slabs, snapshots, row_scales, block_offsets, freq_index):
    freqs = freq_index.shape[0]
    points = snapshots.shape[1]
    width = 2 * block_offsets.shape[0] * lax.axis_size("blk")
    copies = slabs if slabs <= FEW_SLABS else 1
    spectra = block_spectra(copies, snapshots, row_scales, block_offsets, freq_index)
    chunks = spectra.reshape(copies * freqs, -1, points)
    swap = functools.partial(lax.all_to_all, split_axis=0, concat_axis=0, tiled=True)
    if copies == slabs:
        x = swap(chunks, ("space", "blk")).reshape(-1, points)
        grams = []
    else:
        x = swap(chunks, "blk").reshape(-1, points)
        grams = [lax.psum(complex_gram(x), "space")]
    modes, factor = modes_and_factor(x, grams, width, slabs, 1.0 / (points * slabs))
    return modes[None], factor[None]


def solution(mesh):
    return jax.shard_map(
        functools.partial(local, mesh.shape["space"]),
        mesh=mesh,
        in_specs=(P("blk", "space"), P("blk"), P("blk"), P()),
        out_specs=(P("blk", "space", None), P("blk", None, None, None)),
        check_vma=False,
    )
```

```python
import functools
import math

import jax
import jax.numpy as jnp
from jax import lax
from jax.experimental import pallas as pl
from jax.experimental.pallas import tpu as pltpu
from jax.sharding import PartitionSpec as P

NFFT = 512
SUB = 8
NEAR = 1
PIECE = 640
PARTS = 2
FEW_SLABS = 2
SIN_COEFS = (
    0.9999999765895043,
    -0.1666664763439475,
    0.008332899819203531,
    -0.0001980089750772882,
    2.5904879854375602e-06,
)


def cos_of_phase(phase):
    folded = jnp.abs((phase & (NFFT - 1)) - NFFT // 2) - NFFT // 4
    x = folded.astype(jnp.float32) * (2.0 * math.pi / NFFT)
    square = x * x
    total = jnp.full_like(x, SIN_COEFS[-1])
    for coef in SIN_COEFS[-2::-1]:
        total = total * square + coef
    return total * x


def spectra_kernel(
    snap_hbm, scales_hbm, offsets_hbm, freq_hbm, out_ref,
    snap_ref, scales_ref, offsets_ref, freq_ref, coef_ref, small_sems, snap_sems,
):
    snaps = snap_ref.shape[0]
    blocks = offsets_ref.shape[0]
    rows = 2 * blocks
    freqs = freq_ref.shape[0]
    small = [
        pltpu.make_async_copy(src, dst, small_sems.at[i])
        for i, (src, dst) in enumerate(
            ((offsets_hbm, offsets_ref), (freq_hbm, freq_ref), (scales_hbm, scales_ref))
        )
    ]
    pieces = [slice(at, min(at + PIECE, snaps)) for at in range(0, snaps, PIECE)]
    large = [
        pltpu.make_async_copy(snap_hbm.at[piece], snap_ref.at[piece], snap_sems.at[i])
        for i, piece in enumerate(pieces)
    ]
    for copy in small + large:
        copy.start()
    row = lax.broadcasted_iota(jnp.int32, (rows, snaps), 0)
    time = lax.broadcasted_iota(jnp.int32, (rows, snaps), 1)
    for copy in small:
        copy.wait()
    start = jnp.zeros((rows, snaps), jnp.int32)
    for b in range(blocks):
        start = jnp.where(row // 2 == b, offsets_ref[b], start)
    shifted = time - start
    hann = 0.5 - 0.5 * cos_of_phase(shifted)
    inside = (shifted >= 0) & (shifted < NFFT)
    scales = jnp.broadcast_to(scales_ref[...].reshape(1, snaps), (rows, snaps))
    weight = jnp.where(inside, hann * scales * (1.0 / math.sqrt(NFFT)), 0.0)
    quarter = NFFT // 4
    base = shifted[:, :quarter].astype(jnp.float32)
    turn = (row[:, :quarter] % 2) * quarter
    repeats = -(-snaps // NFFT)

    def rows_of(f):
        freq = freq_ref[f]
        phase = (base * freq.astype(jnp.float32)).astype(jnp.int32) + turn
        even, odd = cos_of_phase(phase), cos_of_phase(phase + quarter)
        tiles = [even]
        for j in range(1, 4):
            turns = (freq * j) & 3
            along = ((1 - (turns & 1)) * (1 - turns)).astype(jnp.float32)
            across = ((turns & 1) * (2 - turns)).astype(jnp.float32)
            tiles.append(even * along + odd * across)
        return jnp.concatenate(tiles * repeats, 1)[:, :snaps] * weight

    for f in range(0, freqs, 2):
        pair = jnp.concatenate([rows_of(f), rows_of(f + 1)], 0)
        coef_ref[f * rows:(f + 2) * rows, :] = pair.astype(jnp.bfloat16)
    for copy in large:
        copy.wait()
    total = jnp.dot(coef_ref[...], snap_ref[...], preferred_element_type=jnp.float32)
    result = total.astype(jnp.bfloat16)
    for copy in range(out_ref.shape[0]):
        out_ref[copy] = result


def block_spectra(copies, snapshots, row_scales, block_offsets, freq_index):
    snaps, points = snapshots.shape
    rows = 2 * block_offsets.shape[0] * freq_index.shape[0]
    pieces = -(-snaps // PIECE)
    return pl.pallas_call(
        spectra_kernel,
        out_shape=jax.ShapeDtypeStruct((copies, rows, points), jnp.bfloat16),
        in_specs=[pl.BlockSpec(memory_space=pltpu.HBM)] * 4,
        out_specs=pl.BlockSpec(memory_space=pltpu.VMEM),
        scratch_shapes=[
            pltpu.VMEM((snaps, points), jnp.bfloat16),
            pltpu.VMEM((snaps,), jnp.float32),
            pltpu.SMEM(block_offsets.shape, jnp.int32),
            pltpu.SMEM(freq_index.shape, jnp.int32),
            pltpu.VMEM((rows, snaps), jnp.bfloat16),
            pltpu.SemaphoreType.DMA((3,)),
            pltpu.SemaphoreType.DMA((pieces,)),
        ],
        compiler_params=pltpu.CompilerParams(vmem_limit_bytes=8 * 2**20),
        name="spectra",
    )(*(
        pltpu.with_memory_space_constraint(x, pltpu.HBM)
        for x in (snapshots, row_scales, block_offsets, freq_index)
    ))


def rotated(x, lane):
    axis = x.ndim - 1
    width = x.shape[axis]
    after = pltpu.roll(x, width - 1, axis)
    before = pltpu.roll(x, 1, axis)
    return jnp.where(lane % 2 == 0, -after, before)


def gram_rows(slabs, full_ref):
    width = full_ref.shape[0]
    full_ref[...] = sum(
        lax.dot_general(x, x, (((1,), (1,)), ((), ())), preferred_element_type=jnp.float32)
        for x in slabs
    )
    even = full_ref[pl.ds(0, width // 2, stride=2), :]
    odd = full_ref[pl.ds(1, width // 2, stride=2), :]
    lane = lax.broadcasted_iota(jnp.int32, odd.shape, 1)
    return even - rotated(odd, lane)


def gram_kernel(x_ref, out_ref, full_ref):
    out_ref[...] = gram_rows([x_ref[...]], full_ref)


def complex_gram(x):
    width = x.shape[0]
    return pl.pallas_call(
        gram_kernel,
        out_shape=jax.ShapeDtypeStruct((width // 2, width), jnp.float32),
        in_specs=[pl.BlockSpec(memory_space=pltpu.VMEM)],
        out_specs=pl.BlockSpec(memory_space=pltpu.VMEM),
        scratch_shapes=[pltpu.VMEM((width, width), jnp.float32)],
        compiler_params=pltpu.CompilerParams(vmem_limit_bytes=4 * 2**20),
        name="gram",
    )(x)


def tree_sum(terms):
    while len(terms) > 1:
        terms = [sum(terms[i:i + 2]) for i in range(0, len(terms), 2)]
    return terms[0]


def eliminate(rows, solved_ref, step_ref, done_ref):
    count = len(rows)
    shape = rows[0].shape
    sub = lax.broadcasted_iota(jnp.int32, shape, 0)
    lane = lax.broadcasted_iota(jnp.int32, shape, 1)

    def over_lanes(x, at):
        return jnp.broadcast_to(x[:, at:at + 1], shape)

    def over_rows(x, at):
        return jnp.broadcast_to(x[at:at + 1, :], shape)

    def row_of(ref, *at):
        return ref[(*at[:-1], pl.ds(at[-1], SUB, stride=0), slice(None))]

    rows = list(rows)
    final, final_turned, pivots = [], [], []
    for own in range(count):
        head, turned = rows[own], rotated(rows[own], lane)
        done = slice(own * SUB, (own + 1) * SUB)
        columns = [2 * (own * SUB + c) for c in range(SUB)]
        raw = {
            i: [(over_lanes(rows[i], at), over_lanes(rows[i], at + 1)) for at in columns]
            for i in range(own, min(own + 1 + NEAR, count))
        }
        here = raw[own]
        pivot = over_rows(here[0][0], 0)
        for c in range(SUB):
            here_row = sub == c
            inverse = pl.reciprocal(pivot, approx=True)
            m_re = jnp.where(here_row, -1.0, here[c][0]) * inverse
            m_im = jnp.where(here_row, 0.0, here[c][1]) * inverse
            done_row = slice(own * SUB + c, own * SUB + c + 1)
            for place, value in enumerate((head, turned, pivot)):
                done_ref[place, done_row, :] = value[c:c + 1]
            for later in range(c + 1, SUB):
                re, im = here[later]
                u_re, u_im = over_rows(re, c), over_rows(im, c)
                if later == c + 1:
                    loss = (u_re * inverse) * u_re + (u_im * inverse) * u_im
                    pivot = over_rows(re, c + 1) - loss
                here[later] = (
                    jnp.where(here_row, 0.0, re) - m_re * u_re + m_im * u_im,
                    jnp.where(here_row, 0.0, im) - m_re * u_im - m_im * u_re,
                )
            on_re, on_im = lane == columns[c], lane == columns[c] + 1
            on_pair = on_re | on_im
            step_ref[c, :SUB, :] = head
            step_ref[c, SUB:, :] = turned
            p = jnp.where(on_pair, on_re.astype(jnp.float32), row_of(step_ref, c, c))
            q = jnp.where(on_pair, on_im.astype(jnp.float32), row_of(step_ref, c, SUB + c))
            cleared = here_row | on_pair
            head = jnp.where(cleared, 0.0, head) - (m_re * p + m_im * q)
            turned = jnp.where(cleared, 0.0, turned) - (m_re * q - m_im * p)
        final.append(done_ref[0, done, :])
        final_turned.append(done_ref[1, done, :])
        pivots.append(done_ref[2, done, :])
        if own + 1 == count:
            break
        inside = (lane >= columns[0]) & (lane < columns[0] + 2 * SUB)
        solved_ref[own, pl.ds(0, SUB, stride=2), :] = head
        solved_ref[own, pl.ds(1, SUB, stride=2), :] = turned
        solved = [(over_rows(head, c), over_rows(turned, c)) for c in range(SUB)]
        for i in range(own + 1, min(own + 1 + NEAR, count)):
            rows[i] = jnp.where(inside, 0.0, rows[i]) - tree_sum(
                [re * p + im * q for (re, im), (p, q) in zip(raw[i], solved)]
            )
        far = range(own + 1 + NEAR, count)
        if far:
            below = jnp.concatenate([rows[i] for i in far], 0)
            losses = jnp.dot(
                below[:, columns[0]:columns[0] + 2 * SUB], solved_ref[own],
                precision=lax.Precision.HIGHEST, preferred_element_type=jnp.float32,
            )
            for at, i in enumerate(far):
                loss = losses[at * SUB:(at + 1) * SUB]
                rows[i] = jnp.where(inside, 0.0, rows[i]) - loss
    return final, final_turned, pivots


def modes_kernel(scale, slabs, x_ref, *refs):
    *given, modes_hbm, factor_hbm, basis_ref, solved_ref, step_ref, done_ref = refs[:-4]
    points_ref, modes_ref, factor_ref, sems = refs[-4:]
    width = basis_ref.shape[0]
    size = width // 2
    count = size // SUB
    if given:
        gram = given[0][...]
        mine = x_ref[...]
    else:
        gram = gram_rows([x_ref[i * width:(i + 1) * width] for i in range(slabs)], basis_ref)
        own = lax.axis_index("space")
        mine = x_ref[pl.ds(pl.multiple_of(own * width, width), width)]
    points = jnp.transpose(mine)
    points_ref[...] = jnp.concatenate([points, points], 1)
    gram = gram * scale
    rows, turned, pivots = eliminate([gram[i * SUB:(i + 1) * SUB] for i in range(count)], solved_ref, step_ref, done_ref)
    shape = rows[0].shape
    sub = lax.broadcasted_iota(jnp.int32, shape, 0)
    lane = lax.broadcasted_iota(jnp.int32, shape, 1)
    pick = jnp.where(lane < size, 2 * lane, 2 * (lane - size) + 1)
    for i in range(count):
        own_rows = slice(i * SUB, (i + 1) * SUB)
        root = lax.rsqrt(pivots[i])
        diagonal = 2 * (i * SUB + sub)
        left = jnp.where(lane < diagonal, rows[i], (lane == diagonal).astype(jnp.float32))
        aside = jnp.where(lane < diagonal, turned[i], (lane == diagonal + 1).astype(jnp.float32))
        basis_ref[pl.ds(2 * i * SUB, SUB, stride=2), :] = left * root
        basis_ref[pl.ds(2 * i * SUB + 1, SUB, stride=2), :] = aside * root
        right = jnp.where(lane > diagonal + 1, rows[i], jnp.where(lane == diagonal, pivots[i], 0.0))
        parts = jnp.take_along_axis(right * root, pick, axis=1)
        factor_ref[0, own_rows, :] = parts[:, :size]
        factor_ref[1, own_rows, :] = parts[:, size:]
    copies = [pltpu.make_async_copy(factor_ref, factor_hbm, sems.at[0])]
    copies[0].start()
    basis = basis_ref[...]
    high = basis.astype(jnp.bfloat16)
    low = (basis - high.astype(jnp.float32)).astype(jnp.bfloat16)
    terms = jnp.concatenate([high, low], 1)
    each = modes_ref.shape[0] // PARTS
    for i in range(PARTS):
        part = slice(i * each, (i + 1) * each)
        modes_ref[part] = lax.dot_general(
            points_ref[part], terms, (((1,), (1,)), ((), ())),
            preferred_element_type=jnp.float32,
        )
        copies.append(pltpu.make_async_copy(modes_ref.at[part], modes_hbm.at[part], sems.at[1 + i]))
        copies[-1].start()
    for copy in copies:
        copy.wait()


def modes_and_factor(x, grams, width, slabs, scale):
    points = x.shape[1]
    size = width // 2
    return pl.pallas_call(
        functools.partial(modes_kernel, scale, slabs),
        out_shape=(
            jax.ShapeDtypeStruct((points, width), jnp.float32),
            jax.ShapeDtypeStruct((2, size, size), jnp.float32),
        ),
        in_specs=[pl.BlockSpec(memory_space=pltpu.VMEM)] * (1 + len(grams)),
        out_specs=(pl.BlockSpec(memory_space=pltpu.HBM),) * 2,
        scratch_shapes=[
            pltpu.VMEM((width, width), jnp.float32),
            pltpu.VMEM((size // SUB, 2 * SUB, width), jnp.float32),
            pltpu.VMEM((SUB, 2 * SUB, width), jnp.float32),
            pltpu.VMEM((3, size, width), jnp.float32),
            pltpu.VMEM((points, 2 * width), jnp.bfloat16),
            pltpu.VMEM((points, width), jnp.float32),
            pltpu.VMEM((2, size, size), jnp.float32),
            pltpu.SemaphoreType.DMA((1 + PARTS,)),
        ],
        compiler_params=pltpu.CompilerParams(vmem_limit_bytes=8 * 2**20),
        name="factor_and_modes",
    )(x, *grams)


def local(slabs, snapshots, row_scales, block_offsets, freq_index):
    freqs = freq_index.shape[0]
    points = snapshots.shape[1]
    width = 2 * block_offsets.shape[0] * lax.axis_size("blk")
    copies = slabs if slabs <= FEW_SLABS else 1
    spectra = block_spectra(copies, snapshots, row_scales, block_offsets, freq_index)
    chunks = spectra.reshape(copies * freqs, -1, points)
    swap = functools.partial(lax.all_to_all, split_axis=0, concat_axis=0, tiled=True)
    if copies == slabs:
        x = swap(chunks, ("space", "blk")).reshape(-1, points)
        grams = []
    else:
        x = swap(chunks, "blk").reshape(-1, points)
        grams = [lax.psum(complex_gram(x), "space")]
    modes, factor = modes_and_factor(x, grams, width, slabs, 1.0 / (points * slabs))
    return modes[None], factor[None]


def solution(mesh):
    return jax.shard_map(
        functools.partial(local, mesh.shape["space"]),
        mesh=mesh,
        in_specs=(P("blk", "space"), P("blk"), P("blk"), P()),
        out_specs=(P("blk", "space", None), P("blk", None, None, None)),
        check_vma=False,
    )
```

```python
import functools
import math

import jax
import jax.numpy as jnp
from jax import lax
from jax.experimental import pallas as pl
from jax.experimental.pallas import tpu as pltpu
from jax.sharding import PartitionSpec as P

NFFT = 512
SUB = 8
PIECE = 640
PARTS = 4
FEW_SLABS = 2
SIN_COEFS = (
    0.9999999765895043,
    -0.1666664763439475,
    0.008332899819203531,
    -0.0001980089750772882,
    2.5904879854375602e-06,
)


def cos_of_phase(phase):
    folded = jnp.abs((phase & (NFFT - 1)) - NFFT // 2) - NFFT // 4
    x = folded.astype(jnp.float32) * (2.0 * math.pi / NFFT)
    square = x * x
    total = jnp.full_like(x, SIN_COEFS[-1])
    for coef in SIN_COEFS[-2::-1]:
        total = total * square + coef
    return total * x


def spectra_kernel(
    snap_hbm, scales_hbm, offsets_hbm, freq_hbm, out_ref,
    snap_ref, scales_ref, offsets_ref, freq_ref, coef_ref, small_sems, snap_sems,
):
    snaps = snap_ref.shape[0]
    blocks = offsets_ref.shape[0]
    rows = 2 * blocks
    freqs = freq_ref.shape[0]
    small = [
        pltpu.make_async_copy(src, dst, small_sems.at[i])
        for i, (src, dst) in enumerate(
            ((offsets_hbm, offsets_ref), (freq_hbm, freq_ref), (scales_hbm, scales_ref))
        )
    ]
    pieces = [slice(at, min(at + PIECE, snaps)) for at in range(0, snaps, PIECE)]
    large = [
        pltpu.make_async_copy(snap_hbm.at[piece], snap_ref.at[piece], snap_sems.at[i])
        for i, piece in enumerate(pieces)
    ]
    for copy in large + small:
        copy.start()
    row = lax.broadcasted_iota(jnp.int32, (rows, snaps), 0)
    time = lax.broadcasted_iota(jnp.int32, (rows, snaps), 1)
    for copy in small:
        copy.wait()
    start = jnp.zeros((rows, snaps), jnp.int32)
    for b in range(blocks):
        start = jnp.where(row // 2 == b, offsets_ref[b], start)
    shifted = time - start
    hann = 0.5 - 0.5 * cos_of_phase(shifted)
    inside = (shifted >= 0) & (shifted < NFFT)
    scales = jnp.broadcast_to(scales_ref[...].reshape(1, snaps), (rows, snaps))
    weight = jnp.where(inside, hann * scales * (1.0 / math.sqrt(NFFT)), 0.0)
    quarter = NFFT // 4
    base = shifted[:, :quarter].astype(jnp.float32)
    turn = (row[:, :quarter] % 2) * quarter
    repeats = -(-snaps // NFFT)

    def rows_of(f):
        freq = freq_ref[f]
        phase = (base * freq.astype(jnp.float32)).astype(jnp.int32) + turn
        even, odd = cos_of_phase(phase), cos_of_phase(phase + quarter)
        tiles = [even]
        for j in range(1, 4):
            turns = (freq * j) & 3
            along = ((1 - (turns & 1)) * (1 - turns)).astype(jnp.float32)
            across = ((turns & 1) * (2 - turns)).astype(jnp.float32)
            tiles.append(even * along + odd * across)
        return jnp.concatenate(tiles * repeats, 1)[:, :snaps] * weight

    for f in range(0, freqs, 2):
        pair = jnp.concatenate([rows_of(f), rows_of(f + 1)], 0)
        coef_ref[f * rows:(f + 2) * rows, :] = pair.astype(jnp.bfloat16)
    for copy in large:
        copy.wait()
    total = jnp.dot(coef_ref[...], snap_ref[...], preferred_element_type=jnp.float32)
    result = total.astype(jnp.bfloat16)
    for copy in range(out_ref.shape[0]):
        out_ref[copy] = result


def block_spectra(copies, snapshots, row_scales, block_offsets, freq_index):
    snaps, points = snapshots.shape
    rows = 2 * block_offsets.shape[0] * freq_index.shape[0]
    pieces = -(-snaps // PIECE)
    return pl.pallas_call(
        spectra_kernel,
        out_shape=jax.ShapeDtypeStruct((copies, rows, points), jnp.bfloat16),
        in_specs=[pl.BlockSpec(memory_space=pltpu.HBM)] * 4,
        out_specs=pl.BlockSpec(memory_space=pltpu.VMEM),
        scratch_shapes=[
            pltpu.VMEM((snaps, points), jnp.bfloat16),
            pltpu.VMEM((snaps,), jnp.float32),
            pltpu.SMEM(block_offsets.shape, jnp.int32),
            pltpu.SMEM(freq_index.shape, jnp.int32),
            pltpu.VMEM((rows, snaps), jnp.bfloat16),
            pltpu.SemaphoreType.DMA((3,)),
            pltpu.SemaphoreType.DMA((pieces,)),
        ],
        compiler_params=pltpu.CompilerParams(vmem_limit_bytes=8 * 2**20),
        name="spectra",
    )(*(
        pltpu.with_memory_space_constraint(x, pltpu.HBM)
        for x in (snapshots, row_scales, block_offsets, freq_index)
    ))


def rotated(x, lane):
    axis = x.ndim - 1
    width = x.shape[axis]
    after = pltpu.roll(x, width - 1, axis)
    before = pltpu.roll(x, 1, axis)
    return jnp.where(lane % 2 == 0, -after, before)


def gram_rows(slabs, full_ref):
    width = full_ref.shape[0]
    full_ref[...] = sum(
        lax.dot_general(x, x, (((1,), (1,)), ((), ())), preferred_element_type=jnp.float32)
        for x in slabs
    )
    even = full_ref[pl.ds(0, width // 2, stride=2), :]
    odd = full_ref[pl.ds(1, width // 2, stride=2), :]
    lane = lax.broadcasted_iota(jnp.int32, odd.shape, 1)
    return even - rotated(odd, lane)


def gram_kernel(x_ref, out_ref, full_ref):
    out_ref[...] = gram_rows([x_ref[...]], full_ref)


def complex_gram(x):
    width = x.shape[0]
    return pl.pallas_call(
        gram_kernel,
        out_shape=jax.ShapeDtypeStruct((width // 2, width), jnp.float32),
        in_specs=[pl.BlockSpec(memory_space=pltpu.VMEM)],
        out_specs=pl.BlockSpec(memory_space=pltpu.VMEM),
        scratch_shapes=[pltpu.VMEM((width, width), jnp.float32)],
        compiler_params=pltpu.CompilerParams(vmem_limit_bytes=4 * 2**20),
        name="gram",
    )(x)


def tree_sum(terms):
    while len(terms) > 1:
        terms = [sum(terms[i:i + 2]) for i in range(0, len(terms), 2)]
    return terms[0]


def eliminate(rows, solved_ref, step_ref):
    count = len(rows)
    shape = rows[0].shape
    sub = lax.broadcasted_iota(jnp.int32, shape, 0)
    lane = lax.broadcasted_iota(jnp.int32, shape, 1)

    def over_lanes(x, at):
        return jnp.broadcast_to(x[:, at:at + 1], shape)

    def over_rows(x, at):
        return jnp.broadcast_to(x[at:at + 1, :], shape)

    def row_of(ref, *at):
        return ref[(*at[:-1], pl.ds(at[-1], SUB, stride=0), slice(None))]

    rows = list(rows)
    final, final_turned, pivots = [], [], []
    for own in range(count):
        head, turned = rows[own], rotated(rows[own], lane)
        keep, keep_turned, keep_pivot = head, turned, jnp.ones(shape, jnp.float32)
        columns = [2 * (own * SUB + c) for c in range(SUB)]
        raw = {
            i: [(over_lanes(rows[i], at), over_lanes(rows[i], at + 1)) for at in columns]
            for i in range(own, min(own + 2, count))
        }
        here = raw[own]
        pivot = over_rows(here[0][0], 0)
        for c in range(SUB):
            here_row = sub == c
            inverse = pl.reciprocal(pivot, approx=True)
            m_re = jnp.where(here_row, -1.0, here[c][0]) * inverse
            m_im = jnp.where(here_row, 0.0, here[c][1]) * inverse
            keep = jnp.where(here_row, head, keep)
            keep_turned = jnp.where(here_row, turned, keep_turned)
            keep_pivot = jnp.where(here_row, pivot, keep_pivot)
            for later in range(c + 1, SUB):
                re, im = here[later]
                u_re, u_im = over_rows(re, c), over_rows(im, c)
                if later == c + 1:
                    loss = (u_re * inverse) * u_re + (u_im * inverse) * u_im
                    pivot = over_rows(re, c + 1) - loss
                here[later] = (
                    jnp.where(here_row, 0.0, re) - m_re * u_re + m_im * u_im,
                    jnp.where(here_row, 0.0, im) - m_re * u_im - m_im * u_re,
                )
            on_re, on_im = lane == columns[c], lane == columns[c] + 1
            on_pair = on_re | on_im
            step_ref[c, :SUB, :] = head
            step_ref[c, SUB:, :] = turned
            p = jnp.where(on_pair, on_re.astype(jnp.float32), row_of(step_ref, c, c))
            q = jnp.where(on_pair, on_im.astype(jnp.float32), row_of(step_ref, c, SUB + c))
            cleared = here_row | on_pair
            head = jnp.where(cleared, 0.0, head) - (m_re * p + m_im * q)
            turned = jnp.where(cleared, 0.0, turned) - (m_re * q - m_im * p)
        final.append(keep)
        final_turned.append(keep_turned)
        pivots.append(keep_pivot)
        if own + 1 == count:
            break
        inside = (lane >= columns[0]) & (lane < columns[0] + 2 * SUB)
        solved_ref[own, pl.ds(0, SUB, stride=2), :] = head
        solved_ref[own, pl.ds(1, SUB, stride=2), :] = turned
        solved = [(over_rows(head, c), over_rows(turned, c)) for c in range(SUB)]
        rows[own + 1] = jnp.where(inside, 0.0, rows[own + 1]) - tree_sum(
            [re * p + im * q for (re, im), (p, q) in zip(raw[own + 1], solved)]
        )
        far = range(own + 2, count)
        if far:
            below = jnp.concatenate([rows[i] for i in far], 0)
            losses = jnp.dot(
                below[:, columns[0]:columns[0] + 2 * SUB], solved_ref[own],
                precision=lax.Precision.HIGHEST, preferred_element_type=jnp.float32,
            )
            for at, i in enumerate(far):
                loss = losses[at * SUB:(at + 1) * SUB]
                rows[i] = jnp.where(inside, 0.0, rows[i]) - loss
    return final, final_turned, pivots


def modes_kernel(scale, slabs, x_ref, *refs):
    *given, modes_hbm, factor_hbm, basis_ref, solved_ref, step_ref, points_ref, modes_ref, factor_ref, sems = refs
    width = basis_ref.shape[0]
    size = width // 2
    count = size // SUB
    if given:
        gram = given[0][...]
        mine = x_ref[...]
    else:
        gram = gram_rows([x_ref[i * width:(i + 1) * width] for i in range(slabs)], basis_ref)
        own = lax.axis_index("space")
        mine = x_ref[pl.ds(pl.multiple_of(own * width, width), width)]
    points = jnp.transpose(mine)
    points_ref[...] = jnp.concatenate([points, points], 1)
    gram = gram * scale
    rows, turned, pivots = eliminate([gram[i * SUB:(i + 1) * SUB] for i in range(count)], solved_ref, step_ref)
    shape = rows[0].shape
    sub = lax.broadcasted_iota(jnp.int32, shape, 0)
    lane = lax.broadcasted_iota(jnp.int32, shape, 1)
    pick = jnp.where(lane < size, 2 * lane, 2 * (lane - size) + 1)
    for i in range(count):
        own_rows = slice(i * SUB, (i + 1) * SUB)
        root = lax.rsqrt(pivots[i])
        diagonal = 2 * (i * SUB + sub)
        left = jnp.where(lane < diagonal, rows[i], (lane == diagonal).astype(jnp.float32))
        aside = jnp.where(lane < diagonal, turned[i], (lane == diagonal + 1).astype(jnp.float32))
        basis_ref[pl.ds(2 * i * SUB, SUB, stride=2), :] = left * root
        basis_ref[pl.ds(2 * i * SUB + 1, SUB, stride=2), :] = aside * root
        right = jnp.where(lane > diagonal + 1, rows[i], jnp.where(lane == diagonal, pivots[i], 0.0))
        parts = jnp.take_along_axis(right * root, pick, axis=1)
        factor_ref[0, own_rows, :] = parts[:, :size]
        factor_ref[1, own_rows, :] = parts[:, size:]
    copies = [pltpu.make_async_copy(factor_ref, factor_hbm, sems.at[0])]
    copies[0].start()
    basis = basis_ref[...]
    high = basis.astype(jnp.bfloat16)
    low = (basis - high.astype(jnp.float32)).astype(jnp.bfloat16)
    terms = jnp.concatenate([high, low], 1)
    each = modes_ref.shape[0] // PARTS
    for i in range(PARTS):
        part = slice(i * each, (i + 1) * each)
        modes_ref[part] = lax.dot_general(
            points_ref[part], terms, (((1,), (1,)), ((), ())),
            preferred_element_type=jnp.float32,
        )
        copies.append(pltpu.make_async_copy(modes_ref.at[part], modes_hbm.at[part], sems.at[1 + i]))
        copies[-1].start()
    for copy in copies:
        copy.wait()


def modes_and_factor(x, grams, width, slabs, scale):
    points = x.shape[1]
    size = width // 2
    return pl.pallas_call(
        functools.partial(modes_kernel, scale, slabs),
        out_shape=(
            jax.ShapeDtypeStruct((points, width), jnp.float32),
            jax.ShapeDtypeStruct((2, size, size), jnp.float32),
        ),
        in_specs=[pl.BlockSpec(memory_space=pltpu.VMEM)] * (1 + len(grams)),
        out_specs=(pl.BlockSpec(memory_space=pltpu.HBM),) * 2,
        scratch_shapes=[
            pltpu.VMEM((width, width), jnp.float32),
            pltpu.VMEM((size // SUB, 2 * SUB, width), jnp.float32),
            pltpu.VMEM((SUB, 2 * SUB, width), jnp.float32),
            pltpu.VMEM((points, 2 * width), jnp.bfloat16),
            pltpu.VMEM((points, width), jnp.float32),
            pltpu.VMEM((2, size, size), jnp.float32),
            pltpu.SemaphoreType.DMA((1 + PARTS,)),
        ],
        compiler_params=pltpu.CompilerParams(vmem_limit_bytes=8 * 2**20),
        name="factor_and_modes",
    )(x, *grams)


def local(slabs, snapshots, row_scales, block_offsets, freq_index):
    freqs = freq_index.shape[0]
    points = snapshots.shape[1]
    width = 2 * block_offsets.shape[0] * lax.axis_size("blk")
    copies = slabs if slabs <= FEW_SLABS else 1
    spectra = block_spectra(copies, snapshots, row_scales, block_offsets, freq_index)
    chunks = spectra.reshape(copies * freqs, -1, points)
    swap = functools.partial(lax.all_to_all, split_axis=0, concat_axis=0, tiled=True)
    if copies == slabs:
        x = swap(chunks, ("space", "blk")).reshape(-1, points)
        grams = []
    else:
        x = swap(chunks, "blk").reshape(-1, points)
        grams = [lax.psum(complex_gram(x), "space")]
    modes, factor = modes_and_factor(x, grams, width, slabs, 1.0 / (points * slabs))
    return modes[None], factor[None]


def solution(mesh):
    return jax.shard_map(
        functools.partial(local, mesh.shape["space"]),
        mesh=mesh,
        in_specs=(P("blk", "space"), P("blk"), P("blk"), P()),
        out_specs=(P("blk", "space", None), P("blk", None, None, None)),
        check_vma=False,
    )
```

```python
import functools
import math

import jax
import jax.numpy as jnp
from jax import lax
from jax.experimental import pallas as pl
from jax.experimental.pallas import tpu as pltpu
from jax.sharding import PartitionSpec as P

NFFT = 512
SUB = 8
PIECE = 640
PARTS = 1
FEW_SLABS = 2
SIN_COEFS = (
    0.9999999765895043,
    -0.1666664763439475,
    0.008332899819203531,
    -0.0001980089750772882,
    2.5904879854375602e-06,
)


def cos_of_phase(phase):
    folded = jnp.abs((phase & (NFFT - 1)) - NFFT // 2) - NFFT // 4
    x = folded.astype(jnp.float32) * (2.0 * math.pi / NFFT)
    square = x * x
    total = jnp.full_like(x, SIN_COEFS[-1])
    for coef in SIN_COEFS[-2::-1]:
        total = total * square + coef
    return total * x


def spectra_kernel(
    snap_hbm, scales_hbm, offsets_hbm, freq_hbm, out_ref,
    snap_ref, scales_ref, offsets_ref, freq_ref, coef_ref, small_sems, snap_sems,
):
    snaps = snap_ref.shape[0]
    blocks = offsets_ref.shape[0]
    rows = 2 * blocks
    freqs = freq_ref.shape[0]
    small = [
        pltpu.make_async_copy(src, dst, small_sems.at[i])
        for i, (src, dst) in enumerate(
            ((offsets_hbm, offsets_ref), (freq_hbm, freq_ref), (scales_hbm, scales_ref))
        )
    ]
    pieces = [slice(at, min(at + PIECE, snaps)) for at in range(0, snaps, PIECE)]
    large = [
        pltpu.make_async_copy(snap_hbm.at[piece], snap_ref.at[piece], snap_sems.at[i])
        for i, piece in enumerate(pieces)
    ]
    for copy in small + large:
        copy.start()
    row = lax.broadcasted_iota(jnp.int32, (rows, snaps), 0)
    time = lax.broadcasted_iota(jnp.int32, (rows, snaps), 1)
    for copy in small:
        copy.wait()
    start = jnp.zeros((rows, snaps), jnp.int32)
    for b in range(blocks):
        start = jnp.where(row // 2 == b, offsets_ref[b], start)
    shifted = time - start
    hann = 0.5 - 0.5 * cos_of_phase(shifted)
    inside = (shifted >= 0) & (shifted < NFFT)
    scales = jnp.broadcast_to(scales_ref[...].reshape(1, snaps), (rows, snaps))
    weight = jnp.where(inside, hann * scales * (1.0 / math.sqrt(NFFT)), 0.0)
    quarter = NFFT // 4
    base = shifted[:, :quarter].astype(jnp.float32)
    turn = (row[:, :quarter] % 2) * quarter
    repeats = -(-snaps // NFFT)

    def rows_of(f):
        freq = freq_ref[f]
        phase = (base * freq.astype(jnp.float32)).astype(jnp.int32) + turn
        even, odd = cos_of_phase(phase), cos_of_phase(phase + quarter)
        tiles = [even]
        for j in range(1, 4):
            turns = (freq * j) & 3
            along = ((1 - (turns & 1)) * (1 - turns)).astype(jnp.float32)
            across = ((turns & 1) * (2 - turns)).astype(jnp.float32)
            tiles.append(even * along + odd * across)
        return jnp.concatenate(tiles * repeats, 1)[:, :snaps] * weight

    for f in range(0, freqs, 2):
        pair = jnp.concatenate([rows_of(f), rows_of(f + 1)], 0)
        coef_ref[f * rows:(f + 2) * rows, :] = pair.astype(jnp.bfloat16)
    for copy in large:
        copy.wait()
    total = jnp.dot(coef_ref[...], snap_ref[...], preferred_element_type=jnp.float32)
    result = total.astype(jnp.bfloat16)
    for copy in range(out_ref.shape[0]):
        out_ref[copy] = result


def block_spectra(copies, snapshots, row_scales, block_offsets, freq_index):
    snaps, points = snapshots.shape
    rows = 2 * block_offsets.shape[0] * freq_index.shape[0]
    pieces = -(-snaps // PIECE)
    return pl.pallas_call(
        spectra_kernel,
        out_shape=jax.ShapeDtypeStruct((copies, rows, points), jnp.bfloat16),
        in_specs=[pl.BlockSpec(memory_space=pltpu.HBM)] * 4,
        out_specs=pl.BlockSpec(memory_space=pltpu.VMEM),
        scratch_shapes=[
            pltpu.VMEM((snaps, points), jnp.bfloat16),
            pltpu.VMEM((snaps,), jnp.float32),
            pltpu.SMEM(block_offsets.shape, jnp.int32),
            pltpu.SMEM(freq_index.shape, jnp.int32),
            pltpu.VMEM((rows, snaps), jnp.bfloat16),
            pltpu.SemaphoreType.DMA((3,)),
            pltpu.SemaphoreType.DMA((pieces,)),
        ],
        compiler_params=pltpu.CompilerParams(vmem_limit_bytes=8 * 2**20),
        name="spectra",
    )(*(
        pltpu.with_memory_space_constraint(x, pltpu.HBM)
        for x in (snapshots, row_scales, block_offsets, freq_index)
    ))


def rotated(x, lane):
    axis = x.ndim - 1
    width = x.shape[axis]
    after = pltpu.roll(x, width - 1, axis)
    before = pltpu.roll(x, 1, axis)
    return jnp.where(lane % 2 == 0, -after, before)


def gram_rows(slabs, full_ref):
    width = full_ref.shape[0]
    full_ref[...] = sum(
        lax.dot_general(x, x, (((1,), (1,)), ((), ())), preferred_element_type=jnp.float32)
        for x in slabs
    )
    even = full_ref[pl.ds(0, width // 2, stride=2), :]
    odd = full_ref[pl.ds(1, width // 2, stride=2), :]
    lane = lax.broadcasted_iota(jnp.int32, odd.shape, 1)
    return even - rotated(odd, lane)


def gram_kernel(x_ref, out_ref, full_ref):
    out_ref[...] = gram_rows([x_ref[...]], full_ref)


def complex_gram(x):
    width = x.shape[0]
    return pl.pallas_call(
        gram_kernel,
        out_shape=jax.ShapeDtypeStruct((width // 2, width), jnp.float32),
        in_specs=[pl.BlockSpec(memory_space=pltpu.VMEM)],
        out_specs=pl.BlockSpec(memory_space=pltpu.VMEM),
        scratch_shapes=[pltpu.VMEM((width, width), jnp.float32)],
        compiler_params=pltpu.CompilerParams(vmem_limit_bytes=4 * 2**20),
        name="gram",
    )(x)


def tree_sum(terms):
    while len(terms) > 1:
        terms = [sum(terms[i:i + 2]) for i in range(0, len(terms), 2)]
    return terms[0]


def eliminate(rows, solved_ref, step_ref):
    count = len(rows)
    shape = rows[0].shape
    sub = lax.broadcasted_iota(jnp.int32, shape, 0)
    lane = lax.broadcasted_iota(jnp.int32, shape, 1)

    def over_lanes(x, at):
        return jnp.broadcast_to(x[:, at:at + 1], shape)

    def over_rows(x, at):
        return jnp.broadcast_to(x[at:at + 1, :], shape)

    def row_of(ref, *at):
        return ref[(*at[:-1], pl.ds(at[-1], SUB, stride=0), slice(None))]

    rows = list(rows)
    final, final_turned, pivots = [], [], []
    for own in range(count):
        head, turned = rows[own], rotated(rows[own], lane)
        keep, keep_turned, keep_pivot = head, turned, jnp.ones(shape, jnp.float32)
        columns = [2 * (own * SUB + c) for c in range(SUB)]
        raw = {
            i: [(over_lanes(rows[i], at), over_lanes(rows[i], at + 1)) for at in columns]
            for i in range(own, min(own + 2, count))
        }
        here = raw[own]
        pivot = over_rows(here[0][0], 0)
        for c in range(SUB):
            here_row = sub == c
            inverse = pl.reciprocal(pivot, approx=True)
            m_re = jnp.where(here_row, -1.0, here[c][0]) * inverse
            m_im = jnp.where(here_row, 0.0, here[c][1]) * inverse
            keep = jnp.where(here_row, head, keep)
            keep_turned = jnp.where(here_row, turned, keep_turned)
            keep_pivot = jnp.where(here_row, pivot, keep_pivot)
            for later in range(c + 1, SUB):
                re, im = here[later]
                u_re, u_im = over_rows(re, c), over_rows(im, c)
                if later == c + 1:
                    loss = (u_re * inverse) * u_re + (u_im * inverse) * u_im
                    pivot = over_rows(re, c + 1) - loss
                here[later] = (
                    jnp.where(here_row, 0.0, re) - m_re * u_re + m_im * u_im,
                    jnp.where(here_row, 0.0, im) - m_re * u_im - m_im * u_re,
                )
            on_re, on_im = lane == columns[c], lane == columns[c] + 1
            on_pair = on_re | on_im
            step_ref[c, :SUB, :] = head
            step_ref[c, SUB:, :] = turned
            p = jnp.where(on_pair, on_re.astype(jnp.float32), row_of(step_ref, c, c))
            q = jnp.where(on_pair, on_im.astype(jnp.float32), row_of(step_ref, c, SUB + c))
            cleared = here_row | on_pair
            head = jnp.where(cleared, 0.0, head) - (m_re * p + m_im * q)
            turned = jnp.where(cleared, 0.0, turned) - (m_re * q - m_im * p)
        final.append(keep)
        final_turned.append(keep_turned)
        pivots.append(keep_pivot)
        if own + 1 == count:
            break
        inside = (lane >= columns[0]) & (lane < columns[0] + 2 * SUB)
        solved_ref[own, pl.ds(0, SUB, stride=2), :] = head
        solved_ref[own, pl.ds(1, SUB, stride=2), :] = turned
        solved = [(over_rows(head, c), over_rows(turned, c)) for c in range(SUB)]
        rows[own + 1] = jnp.where(inside, 0.0, rows[own + 1]) - tree_sum(
            [re * p + im * q for (re, im), (p, q) in zip(raw[own + 1], solved)]
        )
        far = range(own + 2, count)
        if far:
            below = jnp.concatenate([rows[i] for i in far], 0)
            losses = jnp.dot(
                below[:, columns[0]:columns[0] + 2 * SUB], solved_ref[own],
                precision=lax.Precision.HIGHEST, preferred_element_type=jnp.float32,
            )
            for at, i in enumerate(far):
                loss = losses[at * SUB:(at + 1) * SUB]
                rows[i] = jnp.where(inside, 0.0, rows[i]) - loss
    return final, final_turned, pivots


def modes_kernel(scale, slabs, x_ref, *refs):
    *given, modes_hbm, factor_hbm, basis_ref, solved_ref, step_ref, points_ref, modes_ref, factor_ref, sems = refs
    width = basis_ref.shape[0]
    size = width // 2
    count = size // SUB
    if given:
        gram = given[0][...]
        mine = x_ref[...]
    else:
        gram = gram_rows([x_ref[i * width:(i + 1) * width] for i in range(slabs)], basis_ref)
        own = lax.axis_index("space")
        mine = x_ref[pl.ds(pl.multiple_of(own * width, width), width)]
    points = jnp.transpose(mine)
    points_ref[...] = jnp.concatenate([points, points], 1)
    gram = gram * scale
    rows, turned, pivots = eliminate([gram[i * SUB:(i + 1) * SUB] for i in range(count)], solved_ref, step_ref)
    shape = rows[0].shape
    sub = lax.broadcasted_iota(jnp.int32, shape, 0)
    lane = lax.broadcasted_iota(jnp.int32, shape, 1)
    pick = jnp.where(lane < size, 2 * lane, 2 * (lane - size) + 1)
    for i in range(count):
        own_rows = slice(i * SUB, (i + 1) * SUB)
        root = lax.rsqrt(pivots[i])
        diagonal = 2 * (i * SUB + sub)
        left = jnp.where(lane < diagonal, rows[i], (lane == diagonal).astype(jnp.float32))
        aside = jnp.where(lane < diagonal, turned[i], (lane == diagonal + 1).astype(jnp.float32))
        basis_ref[pl.ds(2 * i * SUB, SUB, stride=2), :] = left * root
        basis_ref[pl.ds(2 * i * SUB + 1, SUB, stride=2), :] = aside * root
        right = jnp.where(lane > diagonal + 1, rows[i], jnp.where(lane == diagonal, pivots[i], 0.0))
        parts = jnp.take_along_axis(right * root, pick, axis=1)
        factor_ref[0, own_rows, :] = parts[:, :size]
        factor_ref[1, own_rows, :] = parts[:, size:]
    copies = [pltpu.make_async_copy(factor_ref, factor_hbm, sems.at[0])]
    copies[0].start()
    basis = basis_ref[...]
    high = basis.astype(jnp.bfloat16)
    low = (basis - high.astype(jnp.float32)).astype(jnp.bfloat16)
    terms = jnp.concatenate([high, low], 1)
    each = modes_ref.shape[0] // PARTS
    for i in range(PARTS):
        part = slice(i * each, (i + 1) * each)
        modes_ref[part] = lax.dot_general(
            points_ref[part], terms, (((1,), (1,)), ((), ())),
            preferred_element_type=jnp.float32,
        )
        copies.append(pltpu.make_async_copy(modes_ref.at[part], modes_hbm.at[part], sems.at[1 + i]))
        copies[-1].start()
    for copy in copies:
        copy.wait()


def modes_and_factor(x, grams, width, slabs, scale):
    points = x.shape[1]
    size = width // 2
    return pl.pallas_call(
        functools.partial(modes_kernel, scale, slabs),
        out_shape=(
            jax.ShapeDtypeStruct((points, width), jnp.float32),
            jax.ShapeDtypeStruct((2, size, size), jnp.float32),
        ),
        in_specs=[pl.BlockSpec(memory_space=pltpu.VMEM)] * (1 + len(grams)),
        out_specs=(pl.BlockSpec(memory_space=pltpu.HBM),) * 2,
        scratch_shapes=[
            pltpu.VMEM((width, width), jnp.float32),
            pltpu.VMEM((size // SUB, 2 * SUB, width), jnp.float32),
            pltpu.VMEM((SUB, 2 * SUB, width), jnp.float32),
            pltpu.VMEM((points, 2 * width), jnp.bfloat16),
            pltpu.VMEM((points, width), jnp.float32),
            pltpu.VMEM((2, size, size), jnp.float32),
            pltpu.SemaphoreType.DMA((1 + PARTS,)),
        ],
        compiler_params=pltpu.CompilerParams(vmem_limit_bytes=8 * 2**20),
        name="factor_and_modes",
    )(x, *grams)


def local(slabs, snapshots, row_scales, block_offsets, freq_index):
    freqs = freq_index.shape[0]
    points = snapshots.shape[1]
    width = 2 * block_offsets.shape[0] * lax.axis_size("blk")
    copies = slabs if slabs <= FEW_SLABS else 1
    spectra = block_spectra(copies, snapshots, row_scales, block_offsets, freq_index)
    chunks = spectra.reshape(copies * freqs, -1, points)
    swap = functools.partial(lax.all_to_all, split_axis=0, concat_axis=0, tiled=True)
    if copies == slabs:
        x = swap(chunks, ("space", "blk")).reshape(-1, points)
        grams = []
    else:
        x = swap(chunks, "blk").reshape(-1, points)
        grams = [lax.psum(complex_gram(x), "space")]
    modes, factor = modes_and_factor(x, grams, width, slabs, 1.0 / (points * slabs))
    return modes[None], factor[None]


def solution(mesh):
    return jax.shard_map(
        functools.partial(local, mesh.shape["space"]),
        mesh=mesh,
        in_specs=(P("blk", "space"), P("blk"), P("blk"), P()),
        out_specs=(P("blk", "space", None), P("blk", None, None, None)),
        check_vma=False,
    )
```
